32 devices in a mesh: groups: 2 (over x), section: 16 (over z, y, core).
Axes of the slice: x: 2, y: 2, z: 4, core: 2. Of those that a mesh axis runs over, the one named last changes fastest.
Arguments:
- micro: bfloat16 [32, 192, 1024], P(('groups', 'section')), parts along dimension 0, may hold values from -6 to 6
- segment: int32 [32, 192], P(('groups', 'section')), parts along dimension 0, may hold values from 0 to 3, as said below
- gain: bfloat16 [16, 1024], P('section'), may hold values from 0.099609375 to 1.8984375
- w_query: bfloat16 [16, 1024, 2048], P('section'), may hold values from -0.1875 to 0.1875
- w_key: bfloat16 [16, 1024, 1024], P('section'), may hold values from -0.1875 to 0.1875
- w_value: bfloat16 [16, 1024, 1024], P('section'), may hold values from -0.1875 to 0.1875
- w_out: bfloat16 [16, 2048, 1024], P('section'), may hold values from -0.125 to 0.125
Outputs:
- result: bfloat16 [32, 192, 1024], P(('groups', 'section')), parts along dimension 0
The draws below stay inside these ranges and needn't reach their ends.
There are 2 independent parts, one for each index of `groups`. The reference program is written for one: setup_inputs(seed, part) draws one part's arguments, and reference() takes and returns one part's arrays. A program takes and returns all parts, laid end to end along the dimension named above; an argument that names none is the same for every part. Nothing has to cross between parts.
Inputs may be any that keep to these rules, and one draw needn't show every extreme that they name: `segment`: in each micro-batch the ids never fall, each of the 4 pairs holds 24 to 96 consecutive tokens, and one pair holds exactly 96.
All inputs are finite; a program needn't handle non-finite values.
Results may differ from the reference program's by a relative error of at most 0.013.
Values may be sent and summed in bfloat16 or wider, within the bound.
No kernel may reach another device: no remote copies, remote signals or barrier semaphores. Data moves between devices by JAX's collectives and lax.ppermute only.
A program may use at most 128 MiB of HBM per device.

```python
import jax
import jax.numpy as jnp
from jax import lax

D = 1024
HEADS = 16
KV_HEADS = 8
HD = 128
TOK_DEV = 192
TICKS = 4
SECTIONS = 16
MAX_LEN = 96
MIN_LEN = 24


def one_batch(key):
    first_key, second_key = jax.random.split(key)
    extra = TOK_DEV // 8
    cuts = jax.random.randint(first_key, (2,), 0, extra + 1)
    lower_cut = jnp.minimum(cuts[0], cuts[1])
    upper_cut = jnp.maximum(cuts[0], cuts[1])
    smaller = jnp.stack([lower_cut, upper_cut - lower_cut, extra - upper_cut]) + MIN_LEN
    longest_at = jax.random.randint(second_key, (), 0, 4)
    lengths = []
    for slot in range(4):
        before = smaller[min(slot, 2)]
        after = smaller[max(slot - 1, 0)]
        pick = jnp.where(slot < longest_at, before, jnp.where(slot == longest_at, MAX_LEN, after))
        lengths.append(pick.astype(jnp.int32))
    ends = jnp.cumsum(jnp.stack(lengths)).astype(jnp.int32)
    where_at = jnp.arange(TOK_DEV, dtype=jnp.int32)
    return jnp.sum((where_at[:, None] >= ends[None, :3]).astype(jnp.int32), axis=1).astype(jnp.int32)


def draw_segment(key, part):
    keys = jax.random.split(key, SECTIONS)
    return jax.vmap(one_batch)(keys)


def steps_of(stream_key, dims, shards, least, high):
    loudness = 1.0
    for dim, shards_of in shards:
        steps = jax.random.uniform(jax.random.fold_in(jax.random.fold_in(stream_key, 6), dim), (shards_of,), jnp.float32, least / len(shards), high / len(shards))
        loudness = loudness * jnp.repeat(jnp.exp(steps), dims[dim] // shards_of).reshape((-1,) + (1,) * (len(dims) - 1 - dim))
    return loudness


def normal_values(key, extent, width, reach, pieces=(), held_as=jnp.bfloat16):
    factor_of = steps_of(key, extent, pieces, -0.22, 0.18) if pieces else 1.0
    values = jax.random.normal(key, extent, jnp.float32) * width * factor_of
    return jnp.minimum(jnp.maximum(values, -reach), reach).astype(held_as)


def setup_inputs(seed: int = 0, part: int = 0) -> dict:
    key_list = jax.random.split(jax.random.key(seed), 8)
    part_splits = jax.random.split(jax.random.fold_in(key_list[7], part), 8)
    micro = normal_values(part_splits[0], (SECTIONS, TOK_DEV, D), 1.0, 6.0, ((0, 16),))
    segment = draw_segment(jax.random.fold_in(jax.random.fold_in(key_list[7], part), 71), part)
    gain = jnp.clip(1.0 + 0.18 * jax.random.normal(key_list[2], (SECTIONS, D), jnp.float32), 0.099609375, 1.8984375).astype(jnp.bfloat16)
    w_query = normal_values(key_list[3], (SECTIONS, D, HEADS * HD), D ** -0.5, 0.1875, ((0, 16),))
    w_key = normal_values(key_list[4], (SECTIONS, D, KV_HEADS * HD), D ** -0.5, 0.1875, ((0, 16),))
    w_value = normal_values(key_list[5], (SECTIONS, D, KV_HEADS * HD), D ** -0.5, 0.1875, ((0, 16),))
    w_out = normal_values(key_list[6], (SECTIONS, HEADS * HD, D), (HEADS * HD) ** -0.5, 0.125, ((0, 16),))
    return {"micro": micro, "segment": segment, "gain": gain, "w_query": w_query, "w_key": w_key, "w_value": w_value, "w_out": w_out}


def positions(pair_ids):
    length = pair_ids.shape[0]
    matched = pair_ids[:, None] == pair_ids[None, :]
    row_index = lax.broadcasted_iota(jnp.int32, (length, length), 0)
    column = lax.broadcasted_iota(jnp.int32, (length, length), 1)
    earlier = matched & (column < row_index)
    places = lax.optimization_barrier(jnp.sum(earlier.astype(jnp.float32), axis=1))
    allowed = matched & (column <= row_index)
    return (places, allowed)

def rotate(values, places):
    middle = values.shape[2] // 2
    ladder = jnp.arange(middle, dtype=jnp.float32)
    spacing = 1000000.0 ** (-2.0 * ladder / (2 * middle))
    angles = places[:, None, None] * spacing[None, None, :]
    cosine = jnp.cos(angles)
    sine_part = jnp.sin(angles)
    front_part = values[:, :, :middle]
    second = values[:, :, middle:]
    return jnp.concatenate([front_part * cosine - second * sine_part, second * cosine + front_part * sine_part], axis=2)

def apply_layer(stream, pair_ids, gain_row, wq_layer, wk_layer, wv_layer, wo_layer):
    length = stream.shape[0]
    stream_f = stream.astype(jnp.float32)
    scale = lax.rsqrt(lax.optimization_barrier(jnp.mean(stream_f * stream_f, axis=1, keepdims=True)) + 1e-05)
    normed = (stream_f * scale * gain_row.astype(jnp.float32)[None, :]).astype(jnp.bfloat16)
    places, allowed = positions(pair_ids)
    queries = rotate(jnp.dot(normed, wq_layer, preferred_element_type=jnp.float32).reshape(length, HEADS, HD), places).astype(jnp.bfloat16)
    key_rows = rotate(jnp.dot(normed, wk_layer, preferred_element_type=jnp.float32).reshape(length, KV_HEADS, HD), places).astype(jnp.bfloat16)
    value_rows = jnp.dot(normed, wv_layer, preferred_element_type=jnp.float32).reshape(length, KV_HEADS, HD).astype(jnp.bfloat16)
    grouped = queries.reshape(length, KV_HEADS, HEADS // KV_HEADS, HD)
    scores = jnp.einsum('ikgd,jkd->kgij', grouped.astype(jnp.float32), key_rows.astype(jnp.float32)) * HD ** (-0.5)
    expo = jnp.where(allowed[None, None], jnp.exp(scores), jnp.zeros_like(scores))
    totals = lax.optimization_barrier(jnp.sum(expo, axis=3, keepdims=True))
    shares = (expo / totals).astype(jnp.bfloat16)
    mixed = jnp.einsum('kgij,jkd->ikgd', shares.astype(jnp.float32), value_rows.astype(jnp.float32)).astype(jnp.bfloat16)
    mixed = mixed.reshape(length, HEADS * HD)
    return (stream_f + jnp.dot(mixed, wo_layer, preferred_element_type=jnp.float32)).astype(jnp.bfloat16)

def reference(micro, segment, gain, w_query, w_key, w_value, w_out):

    def one_section(section_now):
        anchor = (section_now - (TICKS - 1)) % SECTIONS
        stream = micro[anchor]
        pair_ids = segment[anchor]
        for tick_index in range(TICKS):
            layer_at = (anchor + tick_index) % SECTIONS
            stream = apply_layer(stream, pair_ids, gain[layer_at], w_query[layer_at], w_key[layer_at], w_value[layer_at], w_out[layer_at])
        return stream
    return lax.map(one_section, jnp.arange(SECTIONS, dtype=jnp.int32))
```

```python
import functools

import jax
import jax.numpy as jnp
import numpy as np
from jax import lax
from jax.experimental import pallas as pl
from jax.experimental.pallas import tpu as pltpu
from jax.sharding import PartitionSpec as P

HEADS = 16
KV_HEADS = 8
HD = 128
TICKS = 4
MAX_LEN = 96
SPLITS = (0, 96, 192)
HIDDEN = -1e30
BF16 = jnp.bfloat16
F32 = jnp.float32


def rope_table():
    middle = HD // 2
    spacing = 1000000.0 ** (-2.0 * np.arange(middle) / HD)
    angles = np.arange(MAX_LEN)[:, None] * spacing[None, :]
    cosine, sine = np.cos(angles), np.sin(angles)
    whole = np.concatenate([cosine, cosine, -sine, sine], axis=1).astype(np.float32)
    high = whole.astype(jnp.bfloat16)
    low = (whole - high.astype(np.float32)).astype(jnp.bfloat16)
    return np.concatenate([high, low], axis=0)


def tables_of(ids_row, table):
    length = ids_row.shape[1]
    across = jnp.broadcast_to(ids_row, (length, length))
    down = across.T
    row_index = lax.broadcasted_iota(jnp.int32, (length, length), 0)
    column = lax.broadcasted_iota(jnp.int32, (length, length), 1)
    matched = across == down
    places = jnp.sum(jnp.where(matched & (column < row_index), 1.0, 0.0), axis=1, keepdims=True)
    bias = jnp.where(matched & (column <= row_index), 0.0, HIDDEN)
    slots = lax.broadcasted_iota(jnp.int32, (length, 2 * MAX_LEN), 1)
    slots = jnp.where(slots >= MAX_LEN, slots - MAX_LEN, slots).astype(F32)
    one_hot = jnp.where(slots == places, 1.0, 0.0).astype(BF16)
    factors = jnp.dot(one_hot, table, preferred_element_type=F32)
    return factors, bias


def rotated(values, cosine, sine):
    return values * cosine + pltpu.roll(values, HD // 2, 1) * sine


def layer_rows(rows, keys, x_ref, gain_ref, weights, wait, cos_ref, bias_ref, k_ref, v_ref, mixed_ref, out_ref):
    low, high = rows
    first, last = keys
    size = high - low
    wq_ref, wk_ref, wv_ref, wo_ref = weights
    x = x_ref[...].astype(F32)
    scale = lax.rsqrt(jnp.mean(x * x, axis=1, keepdims=True) + 1e-05)
    normed = (x * scale * gain_ref[...].astype(F32)).astype(BF16)
    cosine = cos_ref[low:high, :HD]
    sine = cos_ref[low:high, HD:]
    factor = HD ** (-0.5) * np.log2(np.e)
    cosine_q = cosine * factor
    sine_q = sine * factor
    bias = bias_ref[low:high, first:last]
    width = 2 * HD
    for part in range(KV_HEADS // 2):
        lanes = slice(part * width, (part + 1) * width)
        wait("k", part)
        got = jnp.dot(normed, wk_ref[:, lanes], preferred_element_type=F32)
        for half in range(2):
            turned = rotated(got[:, half * HD : (half + 1) * HD], cosine, sine)
            k_ref[low:high, part * width + half * HD : part * width + (half + 1) * HD] = turned.astype(BF16)
    for part in range(KV_HEADS // 2):
        lanes = slice(part * width, (part + 1) * width)
        wait("v", part)
        v_ref[low:high, lanes] = jnp.dot(normed, wv_ref[:, lanes], preferred_element_type=F32).astype(BF16)
    ones = jnp.ones((last - first, HD), BF16)

    def query(group):
        wait("q", group)
        got = jnp.dot(normed, wq_ref[:, group * width : (group + 1) * width], preferred_element_type=F32)
        upper = rotated(got[:, :HD], cosine_q, sine_q)
        lower = rotated(got[:, HD:], cosine_q, sine_q)
        return jnp.concatenate([upper, lower], axis=0).astype(BF16)

    def attend(group, queries):
        key_rows = k_ref[first:last, group * HD : (group + 1) * HD]
        value_rows = v_ref[first:last, group * HD : (group + 1) * HD]
        scores = lax.dot_general(queries, key_rows, (((1,), (1,)), ((), ())), preferred_element_type=F32)
        scores = scores.reshape(2, size, last - first) + bias[None]
        most = jnp.max(scores, axis=2, keepdims=True)
        expo = jnp.exp2(scores - most).astype(BF16).reshape(2 * size, last - first)
        got = jnp.dot(expo, jnp.concatenate([value_rows, ones], axis=1), preferred_element_type=F32)
        mixed = (got[:, :HD] / got[:, HD:]).astype(BF16)
        mixed_ref[:, group * width : group * width + HD] = mixed[:size]
        mixed_ref[:, group * width + HD : (group + 1) * width] = mixed[size:]

    queries = query(0)
    for group in range(KV_HEADS):
        following = query(group + 1) if group + 1 < KV_HEADS else None
        attend(group, queries)
        queries = following
    for part in range(out_ref.shape[1] // width):
        lanes = slice(part * width, (part + 1) * width)
        wait("o", part)
        update = jnp.dot(mixed_ref[...], wo_ref[:, lanes], preferred_element_type=F32)
        out_ref[:, lanes] = (x_ref[:, lanes].astype(F32) + update).astype(BF16)


def opening_kernel(
    rows, keys, x_hbm, ids_ref, gain_ref, table_ref, wq_hbm, wk_hbm, wv_hbm, wo_hbm,
    out_ref, k_out, v_out, wq_ref, wk_ref, wv_ref, wo_ref, cos_ref, bias_ref,
    x_ref, mixed_ref, x_sem, sems,
):
    low, high = rows
    width = 2 * HD
    copies = {}
    load_x = pltpu.make_async_copy(x_hbm.at[0, low:high], x_ref, x_sem)
    load_x.start()
    plan = (("k", wk_hbm, wk_ref), ("v", wv_hbm, wv_ref), ("q", wq_hbm, wq_ref), ("o", wo_hbm, wo_ref))
    for name, source, target in plan:
        for part in range(target.shape[1] // width):
            lanes = slice(part * width, (part + 1) * width)
            copy = pltpu.make_async_copy(source.at[0, :, lanes], target.at[:, lanes], sems.at[len(copies)])
            copies[name, part] = copy
            copy.start()
    factors, bias = tables_of(ids_ref[...].astype(F32), table_ref[...])
    cos_ref[...] = factors
    bias_ref[...] = bias
    load_x.wait()
    layer_rows(
        rows, keys, x_ref, gain_ref, (wq_ref, wk_ref, wv_ref, wo_ref),
        lambda name, part: copies[name, part].wait(),
        cos_ref, bias_ref, k_out, v_out, mixed_ref, out_ref,
    )


def tables_kernel(ids_ref, table_ref, *outs):
    table = table_ref[...]
    for tick_index in range(TICKS - 1):
        factors, bias = tables_of(ids_ref[tick_index : tick_index + 1, :].astype(F32), table)
        outs[2 * tick_index][...] = factors
        outs[2 * tick_index + 1][...] = bias


def chunk_kernel(rows, keys, earlier, keep, x_ref, gain_ref, wq_ref, wk_ref, wv_ref, wo_ref, cos_ref, bias_ref, *refs):
    given, refs = refs[:earlier], refs[earlier:]
    out_ref, refs = refs[0], refs[1:]
    k_ref, v_ref, mixed_ref = refs[-3:]
    if earlier:
        k_ref[: rows[0]] = given[0][...]
        v_ref[: rows[0]] = given[1][...]
    layer_rows(
        rows, keys, x_ref, gain_ref, (wq_ref, wk_ref, wv_ref, wo_ref), lambda name, part: None,
        cos_ref, bias_ref, k_ref, v_ref, mixed_ref, out_ref,
    )
    if keep:
        refs[0][...] = k_ref[...]
        refs[1][...] = v_ref[...]


VMEM = pl.BlockSpec(memory_space=pltpu.VMEM)
ANY = pl.BlockSpec(memory_space=pl.ANY)


def kept(shape, dtype):
    return pltpu.VMEM(shape, dtype)


def held(array):
    return pltpu.with_memory_space_constraint(array, pltpu.VMEM)


def keys_of(rows):
    return (max(0, rows[0] - MAX_LEN + 1) // 16 * 16, rows[1])


def passed_along(array, by):
    length = lax.axis_size("section")
    return lax.ppermute(array, "section", [(i, (i + by) % length) for i in range(length)])


def body(micro, segment, gain, w_query, w_key, w_value, w_out):
    length, model = micro.shape[1], micro.shape[2]
    table = jnp.asarray(rope_table())
    later_ids = jnp.concatenate([passed_along(segment, by) for by in range(1, TICKS)], axis=0)
    limits = pltpu.CompilerParams(vmem_limit_bytes=40 * 1024 * 1024)
    kv_width = KV_HEADS * HD
    q_width = HEADS * HD
    pieces = list(zip(SPLITS[:-1], SPLITS[1:]))

    rows = pieces[0]
    size = rows[1] - rows[0]
    first = pl.pallas_call(
        functools.partial(opening_kernel, rows, keys_of(rows)),
        out_shape=(
            kept((size, model), BF16),
            kept((size, kv_width), BF16),
            kept((size, kv_width), BF16),
            kept((model, q_width), BF16),
            kept((model, kv_width), BF16),
            kept((model, kv_width), BF16),
            kept((q_width, model), BF16),
            kept((length, 2 * HD), F32),
            kept((length, length), F32),
        ),
        in_specs=[ANY, VMEM, VMEM, VMEM, ANY, ANY, ANY, ANY],
        out_specs=(VMEM,) * 9,
        scratch_shapes=[
            pltpu.VMEM((size, model), BF16),
            pltpu.VMEM((size, q_width), BF16),
            pltpu.SemaphoreType.DMA,
            pltpu.SemaphoreType.DMA((2 * (kv_width // (2 * HD)) + q_width // (2 * HD) + model // (2 * HD),)),
        ],
        compiler_params=limits,
        name="opening",
    )(micro, segment, gain, table, w_query, w_key, w_value, w_out)
    out, k_rows, v_rows = first[:3]
    weights = first[3:7]
    tables = [first[7:9]]

    def run(tick_index, piece, x, earlier):
        rows = pieces[piece]
        size = rows[1] - rows[0]
        keep = piece + 1 < len(pieces)
        shapes = [kept((size, model), BF16)]
        if keep:
            shapes += [kept((rows[1], kv_width), BF16)] * 2
        got = pl.pallas_call(
            functools.partial(chunk_kernel, rows, keys_of(rows), len(earlier), keep),
            out_shape=tuple(shapes),
            in_specs=[VMEM] * (8 + len(earlier)),
            out_specs=(VMEM,) * len(shapes),
            scratch_shapes=[
                pltpu.VMEM((rows[1], kv_width), BF16),
                pltpu.VMEM((rows[1], kv_width), BF16),
                pltpu.VMEM((size, q_width), BF16),
            ],
            compiler_params=limits,
            name="rows_%d_%d" % (tick_index, piece),
        )(held(x), gain, *map(held, weights), *map(held, tables[tick_index]), *map(held, earlier))
        return got[0], tuple(got[1:])

    streams = []
    for tick_index in range(TICKS):
        outs = []
        earlier = ()
        for piece in range(len(pieces)):
            if tick_index == 0 and piece == 0:
                got, earlier = out, (k_rows, v_rows)
            else:
                if tick_index == 0:
                    x = micro[0, pieces[piece][0] : pieces[piece][1]]
                else:
                    x = streams[piece]
                got, earlier = run(tick_index, piece, x, earlier)
            if tick_index < TICKS - 1:
                got = passed_along(got, 1)
            outs.append(got)
        if tick_index == 0:
            flat = pl.pallas_call(
                tables_kernel,
                out_shape=(kept((length, 2 * HD), F32), kept((length, length), F32)) * (TICKS - 1),
                in_specs=[VMEM, VMEM],
                out_specs=(VMEM,) * (2 * (TICKS - 1)),
                compiler_params=limits,
                name="tables",
            )(later_ids, table)
            tables += [flat[2 * i : 2 * i + 2] for i in range(TICKS - 1)]
        streams = outs
    return jnp.concatenate(streams, axis=0)[None]


def solution(mesh):
    in_specs = (
        P(("groups", "section"), None, None),
        P(("groups", "section"), None),
        P("section", None),
        P("section", None, None),
        P("section", None, None),
        P("section", None, None),
        P("section", None, None),
    )
    out_specs = P(("groups", "section"), None, None)
    return jax.shard_map(body, mesh=mesh, in_specs=in_specs, out_specs=out_specs, check_vma=False)
```

```python
import functools

import jax
import jax.numpy as jnp
import numpy as np
from jax import lax
from jax.experimental import pallas as pl
from jax.experimental.pallas import tpu as pltpu
from jax.sharding import PartitionSpec as P

HEADS = 16
KV_HEADS = 8
HD = 128
TICKS = 4
MAX_LEN = 96
CUTS = (0, 512, 1024)
EXTRA = 16
LIFT = 16.0
HIDDEN = -1e30
PAIR = 2 * HD
Q_WIDTH = HEADS * HD
KV_WIDTH = KV_HEADS * HD
BF16 = jnp.bfloat16
F32 = jnp.float32


def rope_table():
    middle = HD // 2
    spacing = 1000000.0 ** (-2.0 * np.arange(middle) / HD)
    angles = np.arange(MAX_LEN)[:, None] * spacing[None, :]
    cosine, sine = np.cos(angles), np.sin(angles)
    whole = np.concatenate([cosine, cosine, -sine, sine], axis=1).astype(np.float32)
    high = whole.astype(jnp.bfloat16).astype(np.float32)
    low = (whole - high).astype(jnp.bfloat16).astype(np.float32)
    return np.concatenate([high, low], axis=0)


def tables_of(ids_row, table):
    length = ids_row.shape[1]
    across = jnp.broadcast_to(ids_row, (length, length))
    down = across.T
    row_index = lax.broadcasted_iota(jnp.int32, (length, length), 0)
    column = lax.broadcasted_iota(jnp.int32, (length, length), 1)
    matched = across == down
    places = jnp.sum(jnp.where(matched & (column < row_index), 1.0, 0.0), axis=1, keepdims=True)
    bias = jnp.where(matched & (column <= row_index), 0.0, HIDDEN)
    slots = lax.broadcasted_iota(jnp.int32, (length, 2 * MAX_LEN), 1)
    slots = jnp.where(slots >= MAX_LEN, slots - MAX_LEN, slots).astype(F32)
    one_hot = jnp.where(slots == places, 1.0, 0.0).astype(BF16)
    factors = jnp.dot(one_hot, table, preferred_element_type=F32)
    return factors, bias


def rotated(values, cosine, sine):
    return values * cosine + pltpu.roll(values, HD // 2, 1) * sine


def squares(x):
    total = x[:, :HD] * x[:, :HD]
    for start in range(HD, x.shape[1], HD):
        part = x[:, start : start + HD]
        total = total + part * part
    return total


def tiles_of():
    tiles = [("k", start, start) for start in range(0, KV_WIDTH, PAIR)]
    tiles += [("v", start, KV_WIDTH + start) for start in range(0, KV_WIDTH, PAIR)]
    return tiles + [("q", start, 2 * KV_WIDTH + start) for start in range(0, Q_WIDTH, PAIR)]


def partial_products(lifted, slab, weights, acc_ref, source):
    for name, start, place in tiles_of():
        got = jnp.dot(lifted, weights[name][slab, start : start + PAIR], preferred_element_type=F32)
        if source is not None:
            got = got + source[:, place : place + PAIR]
        acc_ref[:, place : place + PAIR] = got


def attention(lifted, slab, total, weights, acc_ref, cos_ref, bias_ref, k_ref, v_ref, mixed_ref):
    length, model = lifted.shape[0], weights["k"].shape[0]
    mean = jnp.sum(total, axis=1, keepdims=True) * (1.0 / model)
    scale = lax.rsqrt(mean + 1e-05) * (1.0 / LIFT)
    cosine = cos_ref[:, :HD] * scale
    sine = cos_ref[:, HD:] * scale
    factor = HD ** (-0.5) * np.log2(np.e)
    cosine_q = cosine * factor
    sine_q = sine * factor
    bias = bias_ref[...]
    ones = jnp.ones((length, HD), BF16)

    def whole(tile):
        name, start, place = tile
        got = jnp.dot(lifted, weights[name][slab, start : start + PAIR], preferred_element_type=F32)
        return got + acc_ref[:, place : place + PAIR]

    def query(tile):
        got = whole(tile)
        upper = rotated(got[:, :HD], cosine_q, sine_q)
        lower = rotated(got[:, HD:], cosine_q, sine_q)
        return jnp.concatenate([upper, lower], axis=0).astype(BF16)

    def score(group, queries):
        key_rows = k_ref[:, group * HD : (group + 1) * HD]
        scores = lax.dot_general(queries, key_rows, (((1,), (1,)), ((), ())), preferred_element_type=F32)
        return scores.reshape(2, length, length) + bias[None]

    def exponents(scores):
        most = jnp.max(scores, axis=2, keepdims=True)
        return jnp.exp2(scores - most).astype(BF16).reshape(2 * length, length)

    def mix(group, expo):
        value_rows = v_ref[:, group * HD : (group + 1) * HD]
        got = jnp.dot(expo, jnp.concatenate([value_rows, ones], axis=1), preferred_element_type=F32)
        mixed = (got[:, :HD] / got[:, HD:]).astype(BF16)
        mixed_ref[:, group * PAIR : group * PAIR + HD] = mixed[:length]
        mixed_ref[:, group * PAIR + HD : (group + 1) * PAIR] = mixed[length:]

    queries, scores, expo = {}, {}, {}
    for tile in tiles_of():
        name, start, place = tile
        if name == "k":
            got = whole(tile)
            for half in range(0, PAIR, HD):
                k_ref[:, start + half : start + half + HD] = rotated(
                    got[:, half : half + HD], cosine, sine
                ).astype(BF16)
        elif name == "v":
            v_ref[:, start : start + PAIR] = (whole(tile) * scale).astype(BF16)
    heads = [tile for tile in tiles_of() if tile[0] == "q"]
    for step in range(KV_HEADS + 3):
        if step < KV_HEADS:
            queries[step] = query(heads[step])
        if 0 <= step - 1 < KV_HEADS:
            scores[step - 1] = score(step - 1, queries.pop(step - 1))
        if 0 <= step - 2 < KV_HEADS:
            expo[step - 2] = exponents(scores.pop(step - 2))
        if 0 <= step - 3 < KV_HEADS:
            mix(step - 3, expo.pop(step - 3))


def out_columns(low, high, mixed_ref, wo_ref, x_ref, out_ref, base):
    length = mixed_ref.shape[0]
    for start in range(low, high, PAIR):
        update = jnp.dot(mixed_ref[...], wo_ref[:, start : start + PAIR], preferred_element_type=F32)
        lanes = slice(start - base, start - base + PAIR)
        out_ref[:length, lanes] = (x_ref[:length, lanes].astype(F32) + update).astype(BF16)


def write_ids(ids_row, out_ref):
    length = ids_row.shape[1]
    out_ref[length:, :] = jnp.zeros((EXTRA, out_ref.shape[1]), BF16)
    out_ref[length:, :length] = jnp.broadcast_to(ids_row, (EXTRA, length)).astype(BF16)


def opening_kernel(
    x_hbm, ids_hbm, gain_hbm, table_hbm, wq_hbm, wk_hbm, wv_hbm, wo_hbm,
    out_ref, mixed_ref, x_last, wq_ref, wk_ref, wv_ref, wo_ref, gain_ref, table_ref,
    x_ref, ids_ref, raw_gain, raw_table, acc_ref, cos_ref, bias_ref, k_ref, v_ref, small_sems, sems,
):
    length, model = x_ref.shape
    slabs = [slice(low, low + PAIR) for low in range(0, model, PAIR)]
    small = [
        pltpu.make_async_copy(x_hbm.at[0], x_ref, small_sems.at[0]),
        pltpu.make_async_copy(gain_hbm, raw_gain, small_sems.at[1]),
        pltpu.make_async_copy(ids_hbm, ids_ref, small_sems.at[2]),
        pltpu.make_async_copy(table_hbm, raw_table, small_sems.at[3]),
        pltpu.make_async_copy(x_hbm.at[0, :, CUTS[1] :], x_last, small_sems.at[4]),
    ]
    for copy in small:
        copy.start()
    copies = {}
    for slab in slabs:
        for name, source, target in (("k", wk_hbm, wk_ref), ("v", wv_hbm, wv_ref), ("q", wq_hbm, wq_ref)):
            copy = pltpu.make_async_copy(source.at[0, slab], target.at[slab], sems.at[len(copies)])
            copies[name, slab.start] = copy
            copy.start()
    quarter = wo_ref.shape[0] // 4
    for low in range(0, wo_ref.shape[0], quarter):
        rows = slice(low, low + quarter)
        copy = pltpu.make_async_copy(wo_hbm.at[0, rows], wo_ref.at[rows], sems.at[len(copies)])
        copies["o", low] = copy
        copy.start()
    for copy in small[:4]:
        copy.wait()
    gain_ref[...] = raw_gain[...].astype(F32) * LIFT
    table_ref[...] = raw_table[...].astype(BF16)
    ids_row = ids_ref[...].astype(F32)
    factors, bias = tables_of(ids_row, table_ref[...])
    cos_ref[...] = factors
    bias_ref[...] = bias
    write_ids(ids_row, out_ref)
    x = x_ref[...].astype(F32)
    total = squares(x)
    lifted = (x * gain_ref[...]).astype(BF16)
    weights = {"k": wk_ref, "v": wv_ref, "q": wq_ref}
    for index, slab in enumerate(slabs):
        for name in "kvq":
            copies[name, slab.start].wait()
        if index + 1 < len(slabs):
            partial_products(lifted[:, slab], slab, weights, acc_ref, acc_ref if index else None)
    attention(
        lifted[:, slabs[-1]], slabs[-1], total, weights, acc_ref, cos_ref, bias_ref, k_ref, v_ref, mixed_ref
    )
    for low in range(0, wo_ref.shape[0], quarter):
        copies["o", low].wait()
    small[4].wait()
    out_columns(CUTS[0], CUTS[1], mixed_ref, wo_ref, x_ref, out_ref, 0)


def first_kernel(
    x_ref, gain_ref, table_ref, wq_ref, wk_ref, wv_ref, acc_ref, total_ref, cos_ref, bias_ref
):
    length = x_ref.shape[0] - EXTRA
    slab = slice(CUTS[0], CUTS[1])
    x = x_ref[:length, :].astype(F32)
    lifted = (x * gain_ref[:, slab]).astype(BF16)
    partial_products(lifted, slab, {"k": wk_ref, "v": wv_ref, "q": wq_ref}, acc_ref, None)
    total_ref[...] = squares(x)
    factors, bias = tables_of(x_ref[length:, :length].astype(F32)[:1], table_ref[...])
    cos_ref[...] = factors
    bias_ref[...] = bias


def second_kernel(
    last, x_first, x_ref, gain_ref, wq_ref, wk_ref, wv_ref, wo_ref, acc_ref, total_ref, cos_ref, bias_ref, *refs
):
    k_ref, v_ref = refs[-2:]
    mixed_ref = refs[-3]
    out_ref = refs[0]
    length = x_ref.shape[0]
    slab = slice(CUTS[1], CUTS[2])
    x = x_ref[...].astype(F32)
    lifted = (x * gain_ref[:, slab]).astype(BF16)
    total = total_ref[...] + squares(x)
    attention(
        lifted, slab, total, {"k": wk_ref, "v": wv_ref, "q": wq_ref}, acc_ref, cos_ref, bias_ref,
        k_ref, v_ref, mixed_ref,
    )
    if last:
        whole = out_ref.at[0]
        out_columns(CUTS[0], CUTS[1], mixed_ref, wo_ref, x_first, whole.at[:, : CUTS[1]], 0)
        out_columns(CUTS[1], CUTS[2], mixed_ref, wo_ref, x_ref, whole.at[:, CUTS[1] :], CUTS[1])
    else:
        out_ref[length:, :] = x_first[length:, :]
        out_columns(CUTS[0], CUTS[1], mixed_ref, wo_ref, x_first, out_ref, 0)


def third_kernel(mixed_ref, x_ref, wo_ref, out_ref):
    out_columns(CUTS[1], CUTS[2], mixed_ref, wo_ref, x_ref, out_ref, CUTS[1])


VMEM = pl.BlockSpec(memory_space=pltpu.VMEM)
HBM = pl.BlockSpec(memory_space=pltpu.HBM)


def kept(shape, dtype):
    return pltpu.VMEM(shape, dtype)


def held(array):
    return pltpu.with_memory_space_constraint(array, pltpu.VMEM)


def left(array):
    return pltpu.with_memory_space_constraint(array, pltpu.HBM)


def passed_along(array, by):
    length = lax.axis_size("section")
    return lax.ppermute(array, "section", [(i, (i + by) % length) for i in range(length)])


def body(micro, segment, gain, w_query, w_key, w_value, w_out):
    length, model = micro.shape[1], micro.shape[2]
    limits = pltpu.CompilerParams(vmem_limit_bytes=32 * 1024 * 1024)
    table = jnp.asarray(rope_table())
    near, far = CUTS[1], CUTS[2] - CUTS[1]
    acc_width = 2 * KV_WIDTH + Q_WIDTH
    mixing = [pltpu.VMEM((length, KV_WIDTH), BF16)] * 2

    def call(kernel, name, shapes, scratch, args):
        shapes = tuple(shapes)
        return pl.pallas_call(
            kernel, out_shape=shapes, in_specs=[VMEM] * len(args), out_specs=(VMEM,) * len(shapes),
            scratch_shapes=scratch, compiler_params=limits, name=name,
        )(*map(held, args))

    out, mixed, x_last, wq, wk, wv, wo, gain, table = pl.pallas_call(
        opening_kernel,
        out_shape=(
            kept((length + EXTRA, near), BF16),
            kept((length, Q_WIDTH), BF16),
            kept((length, far), BF16),
            kept((model, Q_WIDTH), BF16),
            kept((model, KV_WIDTH), BF16),
            kept((model, KV_WIDTH), BF16),
            kept((Q_WIDTH, model), BF16),
            kept((1, model), F32),
            kept(table.shape, BF16),
        ),
        in_specs=[HBM] * 8,
        out_specs=(VMEM,) * 9,
        scratch_shapes=[
            pltpu.VMEM((length, model), BF16),
            pltpu.VMEM(segment.shape, jnp.int32),
            pltpu.VMEM(gain.shape, BF16),
            pltpu.VMEM(table.shape, F32),
            pltpu.VMEM((length, acc_width), F32),
            pltpu.VMEM((length, PAIR), F32),
            pltpu.VMEM((length, length), F32),
            *mixing,
            pltpu.SemaphoreType.DMA((5,)),
            pltpu.SemaphoreType.DMA((3 * (model // PAIR) + 4,)),
        ],
        compiler_params=limits,
        name="opening",
    )(*(left(array) for array in (micro, segment, gain, table, w_query, w_key, w_value, w_out)))

    for tick_index in range(1, TICKS):
        x_first = passed_along(out, 1)
        (rest,) = call(third_kernel, "third", [kept((length, far), BF16)], [], (mixed, x_last, wo))
        x_last = passed_along(rest, 1)
        state = call(
            first_kernel, "first",
            [
                kept((length, acc_width), F32), kept((length, HD), F32),
                kept((length, PAIR), F32), kept((length, length), F32),
            ],
            [], (x_first, gain, table, wq, wk, wv),
        )
        last = tick_index == TICKS - 1
        if last:
            shapes = [jax.ShapeDtypeStruct((1, length, model), BF16)]
            scratch = [pltpu.VMEM((length, Q_WIDTH), BF16), *mixing]
        else:
            shapes = [kept((length + EXTRA, near), BF16), kept((length, Q_WIDTH), BF16)]
            scratch = mixing
        got = call(
            functools.partial(second_kernel, last), "second", shapes, scratch,
            (x_first, x_last, gain, wq, wk, wv, wo, *state),
        )
        if last:
            return got[0]
        out, mixed = got


def solution(mesh):
    in_specs = (
        P(("groups", "section"), None, None),
        P(("groups", "section"), None),
        P("section", None),
        P("section", None, None),
        P("section", None, None),
        P("section", None, None),
        P("section", None, None),
    )
    out_specs = P(("groups", "section"), None, None)
    return jax.shard_map(body, mesh=mesh, in_specs=in_specs, out_specs=out_specs, check_vma=False)
```

```python
import functools

import jax
import jax.numpy as jnp
import numpy as np
from jax import lax
from jax.experimental import pallas as pl
from jax.experimental.pallas import tpu as pltpu
from jax.sharding import PartitionSpec as P

HEADS = 16
KV_HEADS = 8
HD = 128
TICKS = 4
MAX_LEN = 96
CHUNKS = 3
EXTRA = 16
LIFT = 16.0
HIDDEN = -1e30
PAIR = 2 * HD
Q_WIDTH = HEADS * HD
KV_WIDTH = KV_HEADS * HD
BF16 = jnp.bfloat16
F32 = jnp.float32


def rope_table():
    middle = HD // 2
    spacing = 1000000.0 ** (-2.0 * np.arange(middle) / HD)
    angles = np.arange(MAX_LEN)[:, None] * spacing[None, :]
    cosine, sine = np.cos(angles), np.sin(angles)
    whole = np.concatenate([cosine, cosine, -sine, sine], axis=1).astype(np.float32)
    high = whole.astype(jnp.bfloat16).astype(np.float32)
    low = (whole - high).astype(jnp.bfloat16).astype(np.float32)
    return np.concatenate([high, low], axis=0)


def tables_of(ids_row, table):
    length = ids_row.shape[1]
    across = jnp.broadcast_to(ids_row, (length, length))
    down = across.T
    row_index = lax.broadcasted_iota(jnp.int32, (length, length), 0)
    column = lax.broadcasted_iota(jnp.int32, (length, length), 1)
    matched = across == down
    places = jnp.sum(jnp.where(matched & (column < row_index), 1.0, 0.0), axis=1, keepdims=True)
    bias = jnp.where(matched & (column <= row_index), 0.0, HIDDEN)
    slots = lax.broadcasted_iota(jnp.int32, (length, 2 * MAX_LEN), 1)
    slots = jnp.where(slots >= MAX_LEN, slots - MAX_LEN, slots).astype(F32)
    one_hot = jnp.where(slots == places, 1.0, 0.0).astype(BF16)
    factors = jnp.dot(one_hot, table, preferred_element_type=F32)
    return factors, bias


def rotated(values, cosine, sine):
    return values * cosine + pltpu.roll(values, HD // 2, 1) * sine


def layer(x, gain, weights, wait, cos_rows, bias_rows, kept_keys, kept_values, k_ref, v_ref, mixed_ref, write):
    size, model = x.shape
    wq_ref, wk_ref, wv_ref, wo_ref = weights
    scale = lax.rsqrt(jnp.mean(x * x, axis=1, keepdims=True) + 1e-05) * (1.0 / LIFT)
    lifted = (x * gain).astype(BF16)
    cosine = cos_rows[:, :HD] * scale
    sine = cos_rows[:, HD:] * scale
    factor = HD ** (-0.5) * np.log2(np.e)
    cosine_q = cosine * factor
    sine_q = sine * factor

    for start in range(0, KV_WIDTH, PAIR):
        wait("k", start)
        got = jnp.dot(lifted, wk_ref[:, start : start + PAIR], preferred_element_type=F32)
        for half in range(0, PAIR, HD):
            turned = rotated(got[:, half : half + HD], cosine, sine)
            k_ref[:, start + half : start + half + HD] = turned.astype(BF16)
    for start in range(0, KV_WIDTH, PAIR):
        wait("v", start)
        got = jnp.dot(lifted, wv_ref[:, start : start + PAIR], preferred_element_type=F32)
        v_ref[:, start : start + PAIR] = (got * scale).astype(BF16)
    queries = []
    for start in range(0, Q_WIDTH, PAIR):
        wait("q", start)
        got = jnp.dot(lifted, wq_ref[:, start : start + PAIR], preferred_element_type=F32)
        upper = rotated(got[:, :HD], cosine_q, sine_q)
        lower = rotated(got[:, HD:], cosine_q, sine_q)
        queries.append(jnp.concatenate([upper, lower], axis=0).astype(BF16))

    count = bias_rows.shape[1]
    ones = jnp.ones((count, HD), BF16)
    groups = range(KV_HEADS)
    scores = []
    for group in groups:
        lanes = slice(group * HD, (group + 1) * HD)
        key_rows = jnp.concatenate([rows[:, lanes] for rows in kept_keys] + [k_ref[:, lanes]], axis=0)
        got = lax.dot_general(queries[group], key_rows, (((1,), (1,)), ((), ())), preferred_element_type=F32)
        scores.append(got.reshape(2, size, count) + bias_rows[None])
    most = [jnp.max(part, axis=2, keepdims=True) for part in scores]
    expo = [jnp.exp2(scores[g] - most[g]).astype(BF16).reshape(2 * size, count) for g in groups]
    got = []
    for group in groups:
        lanes = slice(group * HD, (group + 1) * HD)
        value_rows = jnp.concatenate([rows[:, lanes] for rows in kept_values] + [v_ref[:, lanes]], axis=0)
        value_rows = jnp.concatenate([value_rows, ones], axis=1)
        got.append(jnp.dot(expo[group], value_rows, preferred_element_type=F32))
    for group in groups:
        total = got[group][:, HD:]
        inverse = pl.reciprocal(total, approx=True)
        inverse = inverse * (2.0 - total * inverse)
        mixed = (got[group][:, :HD] * inverse).astype(BF16)
        mixed_ref[:, group * PAIR : group * PAIR + HD] = mixed[:size]
        mixed_ref[:, group * PAIR + HD : (group + 1) * PAIR] = mixed[size:]
    for start in range(0, model, PAIR):
        wait("o", start)
        update = jnp.dot(mixed_ref[...], wo_ref[:, start : start + PAIR], preferred_element_type=F32)
        write(start, x[:, start : start + PAIR] + update)


def first_key(low):
    return max(0, low - MAX_LEN + 1) // 16 * 16


def kept_rows(index, size, refs):
    least = first_key(index * size)
    return [ref[max(0, least - place * size) :] for place, ref in enumerate(refs) if (place + 1) * size > least]


def write_ids(ids_row, out_ref, size):
    length = ids_row.shape[1]
    out_ref[size:, :] = jnp.zeros((EXTRA, out_ref.shape[1]), BF16)
    out_ref[size:, :length] = jnp.broadcast_to(ids_row, (EXTRA, length)).astype(BF16)


def opening_kernel(
    size, x_hbm, ids_hbm, gain_hbm, table_hbm, wq_hbm, wk_hbm, wv_hbm, wo_hbm,
    out_ref, k_ref, v_ref, cos_ref, bias_ref, wq_ref, wk_ref, wv_ref, wo_ref, gain_ref, table_ref, *refs,
):
    rest_refs, refs = refs[: CHUNKS - 1], refs[CHUNKS - 1 :]
    x_ref, ids_ref, raw_gain, raw_table, mixed_ref, small_sems, sems = refs
    small = [
        pltpu.make_async_copy(ids_hbm, ids_ref, small_sems.at[0]),
        pltpu.make_async_copy(table_hbm, raw_table, small_sems.at[1]),
        pltpu.make_async_copy(gain_hbm, raw_gain, small_sems.at[2]),
        pltpu.make_async_copy(x_hbm.at[0, :size], x_ref, small_sems.at[3]),
    ]
    late = [
        pltpu.make_async_copy(x_hbm.at[0, (i + 1) * size : (i + 2) * size], rest_refs[i], small_sems.at[4 + i])
        for i in range(CHUNKS - 1)
    ]
    made = []

    def batch(source, target, rows, lanes):
        step = (rows.stop - rows.start) // 4
        copies = []
        for low in range(rows.start, rows.stop, step):
            part = (slice(low, low + step), lanes)
            copies.append(pltpu.make_async_copy(source.at[(0, *part)], target.at[part], sems.at[len(made)]))
            made.append(copies[-1])
        return copies

    model, half = wk_ref.shape[0], Q_WIDTH // 2
    everything = slice(0, model)
    batches = [
        batch(wk_hbm, wk_ref, everything, slice(0, KV_WIDTH)),
        batch(wv_hbm, wv_ref, everything, slice(0, KV_WIDTH)),
        batch(wq_hbm, wq_ref, everything, slice(0, half)),
        batch(wq_hbm, wq_ref, everything, slice(half, Q_WIDTH)),
        batch(wo_hbm, wo_ref, slice(0, Q_WIDTH), slice(0, model // 2)),
        batch(wo_hbm, wo_ref, slice(0, Q_WIDTH), slice(model // 2, model)),
    ]
    arrivals = {("k", 0): 0, ("v", 0): 1, ("q", 0): 2, ("q", half): 3, ("o", 0): 4, ("o", model // 2): 5}

    def begin(index):
        if index < len(batches):
            for copy in batches[index]:
                copy.start()
        if index == len(batches):
            for copy in late:
                copy.start()

    def wait(name, start):
        index = arrivals.get((name, start))
        if index is not None:
            for copy in batches[index]:
                copy.wait()
            begin(index + 2)

    for copy in small:
        copy.start()
    begin(0)
    begin(1)
    for copy in small:
        copy.wait()
    gain_ref[...] = raw_gain[...].astype(F32) * LIFT
    table_ref[...] = raw_table[...].astype(BF16)
    ids_row = ids_ref[...].astype(F32)
    factors, bias = tables_of(ids_row, table_ref[...])
    cos_ref[...] = factors
    bias_ref[...] = bias
    write_ids(ids_row, out_ref, size)

    def write(start, values):
        out_ref[:size, start : start + PAIR] = values.astype(BF16)

    layer(
        x_ref[...].astype(F32), gain_ref[...], (wq_ref, wk_ref, wv_ref, wo_ref), wait,
        cos_ref[:size, :], bias_ref[:size, :size], [], [], k_ref, v_ref, mixed_ref, write,
    )
    for copy in late:
        copy.wait()


def chunk_kernel(index, last, x_ref, gain_ref, wq_ref, wk_ref, wv_ref, wo_ref, *refs):
    refs = list(refs)
    mixed_ref = refs.pop(-1)
    size = mixed_ref.shape[0]
    low, high = index * size, (index + 1) * size
    if index == 0:
        table_ref = refs.pop(0)
        out_ref, k_ref, v_ref, cos_ref, bias_ref = refs
        factors, bias = tables_of(x_ref[size:, : CHUNKS * size].astype(F32)[:1], table_ref[...])
        cos_ref[...] = factors
        bias_ref[...] = bias
        if not last:
            out_ref[size:, :] = x_ref[size:, :]
        keys, values = [], []
    else:
        cos_ref, bias_ref = refs[:2]
        keys, values, refs = refs[2 : 2 + index], refs[2 + index : 2 + 2 * index], refs[2 + 2 * index :]
        if last and index == CHUNKS - 1:
            done, (whole_ref, out_ref, k_ref, v_ref, sems) = refs[:index], refs[index:]
            copies = [
                pltpu.make_async_copy(done[i].at[:size], whole_ref.at[0, i * size : (i + 1) * size], sems.at[i])
                for i in range(index)
            ]
            for copy in copies:
                copy.start()
        else:
            out_ref, k_ref, v_ref = refs

    def write(start, result):
        out_ref[:size, start : start + PAIR] = result.astype(BF16)

    layer(
        x_ref[:size, :].astype(F32), gain_ref[...], (wq_ref, wk_ref, wv_ref, wo_ref), lambda name, start: None,
        cos_ref[low:high, :], bias_ref[low:high, first_key(low) : high],
        kept_rows(index, size, keys), kept_rows(index, size, values), k_ref, v_ref, mixed_ref, write,
    )
    if last and index == CHUNKS - 1:
        copy = pltpu.make_async_copy(out_ref, whole_ref.at[0, low:high], sems.at[index])
        copy.start()
        for each in copies + [copy]:
            each.wait()


VMEM = pl.BlockSpec(memory_space=pltpu.VMEM)
HBM = pl.BlockSpec(memory_space=pltpu.HBM)


def kept(shape, dtype):
    return pltpu.VMEM(shape, dtype)


def held(array):
    return pltpu.with_memory_space_constraint(array, pltpu.VMEM)


def left(array):
    return pltpu.with_memory_space_constraint(array, pltpu.HBM)


def passed_along(array, by):
    length = lax.axis_size("section")
    return lax.ppermute(array, "section", [(i, (i + by) % length) for i in range(length)])


def body(micro, segment, gain, w_query, w_key, w_value, w_out):
    length, model = micro.shape[1], micro.shape[2]
    size = length // CHUNKS
    limits = pltpu.CompilerParams(vmem_limit_bytes=32 * 1024 * 1024)
    table = jnp.asarray(rope_table())
    rows = [size + EXTRA] + [size] * (CHUNKS - 1)
    key_values = [kept((size, KV_WIDTH), BF16)] * 2
    tables = [kept((length, PAIR), F32), kept((length, length), F32)]
    mixing = pltpu.VMEM((size, Q_WIDTH), BF16)

    got = pl.pallas_call(
        functools.partial(opening_kernel, size),
        out_shape=(
            kept((rows[0], model), BF16),
            *key_values,
            *tables,
            kept((model, Q_WIDTH), BF16),
            kept((model, KV_WIDTH), BF16),
            kept((model, KV_WIDTH), BF16),
            kept((Q_WIDTH, model), BF16),
            kept((1, model), F32),
            kept(table.shape, BF16),
            *[kept((size, model), BF16)] * (CHUNKS - 1),
        ),
        in_specs=[HBM] * 8,
        out_specs=(VMEM,) * (10 + CHUNKS),
        scratch_shapes=[
            pltpu.VMEM((size, model), BF16),
            pltpu.VMEM(segment.shape, jnp.int32),
            pltpu.VMEM(gain.shape, BF16),
            pltpu.VMEM(table.shape, F32),
            mixing,
            pltpu.SemaphoreType.DMA((3 + CHUNKS,)),
            pltpu.SemaphoreType.DMA((24,)),
        ],
        compiler_params=limits,
        name="opening",
    )(*(left(array) for array in (micro, segment, gain, table, w_query, w_key, w_value, w_out)))
    out, k_rows, v_rows, cosines, bias = got[:5]
    weights = (got[9], *got[5:9])
    table = got[10]
    streams = [out, *got[11:]]

    for tick_index in range(TICKS):
        last = tick_index == TICKS - 1
        outs, keys, values = [], [], []
        for index in range(CHUNKS):
            if tick_index == 0 and index == 0:
                outs.append(passed_along(streams[0], 1))
                keys.append(k_rows)
                values.append(v_rows)
                continue
            args = [streams[index], *weights]
            shapes = [kept((rows[index], model), BF16), *key_values]
            scratch = [mixing]
            if index == 0:
                args.append(table)
                shapes += tables
            else:
                args += [cosines, bias, *keys, *values]
            specs = [VMEM] * len(shapes)
            ending = last and index == CHUNKS - 1
            if ending:
                args += outs
                shapes = [jax.ShapeDtypeStruct((1, length, model), BF16)]
                specs = [pl.BlockSpec(memory_space=pl.ANY)]
                scratch = [
                    pltpu.VMEM((size, model), BF16), *[pltpu.VMEM((size, KV_WIDTH), BF16)] * 2,
                    pltpu.SemaphoreType.DMA((CHUNKS,)), mixing,
                ]
            got = pl.pallas_call(
                functools.partial(chunk_kernel, index, last),
                out_shape=tuple(shapes), in_specs=[VMEM] * len(args), out_specs=tuple(specs),
                scratch_shapes=scratch, compiler_params=limits, name="chunk_%d_%d" % (tick_index, index),
            )(*map(held, args))
            if ending:
                return got[0]
            if index == 0:
                cosines, bias = got[3:]
            keys.append(got[1])
            values.append(got[2])
            outs.append(got[0] if last else passed_along(got[0], 1))
        streams = outs


def solution(mesh):
    in_specs = (
        P(("groups", "section"), None, None),
        P(("groups", "section"), None),
        P("section", None),
        P("section", None, None),
        P("section", None, None),
        P("section", None, None),
        P("section", None, None),
    )
    out_specs = P(("groups", "section"), None, None)
    return jax.shard_map(body, mesh=mesh, in_specs=in_specs, out_specs=out_specs, check_vma=False)
```

```python
import functools

import jax
import jax.numpy as jnp
import numpy as np
from jax import lax
from jax.experimental import pallas as pl
from jax.experimental.pallas import tpu as pltpu
from jax.sharding import PartitionSpec as P

HEADS = 16
KV_HEADS = 8
HD = 128
TICKS = 4
MAX_LEN = 96
CHUNKS = 2
EXTRA = 16
LIFT = 16.0
HIDDEN = -1e30
PAIR = 2 * HD
Q_WIDTH = HEADS * HD
KV_WIDTH = KV_HEADS * HD
BF16 = jnp.bfloat16
F32 = jnp.float32


def rope_table():
    middle = HD // 2
    spacing = 1000000.0 ** (-2.0 * np.arange(middle) / HD)
    angles = np.arange(MAX_LEN)[:, None] * spacing[None, :]
    cosine, sine = np.cos(angles), np.sin(angles)
    whole = np.concatenate([cosine, cosine, -sine, sine], axis=1).astype(np.float32)
    high = whole.astype(jnp.bfloat16).astype(np.float32)
    low = (whole - high).astype(jnp.bfloat16).astype(np.float32)
    return np.concatenate([high, low], axis=0)


def tables_of(ids_row, table):
    length = ids_row.shape[1]
    across = jnp.broadcast_to(ids_row, (length, length))
    down = across.T
    row_index = lax.broadcasted_iota(jnp.int32, (length, length), 0)
    column = lax.broadcasted_iota(jnp.int32, (length, length), 1)
    matched = across == down
    places = jnp.sum(jnp.where(matched & (column < row_index), 1.0, 0.0), axis=1, keepdims=True)
    bias = jnp.where(matched & (column <= row_index), 0.0, HIDDEN)
    slots = lax.broadcasted_iota(jnp.int32, (length, 2 * MAX_LEN), 1)
    slots = jnp.where(slots >= MAX_LEN, slots - MAX_LEN, slots).astype(F32)
    one_hot = jnp.where(slots == places, 1.0, 0.0).astype(BF16)
    factors = jnp.dot(one_hot, table, preferred_element_type=F32)
    return factors, bias


def rotated(values, cosine, sine):
    return values * cosine + pltpu.roll(values, HD // 2, 1) * sine


def layer(x, gain, weights, wait, cos_rows, bias_rows, kept_keys, kept_values, k_ref, v_ref, mixed_ref, write):
    size, model = x.shape
    wq_ref, wk_ref, wv_ref, wo_ref = weights
    scale = lax.rsqrt(jnp.mean(x * x, axis=1, keepdims=True) + 1e-05) * (1.0 / LIFT)
    lifted = (x * gain).astype(BF16)
    cosine = cos_rows[:, :HD] * scale
    sine = cos_rows[:, HD:] * scale
    factor = HD ** (-0.5) * np.log2(np.e)
    cosine_q = cosine * factor
    sine_q = sine * factor

    for start in range(0, KV_WIDTH, PAIR):
        wait("k", start)
        got = jnp.dot(lifted, wk_ref[:, start : start + PAIR], preferred_element_type=F32)
        for half in range(0, PAIR, HD):
            turned = rotated(got[:, half : half + HD], cosine, sine)
            k_ref[:, start + half : start + half + HD] = turned.astype(BF16)
    for start in range(0, KV_WIDTH, PAIR):
        wait("v", start)
        got = jnp.dot(lifted, wv_ref[:, start : start + PAIR], preferred_element_type=F32)
        v_ref[:, start : start + PAIR] = (got * scale).astype(BF16)
    queries = []
    for start in range(0, Q_WIDTH, PAIR):
        wait("q", start)
        got = jnp.dot(lifted, wq_ref[:, start : start + PAIR], preferred_element_type=F32)
        upper = rotated(got[:, :HD], cosine_q, sine_q)
        lower = rotated(got[:, HD:], cosine_q, sine_q)
        queries.append(jnp.concatenate([upper, lower], axis=0).astype(BF16))

    count = bias_rows.shape[1]
    ones = jnp.ones((count, HD), BF16)
    groups = range(KV_HEADS)
    scores = []
    for group in groups:
        lanes = slice(group * HD, (group + 1) * HD)
        key_rows = jnp.concatenate([rows[:, lanes] for rows in kept_keys] + [k_ref[:, lanes]], axis=0)
        got = lax.dot_general(queries[group], key_rows, (((1,), (1,)), ((), ())), preferred_element_type=F32)
        scores.append(got.reshape(2, size, count) + bias_rows[None])
    most = [jnp.max(part, axis=2, keepdims=True) for part in scores]
    expo = [jnp.exp2(scores[g] - most[g]).astype(BF16).reshape(2 * size, count) for g in groups]
    got = []
    for group in groups:
        lanes = slice(group * HD, (group + 1) * HD)
        value_rows = jnp.concatenate([rows[:, lanes] for rows in kept_values] + [v_ref[:, lanes]], axis=0)
        value_rows = jnp.concatenate([value_rows, ones], axis=1)
        got.append(jnp.dot(expo[group], value_rows, preferred_element_type=F32))
    for group in groups:
        total = got[group][:, HD:]
        inverse = pl.reciprocal(total, approx=True)
        inverse = inverse * (2.0 - total * inverse)
        mixed = (got[group][:, :HD] * inverse).astype(BF16)
        mixed_ref[:, group * PAIR : group * PAIR + HD] = mixed[:size]
        mixed_ref[:, group * PAIR + HD : (group + 1) * PAIR] = mixed[size:]
    for start in range(0, model, PAIR):
        wait("o", start)
        update = jnp.dot(mixed_ref[...], wo_ref[:, start : start + PAIR], preferred_element_type=F32)
        write(start, x[:, start : start + PAIR] + update)


def first_key(low):
    return max(0, low - MAX_LEN + 1) // 16 * 16


def kept_rows(index, size, refs):
    least = first_key(index * size)
    return [ref[max(0, least - place * size) :] for place, ref in enumerate(refs) if (place + 1) * size > least]


def write_ids(ids_row, out_ref, size):
    length = ids_row.shape[1]
    out_ref[size:, :] = jnp.zeros((EXTRA, out_ref.shape[1]), BF16)
    out_ref[size:, :length] = jnp.broadcast_to(ids_row, (EXTRA, length)).astype(BF16)


def opening_kernel(
    size, x_hbm, ids_hbm, gain_hbm, table_hbm, wq_hbm, wk_hbm, wv_hbm, wo_hbm,
    out_ref, k_ref, v_ref, cos_ref, bias_ref, wq_ref, wk_ref, wv_ref, wo_ref, gain_ref, table_ref, *refs,
):
    rest_refs, refs = refs[: CHUNKS - 1], refs[CHUNKS - 1 :]
    x_ref, ids_ref, raw_gain, raw_table, mixed_ref, small_sems, sems = refs
    small = [
        pltpu.make_async_copy(ids_hbm, ids_ref, small_sems.at[0]),
        pltpu.make_async_copy(table_hbm, raw_table, small_sems.at[1]),
        pltpu.make_async_copy(gain_hbm, raw_gain, small_sems.at[2]),
        pltpu.make_async_copy(x_hbm.at[0, :size], x_ref, small_sems.at[3]),
    ]
    late = [
        pltpu.make_async_copy(x_hbm.at[0, (i + 1) * size : (i + 2) * size], rest_refs[i], small_sems.at[4 + i])
        for i in range(CHUNKS - 1)
    ]
    made = []

    def batch(source, target, rows, lanes):
        step = (rows.stop - rows.start) // 4
        copies = []
        for low in range(rows.start, rows.stop, step):
            part = (slice(low, low + step), lanes)
            copies.append(pltpu.make_async_copy(source.at[(0, *part)], target.at[part], sems.at[len(made)]))
            made.append(copies[-1])
        return copies

    model, half = wk_ref.shape[0], Q_WIDTH // 2
    narrow, wide = slice(0, KV_WIDTH), slice(0, Q_WIDTH)
    batches = [
        batch(wk_hbm, wk_ref, slice(0, model), narrow),
        batch(wv_hbm, wv_ref, slice(0, model), narrow),
        batch(wq_hbm, wq_ref, slice(0, model // 2), wide),
        batch(wq_hbm, wq_ref, slice(model // 2, model), wide),
        batch(wo_hbm, wo_ref, slice(0, half), slice(0, model)),
        batch(wo_hbm, wo_ref, slice(half, Q_WIDTH), slice(0, model)),
    ]
    arrivals = {("k", 0): (0,), ("v", 0): (1,), ("q", 0): (2, 3), ("o", 0): (4, 5)}

    def begin(index):
        if index < len(batches):
            for copy in batches[index]:
                copy.start()
        if index == len(batches):
            for copy in late:
                copy.start()

    def wait(name, start):
        for index in arrivals.get((name, start), ()):
            for copy in batches[index]:
                copy.wait()
            begin(index + 3)

    for copy in small:
        copy.start()
    for index in range(3):
        begin(index)
    for copy in small:
        copy.wait()
    gain_ref[...] = raw_gain[...].astype(F32) * LIFT
    table_ref[...] = raw_table[...].astype(BF16)
    ids_row = ids_ref[...].astype(F32)
    factors, bias = tables_of(ids_row, table_ref[...])
    cos_ref[...] = factors
    bias_ref[...] = bias
    write_ids(ids_row, out_ref, size)

    def write(start, values):
        out_ref[:size, start : start + PAIR] = values.astype(BF16)

    layer(
        x_ref[...].astype(F32), gain_ref[...], (wq_ref, wk_ref, wv_ref, wo_ref), wait,
        cos_ref[:size, :], bias_ref[:size, :size], [], [], k_ref, v_ref, mixed_ref, write,
    )
    for copy in late:
        copy.wait()


def chunk_kernel(index, last, x_ref, gain_ref, wq_ref, wk_ref, wv_ref, wo_ref, *refs):
    refs = list(refs)
    mixed_ref = refs.pop(-1)
    size = mixed_ref.shape[0]
    low, high = index * size, (index + 1) * size
    if index == 0:
        table_ref = refs.pop(0)
        out_ref, k_ref, v_ref, cos_ref, bias_ref = refs
        factors, bias = tables_of(x_ref[size:, : CHUNKS * size].astype(F32)[:1], table_ref[...])
        cos_ref[...] = factors
        bias_ref[...] = bias
        if not last:
            out_ref[size:, :] = x_ref[size:, :]
        keys, values = [], []
    else:
        cos_ref, bias_ref = refs[:2]
        keys, values, refs = refs[2 : 2 + index], refs[2 + index : 2 + 2 * index], refs[2 + 2 * index :]
        if last and index == CHUNKS - 1:
            done, (whole_ref, out_ref, k_ref, v_ref, sems) = refs[:index], refs[index:]
            copies = [
                pltpu.make_async_copy(done[i].at[:size], whole_ref.at[0, i * size : (i + 1) * size], sems.at[i])
                for i in range(index)
            ]
            for copy in copies:
                copy.start()
        else:
            out_ref, k_ref, v_ref = refs

    def write(start, result):
        out_ref[:size, start : start + PAIR] = result.astype(BF16)

    layer(
        x_ref[:size, :].astype(F32), gain_ref[...], (wq_ref, wk_ref, wv_ref, wo_ref), lambda name, start: None,
        cos_ref[low:high, :], bias_ref[low:high, first_key(low) : high],
        kept_rows(index, size, keys), kept_rows(index, size, values), k_ref, v_ref, mixed_ref, write,
    )
    if last and index == CHUNKS - 1:
        copy = pltpu.make_async_copy(out_ref, whole_ref.at[0, low:high], sems.at[index])
        copy.start()
        for each in copies + [copy]:
            each.wait()


VMEM = pl.BlockSpec(memory_space=pltpu.VMEM)
HBM = pl.BlockSpec(memory_space=pltpu.HBM)


def kept(shape, dtype):
    return pltpu.VMEM(shape, dtype)


def held(array):
    return pltpu.with_memory_space_constraint(array, pltpu.VMEM)


def left(array):
    return pltpu.with_memory_space_constraint(array, pltpu.HBM)


def passed_along(array, by):
    length = lax.axis_size("section")
    return lax.ppermute(array, "section", [(i, (i + by) % length) for i in range(length)])


def body(micro, segment, gain, w_query, w_key, w_value, w_out):
    length, model = micro.shape[1], micro.shape[2]
    size = length // CHUNKS
    limits = pltpu.CompilerParams(vmem_limit_bytes=32 * 1024 * 1024)
    table = jnp.asarray(rope_table())
    rows = [size + EXTRA] + [size] * (CHUNKS - 1)
    key_values = [kept((size, KV_WIDTH), BF16)] * 2
    tables = [kept((length, PAIR), F32), kept((length, length), F32)]
    mixing = pltpu.VMEM((size, Q_WIDTH), BF16)

    got = pl.pallas_call(
        functools.partial(opening_kernel, size),
        out_shape=(
            kept((rows[0], model), BF16),
            *key_values,
            *tables,
            kept((model, Q_WIDTH), BF16),
            kept((model, KV_WIDTH), BF16),
            kept((model, KV_WIDTH), BF16),
            kept((Q_WIDTH, model), BF16),
            kept((1, model), F32),
            kept(table.shape, BF16),
            *[kept((size, model), BF16)] * (CHUNKS - 1),
        ),
        in_specs=[HBM] * 8,
        out_specs=(VMEM,) * (10 + CHUNKS),
        scratch_shapes=[
            pltpu.VMEM((size, model), BF16),
            pltpu.VMEM(segment.shape, jnp.int32),
            pltpu.VMEM(gain.shape, BF16),
            pltpu.VMEM(table.shape, F32),
            mixing,
            pltpu.SemaphoreType.DMA((3 + CHUNKS,)),
            pltpu.SemaphoreType.DMA((24,)),
        ],
        compiler_params=limits,
        name="opening",
    )(*(left(array) for array in (micro, segment, gain, table, w_query, w_key, w_value, w_out)))
    out, k_rows, v_rows, cosines, bias = got[:5]
    weights = (got[9], *got[5:9])
    table = got[10]
    streams = [out, *got[11:]]

    for tick_index in range(TICKS):
        last = tick_index == TICKS - 1
        outs, keys, values = [], [], []
        for index in range(CHUNKS):
            if tick_index == 0 and index == 0:
                outs.append(passed_along(streams[0], 1))
                keys.append(k_rows)
                values.append(v_rows)
                continue
            args = [streams[index], *weights]
            shapes = [kept((rows[index], model), BF16), *key_values]
            scratch = [mixing]
            if index == 0:
                args.append(table)
                shapes += tables
            else:
                args += [cosines, bias, *keys, *values]
            specs = [VMEM] * len(shapes)
            ending = last and index == CHUNKS - 1
            if ending:
                args += outs
                shapes = [jax.ShapeDtypeStruct((1, length, model), BF16)]
                specs = [pl.BlockSpec(memory_space=pl.ANY)]
                scratch = [
                    pltpu.VMEM((size, model), BF16), *[pltpu.VMEM((size, KV_WIDTH), BF16)] * 2,
                    pltpu.SemaphoreType.DMA((CHUNKS,)), mixing,
                ]
            got = pl.pallas_call(
                functools.partial(chunk_kernel, index, last),
                out_shape=tuple(shapes), in_specs=[VMEM] * len(args), out_specs=tuple(specs),
                scratch_shapes=scratch, compiler_params=limits, name="chunk_%d_%d" % (tick_index, index),
            )(*map(held, args))
            if ending:
                return got[0]
            if index == 0:
                cosines, bias = got[3:]
            keys.append(got[1])
            values.append(got[2])
            outs.append(got[0] if last else passed_along(got[0], 1))
        streams = outs


def solution(mesh):
    in_specs = (
        P(("groups", "section"), None, None),
        P(("groups", "section"), None),
        P("section", None),
        P("section", None, None),
        P("section", None, None),
        P("section", None, None),
        P("section", None, None),
    )
    out_specs = P(("groups", "section"), None, None)
    return jax.shard_map(body, mesh=mesh, in_specs=in_specs, out_specs=out_specs, check_vma=False)
```

```python
import functools

import jax
import jax.numpy as jnp
import numpy as np
from jax import lax
from jax.experimental import pallas as pl
from jax.experimental.pallas import tpu as pltpu
from jax.sharding import PartitionSpec as P

HEADS = 16
KV_HEADS = 8
HD = 128
TICKS = 4
MAX_LEN = 96
CHUNKS = 2
EXTRA = 16
LIFT = 16.0
HIDDEN = -1e30
PAIR = 2 * HD
Q_WIDTH = HEADS * HD
KV_WIDTH = KV_HEADS * HD
BF16 = jnp.bfloat16
F32 = jnp.float32


def rope_table():
    middle = HD // 2
    spacing = 1000000.0 ** (-2.0 * np.arange(middle) / HD)
    angles = np.arange(MAX_LEN)[:, None] * spacing[None, :]
    cosine, sine = np.cos(angles), np.sin(angles)
    whole = np.concatenate([cosine, cosine, -sine, sine], axis=1).astype(np.float32)
    high = whole.astype(jnp.bfloat16).astype(np.float32)
    low = (whole - high).astype(jnp.bfloat16).astype(np.float32)
    return np.concatenate([high, low], axis=0)


def blocks_of(low, size):
    if low == 0 and size <= MAX_LEN:
        return [(0, size, 0, size)]
    step = HD - MAX_LEN
    return [(top, step, max(0, low + top - MAX_LEN), low + top + step) for top in range(0, size, step)]


def tables_of(ids_row, table):
    length = ids_row.shape[1]
    size = length // CHUNKS
    down = jnp.broadcast_to(ids_row, (HD, length)).T
    places, biases = [], []
    for low in range(0, length, size):
        for top, height, first, _ in blocks_of(low, size):
            rows = slice(low + top, low + top + height)
            row_index = lax.broadcasted_iota(jnp.int32, (height, HD), 0) + rows.start
            column = lax.broadcasted_iota(jnp.int32, (height, HD), 1) + first
            matched = jnp.broadcast_to(ids_row[:, first : first + HD], (height, HD)) == down[rows]
            earlier = jnp.where(matched & (column < row_index), 1.0, 0.0)
            places.append(jnp.sum(earlier, axis=1, keepdims=True))
            biases.append(jnp.where(matched & (column <= row_index), 0.0, HIDDEN))
    slots = lax.broadcasted_iota(jnp.int32, (length, 2 * MAX_LEN), 1)
    slots = jnp.where(slots >= MAX_LEN, slots - MAX_LEN, slots).astype(F32)
    one_hot = jnp.where(slots == jnp.concatenate(places, axis=0), 1.0, 0.0).astype(BF16)
    factors = jnp.dot(one_hot, table, preferred_element_type=F32)
    return factors, jnp.concatenate(biases, axis=0)


def rotated(values, cosine, sine):
    return values * cosine + pltpu.roll(values, HD // 2, 1) * sine


def layer(
    x, gain, weights, wait, low, cos_rows, bias_ref, kept_keys, kept_values, k_ref, v_ref, mixed_ref, write,
    split_out=False,
):
    size, model = x.shape
    wq_ref, wk_ref, wv_ref, wo_ref = weights
    scale = lax.rsqrt(jnp.mean(x * x, axis=1, keepdims=True) + 1e-05) * (1.0 / LIFT)
    lifted = (x * gain).astype(BF16)
    cosine = cos_rows[:, :HD] * scale
    sine = cos_rows[:, HD:] * scale
    factor = HD ** (-0.5) * np.log2(np.e)
    cosine_q = cosine * factor
    sine_q = sine * factor

    for start in range(0, KV_WIDTH, PAIR):
        wait("v", start)
        got = jnp.dot(lifted, wv_ref[:, start : start + PAIR], preferred_element_type=F32)
        v_ref[:, start : start + PAIR] = (got * scale).astype(BF16)
    for start in range(0, KV_WIDTH, PAIR):
        wait("k", start)
        got = jnp.dot(lifted, wk_ref[:, start : start + PAIR], preferred_element_type=F32)
        for half in range(0, PAIR, HD):
            turned = rotated(got[:, half : half + HD], cosine, sine)
            k_ref[:, start + half : start + half + HD] = turned.astype(BF16)
    queries = []
    for start in range(0, Q_WIDTH, PAIR):
        wait("q", start)
        got = jnp.dot(lifted, wq_ref[:, start : start + PAIR], preferred_element_type=F32)
        upper = rotated(got[:, :HD], cosine_q, sine_q)
        lower = rotated(got[:, HD:], cosine_q, sine_q)
        queries.append((upper.astype(BF16), lower.astype(BF16)))

    blocks = blocks_of(low, size)
    groups = range(KV_HEADS)
    spots = [(group, block) for group in groups for block in blocks]

    def seen(kept_parts, own_ref, lanes, first, last):
        parts = []
        for place, ref in enumerate([*kept_parts, own_ref]):
            start, stop = max(first, place * size), min(last, (place + 1) * size)
            if start < stop:
                parts.append(ref[start - place * size : stop - place * size, lanes])
        return parts[0] if len(parts) == 1 else jnp.concatenate(parts, axis=0)

    scores = []
    for group, (top, height, first, last) in spots:
        lanes = slice(group * HD, (group + 1) * HD)
        upper, lower = queries[group]
        both = jnp.concatenate([upper[top : top + height], lower[top : top + height]], axis=0)
        key_rows = seen(kept_keys, k_ref, lanes, first, last)
        got = lax.dot_general(both, key_rows, (((1,), (1,)), ((), ())), preferred_element_type=F32)
        bias = bias_ref[low + top : low + top + height, : last - first]
        scores.append(got.reshape(2, height, last - first) + bias[None])
    most = [jnp.max(part, axis=2, keepdims=True) for part in scores]
    expo = [
        jnp.exp2((part - peak).astype(BF16)).reshape(2 * part.shape[1], part.shape[2])
        for part, peak in zip(scores, most)
    ]
    got = []
    for (group, (top, height, first, last)), part in zip(spots, expo):
        lanes = slice(group * HD, (group + 1) * HD)
        value_rows = seen(kept_values, v_ref, lanes, first, last)
        value_rows = jnp.concatenate([value_rows, jnp.ones((last - first, HD), BF16)], axis=1)
        got.append(jnp.dot(part, value_rows, preferred_element_type=F32))
    for (group, (top, height, first, last)), part in zip(spots, got):
        total = part[:, HD:]
        inverse = pl.reciprocal(total, approx=True)
        inverse = inverse * (2.0 - total * inverse)
        mixed = (part[:, :HD] * inverse).astype(BF16)
        mixed_ref[top : top + height, group * PAIR : group * PAIR + HD] = mixed[:height]
        mixed_ref[top : top + height, group * PAIR + HD : (group + 1) * PAIR] = mixed[height:]
    half = Q_WIDTH // 2
    if split_out:
        wait("o", 0)
        updates = [
            jnp.dot(mixed_ref[:, :half], wo_ref[:half, start : start + PAIR], preferred_element_type=F32)
            for start in range(0, model, PAIR)
        ]
        wait("o", half)
        for start, update in zip(range(0, model, PAIR), updates):
            update = update + jnp.dot(
                mixed_ref[:, half:], wo_ref[half:, start : start + PAIR], preferred_element_type=F32
            )
            write(start, x[:, start : start + PAIR] + update)
        return
    for start in range(0, model, PAIR):
        update = jnp.dot(mixed_ref[...], wo_ref[:, start : start + PAIR], preferred_element_type=F32)
        write(start, x[:, start : start + PAIR] + update)


def write_ids(ids_row, out_ref, size):
    length = ids_row.shape[1]
    out_ref[size:, :] = jnp.zeros((EXTRA, out_ref.shape[1]), BF16)
    out_ref[size:, :length] = jnp.broadcast_to(ids_row, (EXTRA, length)).astype(BF16)


def opening_kernel(
    size, x_hbm, ids_hbm, gain_hbm, table_hbm, wq_hbm, wk_hbm, wv_hbm, wo_hbm,
    out_ref, k_ref, v_ref, cos_ref, bias_ref, wq_ref, wk_ref, wv_ref, wo_ref, gain_ref, table_ref, *refs,
):
    rest_refs, refs = refs[: CHUNKS - 1], refs[CHUNKS - 1 :]
    x_ref, ids_ref, raw_gain, raw_table, mixed_ref, small_sems, sems = refs
    small = [
        pltpu.make_async_copy(ids_hbm, ids_ref, small_sems.at[0]),
        pltpu.make_async_copy(table_hbm, raw_table, small_sems.at[1]),
        pltpu.make_async_copy(gain_hbm, raw_gain, small_sems.at[2]),
        pltpu.make_async_copy(x_hbm.at[0, :size], x_ref, small_sems.at[3]),
    ]
    late = [
        pltpu.make_async_copy(x_hbm.at[0, (i + 1) * size : (i + 2) * size], rest_refs[i], small_sems.at[4 + i])
        for i in range(CHUNKS - 1)
    ]
    made = []

    def batch(source, target, rows, lanes):
        step = (rows.stop - rows.start) // 4
        copies = []
        for low in range(rows.start, rows.stop, step):
            part = (slice(low, low + step), lanes)
            copies.append(pltpu.make_async_copy(source.at[(0, *part)], target.at[part], sems.at[len(made)]))
            made.append(copies[-1])
        return copies

    model, half = wk_ref.shape[0], Q_WIDTH // 2
    narrow, wide = slice(0, KV_WIDTH), slice(0, Q_WIDTH)
    batches = [
        batch(wv_hbm, wv_ref, slice(0, model), narrow),
        batch(wk_hbm, wk_ref, slice(0, model), narrow),
        batch(wq_hbm, wq_ref, slice(0, model // 2), wide),
        batch(wq_hbm, wq_ref, slice(model // 2, model), wide),
        batch(wo_hbm, wo_ref, slice(0, half), slice(0, model)),
        batch(wo_hbm, wo_ref, slice(half, Q_WIDTH), slice(0, model)),
    ]
    arrivals = {("v", 0): (0,), ("k", 0): (1,), ("q", 0): (2, 3), ("o", 0): (4,), ("o", half): (5,)}

    def begin(index):
        if index < len(batches):
            for copy in batches[index]:
                copy.start()
        if index == len(batches):
            for copy in late:
                copy.start()

    def wait(name, start):
        for index in arrivals.get((name, start), ()):
            for copy in batches[index]:
                copy.wait()
            begin(index + 4)

    for copy in small:
        copy.start()
    for index in range(4):
        begin(index)
    for copy in small:
        copy.wait()
    gain_ref[...] = raw_gain[...].astype(F32) * LIFT
    table_ref[...] = raw_table[...].astype(BF16)
    ids_row = ids_ref[...].astype(F32)
    factors, bias = tables_of(ids_row, table_ref[...])
    cos_ref[...] = factors
    bias_ref[...] = bias
    write_ids(ids_row, out_ref, size)

    def write(start, values):
        out_ref[:size, start : start + PAIR] = values.astype(BF16)

    layer(
        x_ref[...].astype(F32), gain_ref[...], (wq_ref, wk_ref, wv_ref, wo_ref), wait,
        0, cos_ref[:size, :], bias_ref, [], [], k_ref, v_ref, mixed_ref, write, split_out=True,
    )
    for copy in late:
        copy.wait()


def chunk_kernel(index, last, x_ref, gain_ref, wq_ref, wk_ref, wv_ref, wo_ref, *refs):
    refs = list(refs)
    mixed_ref = refs.pop(-1)
    size = mixed_ref.shape[0]
    low, high = index * size, (index + 1) * size
    if index == 0:
        table_ref = refs.pop(0)
        out_ref, k_ref, v_ref, cos_ref, bias_ref = refs
        factors, bias = tables_of(x_ref[size:, : CHUNKS * size].astype(F32)[:1], table_ref[...])
        cos_ref[...] = factors
        bias_ref[...] = bias
        if not last:
            out_ref[size:, :] = x_ref[size:, :]
        keys, values = [], []
    else:
        cos_ref, bias_ref = refs[:2]
        keys, values, refs = refs[2 : 2 + index], refs[2 + index : 2 + 2 * index], refs[2 + 2 * index :]
        if last and index == CHUNKS - 1:
            done, (whole_ref, out_ref, k_ref, v_ref, sems) = refs[:index], refs[index:]
            copies = [
                pltpu.make_async_copy(done[i].at[:size], whole_ref.at[0, i * size : (i + 1) * size], sems.at[i])
                for i in range(index)
            ]
            for copy in copies:
                copy.start()
        else:
            out_ref, k_ref, v_ref = refs

    def write(start, result):
        out_ref[:size, start : start + PAIR] = result.astype(BF16)

    layer(
        x_ref[:size, :].astype(F32), gain_ref[...], (wq_ref, wk_ref, wv_ref, wo_ref), lambda name, start: None,
        low, cos_ref[low:high, :], bias_ref, keys, values, k_ref, v_ref, mixed_ref, write,
    )
    if last and index == CHUNKS - 1:
        copy = pltpu.make_async_copy(out_ref, whole_ref.at[0, low:high], sems.at[index])
        copy.start()
        for each in copies + [copy]:
            each.wait()


VMEM = pl.BlockSpec(memory_space=pltpu.VMEM)
HBM = pl.BlockSpec(memory_space=pltpu.HBM)


def kept(shape, dtype):
    return pltpu.VMEM(shape, dtype)


def held(array):
    return pltpu.with_memory_space_constraint(array, pltpu.VMEM)


def left(array):
    return pltpu.with_memory_space_constraint(array, pltpu.HBM)


def passed_along(array, by):
    length = lax.axis_size("section")
    return lax.ppermute(array, "section", [(i, (i + by) % length) for i in range(length)])


def body(micro, segment, gain, w_query, w_key, w_value, w_out):
    length, model = micro.shape[1], micro.shape[2]
    size = length // CHUNKS
    limits = pltpu.CompilerParams(vmem_limit_bytes=32 * 1024 * 1024)
    table = jnp.asarray(rope_table())
    rows = [size + EXTRA] + [size] * (CHUNKS - 1)
    key_values = [kept((size, KV_WIDTH), BF16)] * 2
    tables = [kept((length, PAIR), F32), kept((length, HD), F32)]
    mixing = pltpu.VMEM((size, Q_WIDTH), BF16)

    got = pl.pallas_call(
        functools.partial(opening_kernel, size),
        out_shape=(
            kept((rows[0], model), BF16),
            *key_values,
            *tables,
            kept((model, Q_WIDTH), BF16),
            kept((model, KV_WIDTH), BF16),
            kept((model, KV_WIDTH), BF16),
            kept((Q_WIDTH, model), BF16),
            kept((1, model), F32),
            kept(table.shape, BF16),
            *[kept((size, model), BF16)] * (CHUNKS - 1),
        ),
        in_specs=[HBM] * 8,
        out_specs=(VMEM,) * (10 + CHUNKS),
        scratch_shapes=[
            pltpu.VMEM((size, model), BF16),
            pltpu.VMEM(segment.shape, jnp.int32),
            pltpu.VMEM(gain.shape, BF16),
            pltpu.VMEM(table.shape, F32),
            mixing,
            pltpu.SemaphoreType.DMA((3 + CHUNKS,)),
            pltpu.SemaphoreType.DMA((24,)),
        ],
        compiler_params=limits,
        name="opening",
    )(*(left(array) for array in (micro, segment, gain, table, w_query, w_key, w_value, w_out)))
    out, k_rows, v_rows, cosines, bias = got[:5]
    weights = (got[9], *got[5:9])
    table = got[10]
    streams = [out, *got[11:]]

    for tick_index in range(TICKS):
        last = tick_index == TICKS - 1
        outs, keys, values = [], [], []
        for index in range(CHUNKS):
            if tick_index == 0 and index == 0:
                outs.append(passed_along(streams[0], 1))
                keys.append(k_rows)
                values.append(v_rows)
                continue
            args = [streams[index], *weights]
            shapes = [kept((rows[index], model), BF16), *key_values]
            scratch = [mixing]
            if index == 0:
                args.append(table)
                shapes += tables
            else:
                args += [cosines, bias, *keys, *values]
            specs = [VMEM] * len(shapes)
            ending = last and index == CHUNKS - 1
            if ending:
                args += outs
                shapes = [jax.ShapeDtypeStruct((1, length, model), BF16)]
                specs = [pl.BlockSpec(memory_space=pl.ANY)]
                scratch = [
                    pltpu.VMEM((size, model), BF16), *[pltpu.VMEM((size, KV_WIDTH), BF16)] * 2,
                    pltpu.SemaphoreType.DMA((CHUNKS,)), mixing,
                ]
            got = pl.pallas_call(
                functools.partial(chunk_kernel, index, last),
                out_shape=tuple(shapes), in_specs=[VMEM] * len(args), out_specs=tuple(specs),
                scratch_shapes=scratch, compiler_params=limits, name="chunk_%d_%d" % (tick_index, index),
            )(*map(held, args))
            if ending:
                return got[0]
            if index == 0:
                cosines, bias = got[3:]
            keys.append(got[1])
            values.append(got[2])
            outs.append(got[0] if last else passed_along(got[0], 1))
        streams = outs


def solution(mesh):
    in_specs = (
        P(("groups", "section"), None, None),
        P(("groups", "section"), None),
        P("section", None),
        P("section", None, None),
        P("section", None, None),
        P("section", None, None),
        P("section", None, None),
    )
    out_specs = P(("groups", "section"), None, None)
    return jax.shard_map(body, mesh=mesh, in_specs=in_specs, out_specs=out_specs, check_vma=False)
```

```python
import functools

import jax
import jax.numpy as jnp
import numpy as np
from jax import lax
from jax.experimental import pallas as pl
from jax.experimental.pallas import tpu as pltpu
from jax.sharding import PartitionSpec as P

HEADS = 16
KV_HEADS = 8
HD = 128
TICKS = 4
MAX_LEN = 96
CHUNKS = 2
EXTRA = 16
LIFT = 16.0
HIDDEN = -1e30
PAIR = 2 * HD
Q_WIDTH = HEADS * HD
KV_WIDTH = KV_HEADS * HD
BF16 = jnp.bfloat16
F32 = jnp.float32


def rope_table():
    middle = HD // 2
    spacing = 1000000.0 ** (-2.0 * np.arange(middle) / HD)
    angles = np.arange(MAX_LEN)[:, None] * spacing[None, :]
    cosine, sine = np.cos(angles), np.sin(angles)
    whole = np.concatenate([cosine, cosine, -sine, sine], axis=1).astype(np.float32)
    high = whole.astype(jnp.bfloat16).astype(np.float32)
    low = (whole - high).astype(jnp.bfloat16).astype(np.float32)
    return np.concatenate([high, low], axis=0)


def tables_of(ids_row, table):
    length = ids_row.shape[1]
    across = jnp.broadcast_to(ids_row, (length, length))
    down = across.T
    row_index = lax.broadcasted_iota(jnp.int32, (length, length), 0)
    column = lax.broadcasted_iota(jnp.int32, (length, length), 1)
    matched = across == down
    places = jnp.sum(jnp.where(matched & (column < row_index), 1.0, 0.0), axis=1, keepdims=True)
    bias = jnp.where(matched & (column <= row_index), 0.0, HIDDEN)
    slots = lax.broadcasted_iota(jnp.int32, (length, 2 * MAX_LEN), 1)
    slots = jnp.where(slots >= MAX_LEN, slots - MAX_LEN, slots).astype(F32)
    one_hot = jnp.where(slots == places, 1.0, 0.0).astype(BF16)
    factors = jnp.dot(one_hot, table, preferred_element_type=F32)
    return factors, bias


def rotated(values, cosine, sine):
    return values * cosine + pltpu.roll(values, HD // 2, 1) * sine


def layer(
    looped, x_ref, size, gain, weights, wait, cos_rows, bias_rows, kept_keys, kept_values,
    k_ref, v_ref, q_ref, mixed_ref, write,
):
    model = x_ref.shape[1]
    x = x_ref[:size, :].astype(F32)
    wq_ref, wk_ref, wv_ref, wo_ref = weights
    scale = lax.rsqrt(jnp.mean(x * x, axis=1, keepdims=True) + 1e-05) * (1.0 / LIFT)
    lifted = (x * gain).astype(BF16)
    cosine = cos_rows[:, :HD] * scale
    sine = cos_rows[:, HD:] * scale
    factor = HD ** (-0.5) * np.log2(np.e)
    cosine_q = cosine * factor
    sine_q = sine * factor

    count = bias_rows.shape[1]
    ones = jnp.ones((count, HD), BF16)

    def lanes_of(index, width):
        if isinstance(index, int):
            return slice(index * width, (index + 1) * width)
        return pl.ds(pl.multiple_of(index * width, width), width)

    def loop(steps, unroll, visit):
        if not looped:
            for index in range(steps):
                visit([index])
            return

        def step(turn, carry):
            visit([turn * unroll + offset for offset in range(unroll)])
            return carry

        lax.fori_loop(0, steps // unroll, step, 0)

    def keys_and_values(indices):
        for index in indices:
            lanes = lanes_of(index, PAIR)
            wait("k", index)
            got = jnp.dot(lifted, wk_ref[:, lanes], preferred_element_type=F32)
            turned = [rotated(got[:, half : half + HD], cosine, sine) for half in range(0, PAIR, HD)]
            k_ref[:, lanes] = jnp.concatenate(turned, axis=1).astype(BF16)
            wait("v", index)
            got = jnp.dot(lifted, wv_ref[:, lanes], preferred_element_type=F32)
            v_ref[:, lanes] = (got * scale).astype(BF16)

    def queries(indices):
        for index in indices:
            wait("q", index)
            got = jnp.dot(lifted, wq_ref[:, lanes_of(index, PAIR)], preferred_element_type=F32)
            q_ref[index, :size] = rotated(got[:, :HD], cosine_q, sine_q).astype(BF16)
            q_ref[index, size:] = rotated(got[:, HD:], cosine_q, sine_q).astype(BF16)

    def attend(groups):
        scores = []
        for group in groups:
            lanes = lanes_of(group, HD)
            key_rows = jnp.concatenate([rows[:, lanes] for rows in kept_keys] + [k_ref[:, lanes]], axis=0)
            got = lax.dot_general(q_ref[group], key_rows, (((1,), (1,)), ((), ())), preferred_element_type=F32)
            scores.append(got.reshape(2, size, count) + bias_rows[None])
        most = [jnp.max(part, axis=2, keepdims=True) for part in scores]
        expo = [jnp.exp2(part - peak).astype(BF16).reshape(2 * size, count) for part, peak in zip(scores, most)]
        got = []
        for group, part in zip(groups, expo):
            lanes = lanes_of(group, HD)
            value_rows = jnp.concatenate([rows[:, lanes] for rows in kept_values] + [v_ref[:, lanes]], axis=0)
            value_rows = jnp.concatenate([value_rows, ones], axis=1)
            got.append(jnp.dot(part, value_rows, preferred_element_type=F32))
        for group, part in zip(groups, got):
            total = part[:, HD:]
            inverse = pl.reciprocal(total, approx=True)
            inverse = inverse * (2.0 - total * inverse)
            mixed = (part[:, :HD] * inverse).astype(BF16)
            mixed_ref[:, lanes_of(group, PAIR)] = jnp.concatenate([mixed[:size], mixed[size:]], axis=1)

    def outputs(indices):
        for index in indices:
            wait("o", index)
            lanes = lanes_of(index, PAIR)
            update = jnp.dot(mixed_ref[...], wo_ref[:, lanes], preferred_element_type=F32)
            write(lanes, x_ref[:size, lanes].astype(F32) + update)

    loop(KV_WIDTH // PAIR, 1, keys_and_values)
    loop(Q_WIDTH // PAIR, 2, queries)
    if looped:
        loop(KV_HEADS, 4, attend)
    else:
        attend(range(KV_HEADS))
    loop(model // PAIR, 2, outputs)


def first_key(low):
    return max(0, low - MAX_LEN + 1) // 16 * 16


def kept_rows(index, size, refs):
    least = first_key(index * size)
    return [ref.at[max(0, least - place * size) :] for place, ref in enumerate(refs) if (place + 1) * size > least]


def write_ids(ids_row, out_ref, size):
    length = ids_row.shape[1]
    out_ref[size:, :] = jnp.zeros((EXTRA, out_ref.shape[1]), BF16)
    out_ref[size:, :length] = jnp.broadcast_to(ids_row, (EXTRA, length)).astype(BF16)


def opening_kernel(
    size, x_hbm, ids_hbm, gain_hbm, table_hbm, wq_hbm, wk_hbm, wv_hbm, wo_hbm,
    out_ref, k_ref, v_ref, cos_ref, bias_ref, wq_ref, wk_ref, wv_ref, wo_ref, gain_ref, table_ref, *refs,
):
    rest_refs, refs = refs[: CHUNKS - 1], refs[CHUNKS - 1 :]
    x_ref, ids_ref, raw_gain, raw_table, q_ref, mixed_ref, small_sems, sems = refs
    small = [
        pltpu.make_async_copy(ids_hbm, ids_ref, small_sems.at[0]),
        pltpu.make_async_copy(table_hbm, raw_table, small_sems.at[1]),
        pltpu.make_async_copy(gain_hbm, raw_gain, small_sems.at[2]),
        pltpu.make_async_copy(x_hbm.at[0, :size], x_ref, small_sems.at[3]),
    ]
    late = [
        pltpu.make_async_copy(x_hbm.at[0, (i + 1) * size : (i + 2) * size], rest_refs[i], small_sems.at[4 + i])
        for i in range(CHUNKS - 1)
    ]
    made = []

    def batch(source, target, rows, lanes):
        step = (rows.stop - rows.start) // 4
        copies = []
        for low in range(rows.start, rows.stop, step):
            part = (slice(low, low + step), lanes)
            copies.append(pltpu.make_async_copy(source.at[(0, *part)], target.at[part], sems.at[len(made)]))
            made.append(copies[-1])
        return copies

    model, half = wk_ref.shape[0], Q_WIDTH // 2
    narrow, wide = slice(0, KV_WIDTH), slice(0, Q_WIDTH)
    batches = [
        batch(wk_hbm, wk_ref, slice(0, model), narrow),
        batch(wv_hbm, wv_ref, slice(0, model), narrow),
        batch(wq_hbm, wq_ref, slice(0, model // 2), wide),
        batch(wq_hbm, wq_ref, slice(model // 2, model), wide),
        batch(wo_hbm, wo_ref, slice(0, half), slice(0, model)),
        batch(wo_hbm, wo_ref, slice(half, Q_WIDTH), slice(0, model)),
    ]
    arrivals = {("k", 0): (0,), ("v", 0): (1,), ("q", 0): (2, 3), ("o", 0): (4, 5)}

    def begin(index):
        if index < len(batches):
            for copy in batches[index]:
                copy.start()
        if index == len(batches):
            for copy in late:
                copy.start()

    def wait(name, tile):
        for index in arrivals.get((name, tile), ()):
            for copy in batches[index]:
                copy.wait()
            begin(index + 3)

    for copy in small:
        copy.start()
    for index in range(3):
        begin(index)
    for copy in small:
        copy.wait()
    gain_ref[...] = raw_gain[...].astype(F32) * LIFT
    table_ref[...] = raw_table[...].astype(BF16)
    ids_row = ids_ref[...].astype(F32)
    factors, bias = tables_of(ids_row, table_ref[...])
    cos_ref[...] = factors
    bias_ref[...] = bias
    write_ids(ids_row, out_ref, size)

    def write(lanes, values):
        out_ref[:size, lanes] = values.astype(BF16)

    layer(
        False, x_ref, size, gain_ref[...], (wq_ref, wk_ref, wv_ref, wo_ref), wait,
        cos_ref[:size, :], bias_ref[:size, :size], [], [], k_ref, v_ref, q_ref, mixed_ref, write,
    )
    for copy in late:
        copy.wait()


def chunk_kernel(index, last, x_ref, gain_ref, wq_ref, wk_ref, wv_ref, wo_ref, *refs):
    refs = list(refs)
    mixed_ref = refs.pop(-1)
    q_ref = refs.pop(-1)
    size = mixed_ref.shape[0]
    low, high = index * size, (index + 1) * size
    if index == 0:
        table_ref = refs.pop(0)
        out_ref, k_ref, v_ref, cos_ref, bias_ref = refs
        factors, bias = tables_of(x_ref[size:, : CHUNKS * size].astype(F32)[:1], table_ref[...])
        cos_ref[...] = factors
        bias_ref[...] = bias
        if not last:
            out_ref[size:, :] = x_ref[size:, :]
        keys, values = [], []
    else:
        cos_ref, bias_ref = refs[:2]
        keys, values, refs = refs[2 : 2 + index], refs[2 + index : 2 + 2 * index], refs[2 + 2 * index :]
        if last and index == CHUNKS - 1:
            done, (whole_ref, out_ref, k_ref, v_ref, sems) = refs[:index], refs[index:]
            copies = [
                pltpu.make_async_copy(done[i].at[:size], whole_ref.at[0, i * size : (i + 1) * size], sems.at[i])
                for i in range(index)
            ]
            for copy in copies:
                copy.start()
        else:
            out_ref, k_ref, v_ref = refs

    def write(lanes, result):
        out_ref[:size, lanes] = result.astype(BF16)

    layer(
        True, x_ref, size, gain_ref[...], (wq_ref, wk_ref, wv_ref, wo_ref), lambda name, index: None,
        cos_ref[low:high, :], bias_ref[low:high, first_key(low) : high],
        kept_rows(index, size, keys), kept_rows(index, size, values), k_ref, v_ref, q_ref, mixed_ref, write,
    )
    if last and index == CHUNKS - 1:
        copy = pltpu.make_async_copy(out_ref, whole_ref.at[0, low:high], sems.at[index])
        copy.start()
        for each in copies + [copy]:
            each.wait()


VMEM = pl.BlockSpec(memory_space=pltpu.VMEM)
HBM = pl.BlockSpec(memory_space=pltpu.HBM)


def kept(shape, dtype):
    return pltpu.VMEM(shape, dtype)


def held(array):
    return pltpu.with_memory_space_constraint(array, pltpu.VMEM)


def left(array):
    return pltpu.with_memory_space_constraint(array, pltpu.HBM)


def passed_along(array, by):
    length = lax.axis_size("section")
    return lax.ppermute(array, "section", [(i, (i + by) % length) for i in range(length)])


def body(micro, segment, gain, w_query, w_key, w_value, w_out):
    length, model = micro.shape[1], micro.shape[2]
    size = length // CHUNKS
    limits = pltpu.CompilerParams(vmem_limit_bytes=32 * 1024 * 1024)
    table = jnp.asarray(rope_table())
    rows = [size + EXTRA] + [size] * (CHUNKS - 1)
    key_values = [kept((size, KV_WIDTH), BF16)] * 2
    tables = [kept((length, PAIR), F32), kept((length, length), F32)]
    mixing = [pltpu.VMEM((KV_HEADS, 2 * size, HD), BF16), pltpu.VMEM((size, Q_WIDTH), BF16)]

    got = pl.pallas_call(
        functools.partial(opening_kernel, size),
        out_shape=(
            kept((rows[0], model), BF16),
            *key_values,
            *tables,
            kept((model, Q_WIDTH), BF16),
            kept((model, KV_WIDTH), BF16),
            kept((model, KV_WIDTH), BF16),
            kept((Q_WIDTH, model), BF16),
            kept((1, model), F32),
            kept(table.shape, BF16),
            *[kept((size, model), BF16)] * (CHUNKS - 1),
        ),
        in_specs=[HBM] * 8,
        out_specs=(VMEM,) * (10 + CHUNKS),
        scratch_shapes=[
            pltpu.VMEM((size, model), BF16),
            pltpu.VMEM(segment.shape, jnp.int32),
            pltpu.VMEM(gain.shape, BF16),
            pltpu.VMEM(table.shape, F32),
            *mixing,
            pltpu.SemaphoreType.DMA((3 + CHUNKS,)),
            pltpu.SemaphoreType.DMA((24,)),
        ],
        compiler_params=limits,
        name="opening",
    )(*(left(array) for array in (micro, segment, gain, table, w_query, w_key, w_value, w_out)))
    out, k_rows, v_rows, cosines, bias = got[:5]
    weights = (got[9], *got[5:9])
    table = got[10]
    streams = [out, *got[11:]]

    for tick_index in range(TICKS):
        last = tick_index == TICKS - 1
        outs, keys, values = [], [], []
        for index in range(CHUNKS):
            if tick_index == 0 and index == 0:
                outs.append(passed_along(streams[0], 1))
                keys.append(k_rows)
                values.append(v_rows)
                continue
            args = [streams[index], *weights]
            shapes = [kept((rows[index], model), BF16), *key_values]
            scratch = mixing
            if index == 0:
                args.append(table)
                shapes += tables
            else:
                args += [cosines, bias, *keys, *values]
            specs = [VMEM] * len(shapes)
            ending = last and index == CHUNKS - 1
            if ending:
                args += outs
                shapes = [jax.ShapeDtypeStruct((1, length, model), BF16)]
                specs = [pl.BlockSpec(memory_space=pl.ANY)]
                scratch = [
                    pltpu.VMEM((size, model), BF16), *[pltpu.VMEM((size, KV_WIDTH), BF16)] * 2,
                    pltpu.SemaphoreType.DMA((CHUNKS,)), *mixing,
                ]
            got = pl.pallas_call(
                functools.partial(chunk_kernel, index, last),
                out_shape=tuple(shapes), in_specs=[VMEM] * len(args), out_specs=tuple(specs),
                scratch_shapes=scratch, compiler_params=limits, name="chunk_%d_%d" % (tick_index, index),
            )(*map(held, args))
            if ending:
                return got[0]
            if index == 0:
                cosines, bias = got[3:]
            keys.append(got[1])
            values.append(got[2])
            outs.append(got[0] if last else passed_along(got[0], 1))
        streams = outs


def solution(mesh):
    in_specs = (
        P(("groups", "section"), None, None),
        P(("groups", "section"), None),
        P("section", None),
        P("section", None, None),
        P("section", None, None),
        P("section", None, None),
        P("section", None, None),
    )
    out_specs = P(("groups", "section"), None, None)
    return jax.shard_map(body, mesh=mesh, in_specs=in_specs, out_specs=out_specs, check_vma=False)
```

```python
import functools

import jax
import jax.numpy as jnp
import numpy as np
from jax import lax
from jax.experimental import pallas as pl
from jax.experimental.pallas import tpu as pltpu
from jax.sharding import PartitionSpec as P

HEADS = 16
KV_HEADS = 8
HD = 128
TICKS = 4
MAX_LEN = 96
CHUNKS = 2
EXTRA = 16
LIFT = 16.0
HIDDEN = -1e30
PAIR = 2 * HD
Q_WIDTH = HEADS * HD
KV_WIDTH = KV_HEADS * HD
BF16 = jnp.bfloat16
F32 = jnp.float32


def rope_table():
    middle = HD // 2
    spacing = 1000000.0 ** (-2.0 * np.arange(middle) / HD)
    angles = np.arange(MAX_LEN)[:, None] * spacing[None, :]
    cosine, sine = np.cos(angles), np.sin(angles)
    whole = np.concatenate([cosine, cosine, -sine, sine], axis=1).astype(np.float32)
    high = whole.astype(jnp.bfloat16).astype(np.float32)
    low = (whole - high).astype(jnp.bfloat16).astype(np.float32)
    return np.concatenate([high, low], axis=0)


def tables_of(ids_row, table):
    length = ids_row.shape[1]
    across = jnp.broadcast_to(ids_row, (length, length))
    down = across.T
    row_index = lax.broadcasted_iota(jnp.int32, (length, length), 0)
    column = lax.broadcasted_iota(jnp.int32, (length, length), 1)
    matched = across == down
    places = jnp.sum(jnp.where(matched & (column < row_index), 1.0, 0.0), axis=1, keepdims=True)
    bias = jnp.where(matched & (column <= row_index), 0.0, HIDDEN)
    slots = lax.broadcasted_iota(jnp.int32, (length, 2 * MAX_LEN), 1)
    slots = jnp.where(slots >= MAX_LEN, slots - MAX_LEN, slots).astype(F32)
    one_hot = jnp.where(slots == places, 1.0, 0.0).astype(BF16)
    factors = jnp.dot(one_hot, table, preferred_element_type=F32)
    return factors, bias


def rotated(values, cosine, sine):
    return values * cosine + pltpu.roll(values, HD // 2, 1) * sine


def layer(x, gain, weights, wait, cos_rows, bias_rows, kept_keys, kept_values, k_ref, v_ref, mixed_ref, write):
    size, model = x.shape
    wq_ref, wk_ref, wv_ref, wo_ref = weights
    scale = lax.rsqrt(jnp.mean(x * x, axis=1, keepdims=True) + 1e-05) * (1.0 / LIFT)
    lifted = (x * gain).astype(BF16)
    cosine = cos_rows[:, :HD] * scale
    sine = cos_rows[:, HD:] * scale
    factor = HD ** (-0.5) * np.log2(np.e)
    cosine_q = cosine * factor
    sine_q = sine * factor

    for start in range(0, KV_WIDTH, PAIR):
        wait("k", start)
        got = jnp.dot(lifted, wk_ref[:, start : start + PAIR], preferred_element_type=F32)
        for half in range(0, PAIR, HD):
            turned = rotated(got[:, half : half + HD], cosine, sine)
            k_ref[:, start + half : start + half + HD] = turned.astype(BF16)
    for start in range(0, KV_WIDTH, PAIR):
        wait("v", start)
        got = jnp.dot(lifted, wv_ref[:, start : start + PAIR], preferred_element_type=F32)
        v_ref[:, start : start + PAIR] = (got * scale).astype(BF16)
    queries = []
    for start in range(0, Q_WIDTH, PAIR):
        wait("q", start)
        got = jnp.dot(lifted, wq_ref[:, start : start + PAIR], preferred_element_type=F32)
        upper = rotated(got[:, :HD], cosine_q, sine_q)
        lower = rotated(got[:, HD:], cosine_q, sine_q)
        queries.append(jnp.concatenate([upper, lower], axis=0).astype(BF16))

    count = bias_rows.shape[1]
    ones = jnp.ones((count, HD), BF16)
    groups = range(KV_HEADS)
    scores = []
    for group in groups:
        lanes = slice(group * HD, (group + 1) * HD)
        key_rows = jnp.concatenate([rows[:, lanes] for rows in kept_keys] + [k_ref[:, lanes]], axis=0)
        got = lax.dot_general(queries[group], key_rows, (((1,), (1,)), ((), ())), preferred_element_type=F32)
        scores.append(got.reshape(2, size, count) + bias_rows[None])
    most = [jnp.max(part, axis=2, keepdims=True) for part in scores]
    expo = [jnp.exp2(scores[g] - most[g]).astype(BF16).reshape(2 * size, count) for g in groups]
    got = []
    for group in groups:
        lanes = slice(group * HD, (group + 1) * HD)
        value_rows = jnp.concatenate([rows[:, lanes] for rows in kept_values] + [v_ref[:, lanes]], axis=0)
        value_rows = jnp.concatenate([value_rows, ones], axis=1)
        got.append(jnp.dot(expo[group], value_rows, preferred_element_type=F32))
    for group in groups:
        total = got[group][:, HD:]
        inverse = pl.reciprocal(total, approx=True)
        inverse = inverse * (2.0 - total * inverse)
        mixed = (got[group][:, :HD] * inverse).astype(BF16)
        mixed_ref[:, group * PAIR : group * PAIR + HD] = mixed[:size]
        mixed_ref[:, group * PAIR + HD : (group + 1) * PAIR] = mixed[size:]
    for start in range(0, model, PAIR):
        wait("o", start)
        update = jnp.dot(mixed_ref[...], wo_ref[:, start : start + PAIR], preferred_element_type=F32)
        write(start, x[:, start : start + PAIR] + update)


def first_key(low):
    return max(0, low - MAX_LEN + 1) // 16 * 16


def kept_rows(index, size, refs):
    least = first_key(index * size)
    return [ref[max(0, least - place * size) :] for place, ref in enumerate(refs) if (place + 1) * size > least]


def write_ids(ids_row, out_ref, size):
    length = ids_row.shape[1]
    out_ref[size:, :] = jnp.zeros((EXTRA, out_ref.shape[1]), BF16)
    out_ref[size:, :length] = jnp.broadcast_to(ids_row, (EXTRA, length)).astype(BF16)


def opening_kernel(
    size, x_hbm, ids_hbm, gain_hbm, table_hbm, wq_hbm, wk_hbm, wv_hbm, wo_hbm,
    out_ref, k_ref, v_ref, cos_ref, bias_ref, wq_ref, wk_ref, wv_ref, wo_ref, gain_ref, table_ref, *refs,
):
    rest_refs, refs = refs[: CHUNKS - 1], refs[CHUNKS - 1 :]
    x_ref, ids_ref, raw_gain, raw_table, mixed_ref, small_sems, sems = refs
    small = [
        pltpu.make_async_copy(ids_hbm, ids_ref, small_sems.at[0]),
        pltpu.make_async_copy(table_hbm, raw_table, small_sems.at[1]),
        pltpu.make_async_copy(gain_hbm, raw_gain, small_sems.at[2]),
        pltpu.make_async_copy(x_hbm.at[0, :size], x_ref, small_sems.at[3]),
    ]
    late = [
        pltpu.make_async_copy(x_hbm.at[0, (i + 1) * size : (i + 2) * size], rest_refs[i], small_sems.at[4 + i])
        for i in range(CHUNKS - 1)
    ]
    made = []

    def batch(source, target, rows, lanes):
        step = (rows.stop - rows.start) // 4
        copies = []
        for low in range(rows.start, rows.stop, step):
            part = (slice(low, low + step), lanes)
            copies.append(pltpu.make_async_copy(source.at[(0, *part)], target.at[part], sems.at[len(made)]))
            made.append(copies[-1])
        return copies

    model, half = wk_ref.shape[0], Q_WIDTH // 2
    narrow, wide = slice(0, KV_WIDTH), slice(0, Q_WIDTH)
    batches = [
        batch(wk_hbm, wk_ref, slice(0, model), narrow),
        batch(wv_hbm, wv_ref, slice(0, model), narrow),
        batch(wq_hbm, wq_ref, slice(0, model // 2), wide),
        batch(wq_hbm, wq_ref, slice(model // 2, model), wide),
        batch(wo_hbm, wo_ref, slice(0, half), slice(0, model)),
        batch(wo_hbm, wo_ref, slice(half, Q_WIDTH), slice(0, model)),
    ]
    arrivals = {("k", 0): (0,), ("v", 0): (1,), ("q", 0): (2, 3), ("o", 0): (4, 5)}

    def begin(index):
        if index < len(batches):
            for copy in batches[index]:
                copy.start()
        if index == len(batches):
            for copy in late:
                copy.start()

    def wait(name, start):
        for index in arrivals.get((name, start), ()):
            for copy in batches[index]:
                copy.wait()
            begin(index + 3)

    for copy in small:
        copy.start()
    for index in range(3):
        begin(index)
    for copy in small:
        copy.wait()
    gain_ref[...] = raw_gain[...].astype(F32) * LIFT
    table_ref[...] = raw_table[...].astype(BF16)
    ids_row = ids_ref[...].astype(F32)
    factors, bias = tables_of(ids_row, table_ref[...])
    cos_ref[...] = factors
    bias_ref[...] = bias
    write_ids(ids_row, out_ref, size)

    def write(start, values):
        out_ref[:size, start : start + PAIR] = values.astype(BF16)

    layer(
        x_ref[...].astype(F32), gain_ref[...], (wq_ref, wk_ref, wv_ref, wo_ref), wait,
        cos_ref[:size, :], bias_ref[:size, :size], [], [], k_ref, v_ref, mixed_ref, write,
    )
    for copy in late:
        copy.wait()


def chunk_kernel(parity, index, last, x_ref, gain_ref, wq_ref, wk_ref, wv_ref, wo_ref, before_ref, *refs):
    section = lax.axis_index("section")
    refs = list(refs)
    mixed_ref = refs.pop(-1)
    size = mixed_ref.shape[0]
    low, high = index * size, (index + 1) * size
    ending = last and index == CHUNKS - 1 and parity == 0
    done, others = [], []
    if index == 0:
        table_ref = refs.pop(0)
        out_ref, k_ref, v_ref, cos_ref, bias_ref = refs
        keys, values = [], []
    else:
        cos_ref, bias_ref = refs[:2]
        keys, values, refs = refs[2 : 2 + index], refs[2 + index : 2 + 2 * index], refs[2 + 2 * index :]
        if ending:
            done, others, refs = refs[:index], refs[index : 2 * index + 1], refs[2 * index + 1 :]
            whole_ref, out_ref, k_ref, v_ref, sems = refs
        else:
            out_ref, k_ref, v_ref = refs

    def to_whole(ref, place):
        return pltpu.make_async_copy(
            ref.at[:size], whole_ref.at[0, place * size : (place + 1) * size], sems.at[place]
        )

    def write(start, result):
        out_ref[:size, start : start + PAIR] = result.astype(BF16)

    @pl.when(lax.rem(section, 2) == parity)
    def _():
        copies = [to_whole(ref, place) for place, ref in enumerate(done)]
        for copy in copies:
            copy.start()
        if index == 0:
            factors, bias = tables_of(x_ref[size : size + EXTRA, : CHUNKS * size].astype(F32)[:1], table_ref[...])
            cos_ref[...] = factors
            bias_ref[...] = bias
            if not last:
                out_ref[size : size + EXTRA, :] = x_ref[size : size + EXTRA, :]
        layer(
            x_ref[:size, :].astype(F32), gain_ref[...], (wq_ref, wk_ref, wv_ref, wo_ref), lambda name, start: None,
            cos_ref[low:high, :], bias_ref[low:high, first_key(low) : high],
            kept_rows(index, size, keys), kept_rows(index, size, values), k_ref, v_ref, mixed_ref, write,
        )
        if ending:
            copies.append(to_whole(out_ref, index))
            copies[-1].start()
        for copy in copies:
            copy.wait()

    if ending:

        @pl.when(lax.rem(section, 2) != parity)
        def _():
            copies = [to_whole(ref, place) for place, ref in enumerate(others)]
            for copy in copies:
                copy.start()
            for copy in copies:
                copy.wait()


VMEM = pl.BlockSpec(memory_space=pltpu.VMEM)
HBM = pl.BlockSpec(memory_space=pltpu.HBM)


def kept(shape, dtype):
    return pltpu.VMEM(shape, dtype)


def held(array):
    return pltpu.with_memory_space_constraint(array, pltpu.VMEM)


def left(array):
    return pltpu.with_memory_space_constraint(array, pltpu.HBM)


def passed_along(array, parity):
    length = lax.axis_size("section")
    return lax.ppermute(array, "section", [(i, (i + 1) % length) for i in range(parity, length, 2)])


def body(micro, segment, gain, w_query, w_key, w_value, w_out):
    length, model = micro.shape[1], micro.shape[2]
    size = length // CHUNKS
    limits = pltpu.CompilerParams(vmem_limit_bytes=32 * 1024 * 1024)
    brief = pl.CostEstimate(flops=1024, bytes_accessed=1024, transcendentals=0)
    table = jnp.asarray(rope_table())
    rows = [size + EXTRA] + [size] * (CHUNKS - 1)
    key_values = [kept((size, KV_WIDTH), BF16)] * 2
    tables = [kept((length, PAIR), F32), kept((length, length), F32)]
    mixing = pltpu.VMEM((size, Q_WIDTH), BF16)

    got = pl.pallas_call(
        functools.partial(opening_kernel, size),
        out_shape=(
            kept((rows[0], model), BF16),
            *key_values,
            *tables,
            kept((model, Q_WIDTH), BF16),
            kept((model, KV_WIDTH), BF16),
            kept((model, KV_WIDTH), BF16),
            kept((Q_WIDTH, model), BF16),
            kept((1, model), F32),
            kept(table.shape, BF16),
            *[kept((size, model), BF16)] * (CHUNKS - 1),
        ),
        in_specs=[HBM] * 8,
        out_specs=(VMEM,) * (10 + CHUNKS),
        scratch_shapes=[
            pltpu.VMEM((size, model), BF16),
            pltpu.VMEM(segment.shape, jnp.int32),
            pltpu.VMEM(gain.shape, BF16),
            pltpu.VMEM(table.shape, F32),
            mixing,
            pltpu.SemaphoreType.DMA((3 + CHUNKS,)),
            pltpu.SemaphoreType.DMA((24,)),
        ],
        compiler_params=limits,
        name="opening",
    )(*(left(array) for array in (micro, segment, gain, table, w_query, w_key, w_value, w_out)))
    out, k_rows, v_rows, cosines, bias = got[:5]
    weights = (got[9], *got[5:9])
    table = got[10]
    before = out
    state = {
        parity: {"tables": (cosines, bias), "keys": [k_rows], "values": [v_rows], "outs": [], "coming": [got[11]]}
        for parity in (0, 1)
    }
    for parity in (1, 0):
        state[1 - parity]["coming"].append(passed_along(out, parity))

    for step in range(1, TICKS * CHUNKS):
        tick_index, index = divmod(step, CHUNKS)
        last = tick_index == TICKS - 1
        for parity in (1, 0):
            mine = state[parity]
            ending = last and index == CHUNKS - 1 and parity == 0
            args = [mine["coming"].pop(0), *weights, before]
            shapes = [kept((rows[index] + EXTRA * parity, model), BF16), *key_values]
            scratch = [mixing]
            if index == 0:
                mine.update(keys=[], values=[], outs=[])
                args.append(table)
                shapes += tables
            else:
                args += [*mine["tables"], *mine["keys"], *mine["values"]]
            specs = [VMEM] * len(shapes)
            if ending:
                args += mine["outs"] + state[1]["outs"]
                shapes = [jax.ShapeDtypeStruct((1, length, model), BF16)]
                specs = [pl.BlockSpec(memory_space=pl.ANY)]
                scratch = [
                    pltpu.VMEM((size, model), BF16), *[pltpu.VMEM((size, KV_WIDTH), BF16)] * 2,
                    pltpu.SemaphoreType.DMA((CHUNKS,)), mixing,
                ]
            got = pl.pallas_call(
                functools.partial(chunk_kernel, parity, index, last),
                out_shape=tuple(shapes), in_specs=[VMEM] * len(args), out_specs=tuple(specs),
                scratch_shapes=scratch, compiler_params=limits, cost_estimate=brief, name="chunk_%d_%d_%d" % (tick_index, index, parity),
            )(*map(held, args))
            if ending:
                return got[0]
            if index == 0:
                mine["tables"] = got[3:]
            before = got[0]
            mine["keys"].append(got[1])
            mine["values"].append(got[2])
            mine["outs"].append(got[0])
            if not last:
                state[1 - parity]["coming"].append(passed_along(got[0], parity))


def solution(mesh):
    in_specs = (
        P(("groups", "section"), None, None),
        P(("groups", "section"), None),
        P("section", None),
        P("section", None, None),
        P("section", None, None),
        P("section", None, None),
        P("section", None, None),
    )
    out_specs = P(("groups", "section"), None, None)
    return jax.shard_map(body, mesh=mesh, in_specs=in_specs, out_specs=out_specs, check_vma=False)
```

```python
import functools

import jax
import jax.numpy as jnp
import numpy as np
from jax import lax
from jax.experimental import pallas as pl
from jax.experimental.pallas import tpu as pltpu
from jax.sharding import PartitionSpec as P

HEADS = 16
KV_HEADS = 8
HD = 128
TICKS = 4
MAX_LEN = 96
CHUNKS = 2
EXTRA = 16
LIFT = 16.0
HIDDEN = -1e30
PAIR = 2 * HD
Q_WIDTH = HEADS * HD
KV_WIDTH = KV_HEADS * HD
BF16 = jnp.bfloat16
F32 = jnp.float32


def rope_table():
    middle = HD // 2
    spacing = 1000000.0 ** (-2.0 * np.arange(middle) / HD)
    angles = np.arange(MAX_LEN)[:, None] * spacing[None, :]
    cosine, sine = np.cos(angles), np.sin(angles)
    whole = np.concatenate([cosine, cosine, -sine, sine], axis=1).astype(np.float32)
    high = whole.astype(jnp.bfloat16).astype(np.float32)
    low = (whole - high).astype(jnp.bfloat16).astype(np.float32)
    return np.concatenate([high, low], axis=0)


def tables_of(ids_row, table):
    length = ids_row.shape[1]
    across = jnp.broadcast_to(ids_row, (length, length))
    down = across.T
    row_index = lax.broadcasted_iota(jnp.int32, (length, length), 0)
    column = lax.broadcasted_iota(jnp.int32, (length, length), 1)
    matched = across == down
    places = jnp.sum(jnp.where(matched & (column < row_index), 1.0, 0.0), axis=1, keepdims=True)
    bias = jnp.where(matched & (column <= row_index), 0.0, HIDDEN)
    slots = lax.broadcasted_iota(jnp.int32, (length, 2 * MAX_LEN), 1)
    slots = jnp.where(slots >= MAX_LEN, slots - MAX_LEN, slots).astype(F32)
    one_hot = jnp.where(slots == places, 1.0, 0.0).astype(BF16)
    factors = jnp.dot(one_hot, table, preferred_element_type=F32)
    return factors, bias


def rotated(values, cosine, sine):
    return values * cosine + pltpu.roll(values, HD // 2, 1) * sine


def layer(x, gain, weights, wait, cos_rows, bias_rows, kept_keys, kept_values, k_ref, v_ref, mixed_ref, write):
    size, model = x.shape
    wq_ref, wk_ref, wv_ref, wo_ref = weights
    scale = lax.rsqrt(jnp.mean(x * x, axis=1, keepdims=True) + 1e-05) * (1.0 / LIFT)
    lifted = (x * gain).astype(BF16)
    cosine = cos_rows[:, :HD] * scale
    sine = cos_rows[:, HD:] * scale
    factor = HD ** (-0.5) * np.log2(np.e)
    cosine_q = cosine * factor
    sine_q = sine * factor

    for start in range(0, KV_WIDTH, PAIR):
        wait("k", start)
        got = jnp.dot(lifted, wk_ref[:, start : start + PAIR], preferred_element_type=F32)
        for half in range(0, PAIR, HD):
            turned = rotated(got[:, half : half + HD], cosine, sine)
            k_ref[:, start + half : start + half + HD] = turned.astype(BF16)
    for start in range(0, KV_WIDTH, PAIR):
        wait("v", start)
        got = jnp.dot(lifted, wv_ref[:, start : start + PAIR], preferred_element_type=F32)
        v_ref[:, start : start + PAIR] = (got * scale).astype(BF16)
    queries = []
    for start in range(0, Q_WIDTH, PAIR):
        wait("q", start)
        got = jnp.dot(lifted, wq_ref[:, start : start + PAIR], preferred_element_type=F32)
        upper = rotated(got[:, :HD], cosine_q, sine_q)
        lower = rotated(got[:, HD:], cosine_q, sine_q)
        queries.append(jnp.concatenate([upper, lower], axis=0).astype(BF16))

    count = bias_rows.shape[1]
    ones = jnp.ones((count, HD), BF16)
    groups = range(KV_HEADS)
    scores = []
    for group in groups:
        lanes = slice(group * HD, (group + 1) * HD)
        key_rows = jnp.concatenate([rows[:, lanes] for rows in kept_keys] + [k_ref[:, lanes]], axis=0)
        got = lax.dot_general(queries[group], key_rows, (((1,), (1,)), ((), ())), preferred_element_type=F32)
        scores.append(got.reshape(2, size, count) + bias_rows[None])
    most = [jnp.max(part, axis=2, keepdims=True) for part in scores]
    expo = [jnp.exp2(scores[g] - most[g]).astype(BF16).reshape(2 * size, count) for g in groups]
    got = []
    for group in groups:
        lanes = slice(group * HD, (group + 1) * HD)
        value_rows = jnp.concatenate([rows[:, lanes] for rows in kept_values] + [v_ref[:, lanes]], axis=0)
        value_rows = jnp.concatenate([value_rows, ones], axis=1)
        got.append(jnp.dot(expo[group], value_rows, preferred_element_type=F32))
    for group in groups:
        total = got[group][:, HD:]
        inverse = pl.reciprocal(total, approx=True)
        inverse = inverse * (2.0 - total * inverse)
        mixed = (got[group][:, :HD] * inverse).astype(BF16)
        mixed_ref[:, group * PAIR : group * PAIR + HD] = mixed[:size]
        mixed_ref[:, group * PAIR + HD : (group + 1) * PAIR] = mixed[size:]
    for start in range(0, model, PAIR):
        wait("o", start)
        update = jnp.dot(mixed_ref[...], wo_ref[:, start : start + PAIR], preferred_element_type=F32)
        write(start, x[:, start : start + PAIR] + update)


def first_key(low):
    return max(0, low - MAX_LEN + 1) // 16 * 16


def kept_rows(index, size, refs):
    least = first_key(index * size)
    return [ref[max(0, least - place * size) :] for place, ref in enumerate(refs) if (place + 1) * size > least]


def write_ids(ids_row, out_ref, size):
    length = ids_row.shape[1]
    out_ref[size:, :] = jnp.zeros((EXTRA, out_ref.shape[1]), BF16)
    out_ref[size:, :length] = jnp.broadcast_to(ids_row, (EXTRA, length)).astype(BF16)


def opening_kernel(
    size, x_hbm, ids_hbm, gain_hbm, table_hbm, wq_hbm, wk_hbm, wv_hbm, wo_hbm,
    out_ref, k_ref, v_ref, cos_ref, bias_ref, wq_ref, wk_ref, wv_ref, wo_ref, gain_ref, table_ref, *refs,
):
    rest_refs, refs = refs[: CHUNKS - 1], refs[CHUNKS - 1 :]
    x_ref, ids_ref, raw_gain, raw_table, mixed_ref, small_sems, sems = refs
    small = [
        pltpu.make_async_copy(ids_hbm, ids_ref, small_sems.at[0]),
        pltpu.make_async_copy(table_hbm, raw_table, small_sems.at[1]),
        pltpu.make_async_copy(gain_hbm, raw_gain, small_sems.at[2]),
        pltpu.make_async_copy(x_hbm.at[0, :size], x_ref, small_sems.at[3]),
    ]
    late = [
        pltpu.make_async_copy(x_hbm.at[0, (i + 1) * size : (i + 2) * size], rest_refs[i], small_sems.at[4 + i])
        for i in range(CHUNKS - 1)
    ]
    made = []

    def batch(source, target, rows, lanes):
        step = (rows.stop - rows.start) // 4
        copies = []
        for low in range(rows.start, rows.stop, step):
            part = (slice(low, low + step), lanes)
            copies.append(pltpu.make_async_copy(source.at[(0, *part)], target.at[part], sems.at[len(made)]))
            made.append(copies[-1])
        return copies

    model, half = wk_ref.shape[0], Q_WIDTH // 2
    narrow, wide = slice(0, KV_WIDTH), slice(0, Q_WIDTH)
    batches = [
        batch(wk_hbm, wk_ref, slice(0, model), narrow),
        batch(wv_hbm, wv_ref, slice(0, model), narrow),
        batch(wq_hbm, wq_ref, slice(0, model // 2), wide),
        batch(wq_hbm, wq_ref, slice(model // 2, model), wide),
        batch(wo_hbm, wo_ref, slice(0, half), slice(0, model)),
        batch(wo_hbm, wo_ref, slice(half, Q_WIDTH), slice(0, model)),
    ]
    arrivals = {("k", 0): (0,), ("v", 0): (1,), ("q", 0): (2, 3), ("o", 0): (4, 5)}

    def begin(index):
        if index < len(batches):
            for copy in batches[index]:
                copy.start()
        if index == len(batches):
            for copy in late:
                copy.start()

    def wait(name, start):
        for index in arrivals.get((name, start), ()):
            for copy in batches[index]:
                copy.wait()
            begin(index + 3)

    for copy in small:
        copy.start()
    for index in range(3):
        begin(index)
    for copy in small:
        copy.wait()
    gain_ref[...] = raw_gain[...].astype(F32) * LIFT
    table_ref[...] = raw_table[...].astype(BF16)
    ids_row = ids_ref[...].astype(F32)
    factors, bias = tables_of(ids_row, table_ref[...])
    cos_ref[...] = factors
    bias_ref[...] = bias
    write_ids(ids_row, out_ref, size)

    def write(start, values):
        out_ref[:size, start : start + PAIR] = values.astype(BF16)

    layer(
        x_ref[...].astype(F32), gain_ref[...], (wq_ref, wk_ref, wv_ref, wo_ref), wait,
        cos_ref[:size, :], bias_ref[:size, :size], [], [], k_ref, v_ref, mixed_ref, write,
    )
    for copy in late:
        copy.wait()


def chunk_kernel(index, last, paired, *refs):
    refs = list(refs)
    if paired:
        outer, inner, sem, x_ref = refs.pop(0), refs.pop(0), refs.pop(-1), refs.pop(-1)
        odd = lax.rem(lax.axis_index("section"), 2)

        @pl.when(odd == 0)
        def _():
            copy = pltpu.make_async_copy(outer.at[0], x_ref, sem)
            copy.start()
            copy.wait()

        @pl.when(odd == 1)
        def _():
            copy = pltpu.make_async_copy(inner.at[0], x_ref, sem)
            copy.start()
            copy.wait()

    else:
        x_ref = refs.pop(0)
    chunk_rows(index, last, x_ref, *refs)


def chunk_rows(index, last, x_ref, gain_ref, wq_ref, wk_ref, wv_ref, wo_ref, *refs):
    refs = list(refs)
    mixed_ref = refs.pop(-1)
    size = mixed_ref.shape[0]
    low, high = index * size, (index + 1) * size
    if index == 0:
        table_ref = refs.pop(0)
        out_ref, k_ref, v_ref, cos_ref, bias_ref = refs
        factors, bias = tables_of(x_ref[size:, : CHUNKS * size].astype(F32)[:1], table_ref[...])
        cos_ref[...] = factors
        bias_ref[...] = bias
        if not last:
            out_ref[size:, :] = x_ref[size:, :]
        keys, values = [], []
    else:
        cos_ref, bias_ref = refs[:2]
        keys, values, refs = refs[2 : 2 + index], refs[2 + index : 2 + 2 * index], refs[2 + 2 * index :]
        if last and index == CHUNKS - 1:
            done, (whole_ref, out_ref, k_ref, v_ref, sems) = refs[:index], refs[index:]
            copies = [
                pltpu.make_async_copy(done[i].at[:size], whole_ref.at[0, i * size : (i + 1) * size], sems.at[i])
                for i in range(index)
            ]
            for copy in copies:
                copy.start()
        else:
            out_ref, k_ref, v_ref = refs

    def write(start, result):
        out_ref[:size, start : start + PAIR] = result.astype(BF16)

    layer(
        x_ref[:size, :].astype(F32), gain_ref[...], (wq_ref, wk_ref, wv_ref, wo_ref), lambda name, start: None,
        cos_ref[low:high, :], bias_ref[low:high, first_key(low) : high],
        kept_rows(index, size, keys), kept_rows(index, size, values), k_ref, v_ref, mixed_ref, write,
    )
    if last and index == CHUNKS - 1:
        copy = pltpu.make_async_copy(out_ref, whole_ref.at[0, low:high], sems.at[index])
        copy.start()
        for each in copies + [copy]:
            each.wait()


VMEM = pl.BlockSpec(memory_space=pltpu.VMEM)
HBM = pl.BlockSpec(memory_space=pltpu.HBM)


def kept(shape, dtype):
    return pltpu.VMEM(shape, dtype)


def held(array):
    return pltpu.with_memory_space_constraint(array, pltpu.VMEM)


def left(array):
    return pltpu.with_memory_space_constraint(array, pltpu.HBM)


def passed_along(array):
    length = lax.axis_size("section")
    inner = [[i, i + 1] for i in range(0, length, 2)]
    outer = [[i, (i + 1) % length] for i in range(1, length, 2)]
    return tuple(lax.all_gather(array, "section", axis_index_groups=groups) for groups in (outer, inner))


def body(micro, segment, gain, w_query, w_key, w_value, w_out):
    length, model = micro.shape[1], micro.shape[2]
    size = length // CHUNKS
    limits = pltpu.CompilerParams(vmem_limit_bytes=32 * 1024 * 1024)
    table = jnp.asarray(rope_table())
    rows = [size + EXTRA] + [size] * (CHUNKS - 1)
    key_values = [kept((size, KV_WIDTH), BF16)] * 2
    tables = [kept((length, PAIR), F32), kept((length, length), F32)]
    mixing = pltpu.VMEM((size, Q_WIDTH), BF16)

    got = pl.pallas_call(
        functools.partial(opening_kernel, size),
        out_shape=(
            kept((rows[0], model), BF16),
            *key_values,
            *tables,
            kept((model, Q_WIDTH), BF16),
            kept((model, KV_WIDTH), BF16),
            kept((model, KV_WIDTH), BF16),
            kept((Q_WIDTH, model), BF16),
            kept((1, model), F32),
            kept(table.shape, BF16),
            *[kept((size, model), BF16)] * (CHUNKS - 1),
        ),
        in_specs=[HBM] * 8,
        out_specs=(VMEM,) * (10 + CHUNKS),
        scratch_shapes=[
            pltpu.VMEM((size, model), BF16),
            pltpu.VMEM(segment.shape, jnp.int32),
            pltpu.VMEM(gain.shape, BF16),
            pltpu.VMEM(table.shape, F32),
            mixing,
            pltpu.SemaphoreType.DMA((3 + CHUNKS,)),
            pltpu.SemaphoreType.DMA((24,)),
        ],
        compiler_params=limits,
        name="opening",
    )(*(left(array) for array in (micro, segment, gain, table, w_query, w_key, w_value, w_out)))
    out, k_rows, v_rows, cosines, bias = got[:5]
    weights = (got[9], *got[5:9])
    table = got[10]
    streams = [out, *got[11:]]

    for tick_index in range(TICKS):
        last = tick_index == TICKS - 1
        outs, keys, values = [], [], []
        for index in range(CHUNKS):
            if tick_index == 0 and index == 0:
                outs.append(passed_along(streams[0]))
                keys.append(k_rows)
                values.append(v_rows)
                continue
            paired = isinstance(streams[index], tuple)
            args = [*(streams[index] if paired else [streams[index]]), *weights]
            shapes = [kept((rows[index], model), BF16), *key_values]
            scratch = [mixing]
            if index == 0:
                args.append(table)
                shapes += tables
            else:
                args += [cosines, bias, *keys, *values]
            specs = [VMEM] * len(shapes)
            ending = last and index == CHUNKS - 1
            if ending:
                args += outs
                shapes = [jax.ShapeDtypeStruct((1, length, model), BF16)]
                specs = [pl.BlockSpec(memory_space=pl.ANY)]
                scratch = [
                    pltpu.VMEM((size, model), BF16), *[pltpu.VMEM((size, KV_WIDTH), BF16)] * 2,
                    pltpu.SemaphoreType.DMA((CHUNKS,)), mixing,
                ]
            if paired:
                scratch = [*scratch, pltpu.VMEM((rows[index], model), BF16), pltpu.SemaphoreType.DMA]
            got = pl.pallas_call(
                functools.partial(chunk_kernel, index, last, paired),
                out_shape=tuple(shapes), in_specs=[HBM] * (2 * paired) + [VMEM] * (len(args) - 2 * paired), out_specs=tuple(specs),
                scratch_shapes=scratch, compiler_params=limits, name="chunk_%d_%d" % (tick_index, index),
            )(*map(left, args[: 2 * paired]), *map(held, args[2 * paired :]))
            if ending:
                return got[0]
            if index == 0:
                cosines, bias = got[3:]
            keys.append(got[1])
            values.append(got[2])
            outs.append(got[0] if last else passed_along(got[0]))
        streams = outs


def solution(mesh):
    in_specs = (
        P(("groups", "section"), None, None),
        P(("groups", "section"), None),
        P("section", None),
        P("section", None, None),
        P("section", None, None),
        P("section", None, None),
        P("section", None, None),
    )
    out_specs = P(("groups", "section"), None, None)
    return jax.shard_map(body, mesh=mesh, in_specs=in_specs, out_specs=out_specs, check_vma=False)
```

```python
import functools

import jax
import jax.numpy as jnp
import numpy as np
from jax import lax
from jax.experimental import pallas as pl
from jax.experimental.pallas import tpu as pltpu
from jax.sharding import PartitionSpec as P

HEADS = 16
KV_HEADS = 8
HD = 128
TICKS = 4
MAX_LEN = 96
CHUNKS = 2
EXTRA = 16
LIFT = 16.0
HIDDEN = -1e30
PAIR = 2 * HD
Q_WIDTH = HEADS * HD
KV_WIDTH = KV_HEADS * HD
BF16 = jnp.bfloat16
F32 = jnp.float32


def rope_table():
    middle = HD // 2
    spacing = 1000000.0 ** (-2.0 * np.arange(middle) / HD)
    angles = np.arange(MAX_LEN)[:, None] * spacing[None, :]
    cosine, sine = np.cos(angles), np.sin(angles)
    whole = np.concatenate([cosine, cosine, -sine, sine], axis=1).astype(np.float32)
    high = whole.astype(jnp.bfloat16).astype(np.float32)
    low = (whole - high).astype(jnp.bfloat16).astype(np.float32)
    return np.concatenate([high, low], axis=0)


def tables_of(ids_row, table):
    length = ids_row.shape[1]
    across = jnp.broadcast_to(ids_row, (length, length))
    down = across.T
    row_index = lax.broadcasted_iota(jnp.int32, (length, length), 0)
    column = lax.broadcasted_iota(jnp.int32, (length, length), 1)
    matched = across == down
    places = jnp.sum(jnp.where(matched & (column < row_index), 1.0, 0.0), axis=1, keepdims=True)
    bias = jnp.where(matched & (column <= row_index), 0.0, HIDDEN)
    slots = lax.broadcasted_iota(jnp.int32, (length, 2 * MAX_LEN), 1)
    slots = jnp.where(slots >= MAX_LEN, slots - MAX_LEN, slots).astype(F32)
    one_hot = jnp.where(slots == places, 1.0, 0.0).astype(BF16)
    factors = jnp.dot(one_hot, table, preferred_element_type=F32)
    return factors, bias


def rotated(values, cosine, sine):
    return values * cosine + pltpu.roll(values, HD // 2, 1) * sine


def blocks_of(low, size):
    if low == 0 and size <= MAX_LEN:
        return [(0, size, 0, size)]
    step = HD - MAX_LEN
    return [(top, step, max(0, low + top - MAX_LEN), low + top + step) for top in range(0, size, step)]


def layer(x, gain, weights, wait, low, cos_rows, bias_ref, kept_keys, kept_values, k_ref, v_ref, mixed_ref, write):
    size, model = x.shape
    wq_ref, wk_ref, wv_ref, wo_ref = weights
    scale = lax.rsqrt(jnp.mean(x * x, axis=1, keepdims=True) + 1e-05) * (1.0 / LIFT)
    lifted = (x * gain).astype(BF16)
    cosine = cos_rows[:, :HD] * scale
    sine = cos_rows[:, HD:] * scale
    factor = HD ** (-0.5) * np.log2(np.e)
    cosine_q = cosine * factor
    sine_q = sine * factor

    for start in range(0, KV_WIDTH, PAIR):
        wait("k", start)
        got = jnp.dot(lifted, wk_ref[:, start : start + PAIR], preferred_element_type=F32)
        for half in range(0, PAIR, HD):
            turned = rotated(got[:, half : half + HD], cosine, sine)
            k_ref[:, start + half : start + half + HD] = turned.astype(BF16)
    for start in range(0, KV_WIDTH, PAIR):
        wait("v", start)
        got = jnp.dot(lifted, wv_ref[:, start : start + PAIR], preferred_element_type=F32)
        v_ref[:, start : start + PAIR] = (got * scale).astype(BF16)
    queries = []
    for start in range(0, Q_WIDTH, PAIR):
        wait("q", start)
        got = jnp.dot(lifted, wq_ref[:, start : start + PAIR], preferred_element_type=F32)
        upper = rotated(got[:, :HD], cosine_q, sine_q)
        lower = rotated(got[:, HD:], cosine_q, sine_q)
        queries.append((upper.astype(BF16), lower.astype(BF16)))

    blocks = blocks_of(low, size)
    biases = [bias_ref[low + top : low + top + height, first:last] for top, height, first, last in blocks]
    spots = [(group, index) for group in range(KV_HEADS) for index in range(len(blocks))]

    def seen(kept_parts, own_ref, group, first, last):
        lanes, parts = slice(group * HD, (group + 1) * HD), []
        for place, ref in enumerate([*kept_parts, own_ref]):
            start, stop = max(first, place * size), min(last, (place + 1) * size)
            if start < stop:
                parts.append(ref[start - place * size : stop - place * size, lanes])
        return parts[0] if len(parts) == 1 else jnp.concatenate(parts, axis=0)

    scores = []
    for group, index in spots:
        top, height, first, last = blocks[index]
        both = jnp.concatenate([half[top : top + height] for half in queries[group]], axis=0)
        key_rows = seen(kept_keys, k_ref, group, first, last)
        got = lax.dot_general(both, key_rows, (((1,), (1,)), ((), ())), preferred_element_type=F32)
        scores.append(got.reshape(2, height, last - first) + biases[index][None])
    most = [jnp.max(part, axis=2, keepdims=True) for part in scores]
    expo = [
        jnp.exp2(part - peak).astype(BF16).reshape(2 * part.shape[1], part.shape[2])
        for part, peak in zip(scores, most)
    ]
    got = []
    for (group, index), part in zip(spots, expo):
        first, last = blocks[index][2:]
        ones = jnp.ones((last - first, HD), BF16)
        value_rows = jnp.concatenate([seen(kept_values, v_ref, group, first, last), ones], axis=1)
        got.append(jnp.dot(part, value_rows, preferred_element_type=F32))
    for (group, index), part in zip(spots, got):
        top, height = blocks[index][:2]
        total = part[:, HD:]
        inverse = pl.reciprocal(total, approx=True)
        inverse = inverse * (2.0 - total * inverse)
        mixed = (part[:, :HD] * inverse).astype(BF16)
        mixed_ref[top : top + height, group * PAIR : group * PAIR + HD] = mixed[:height]
        mixed_ref[top : top + height, group * PAIR + HD : (group + 1) * PAIR] = mixed[height:]
    for start in range(0, model, PAIR):
        wait("o", start)
        update = jnp.dot(mixed_ref[...], wo_ref[:, start : start + PAIR], preferred_element_type=F32)
        write(start, x[:, start : start + PAIR] + update)


def write_ids(ids_row, out_ref, size):
    length = ids_row.shape[1]
    out_ref[size:, :] = jnp.zeros((EXTRA, out_ref.shape[1]), BF16)
    out_ref[size:, :length] = jnp.broadcast_to(ids_row, (EXTRA, length)).astype(BF16)


def opening_kernel(
    size, x_hbm, ids_hbm, gain_hbm, table_hbm, wq_hbm, wk_hbm, wv_hbm, wo_hbm,
    out_ref, k_ref, v_ref, cos_ref, bias_ref, wq_ref, wk_ref, wv_ref, wo_ref, gain_ref, table_ref, *refs,
):
    rest_refs, refs = refs[: CHUNKS - 1], refs[CHUNKS - 1 :]
    x_ref, ids_ref, raw_gain, raw_table, mixed_ref, small_sems, sems = refs
    small = [
        pltpu.make_async_copy(ids_hbm, ids_ref, small_sems.at[0]),
        pltpu.make_async_copy(table_hbm, raw_table, small_sems.at[1]),
        pltpu.make_async_copy(gain_hbm, raw_gain, small_sems.at[2]),
        pltpu.make_async_copy(x_hbm.at[0, :size], x_ref, small_sems.at[3]),
    ]
    late = [
        pltpu.make_async_copy(x_hbm.at[0, (i + 1) * size : (i + 2) * size], rest_refs[i], small_sems.at[4 + i])
        for i in range(CHUNKS - 1)
    ]
    made = []

    def batch(source, target, rows, lanes):
        step = (rows.stop - rows.start) // 8
        copies = []
        for low in range(rows.start, rows.stop, step):
            part = (slice(low, low + step), lanes)
            copies.append(pltpu.make_async_copy(source.at[(0, *part)], target.at[part], sems.at[len(made)]))
            made.append(copies[-1])
        return copies

    model, half = wk_ref.shape[0], Q_WIDTH // 2
    narrow, wide = slice(0, KV_WIDTH), slice(0, Q_WIDTH)
    batches = [
        batch(wk_hbm, wk_ref, slice(0, model), narrow),
        batch(wv_hbm, wv_ref, slice(0, model), narrow),
        batch(wq_hbm, wq_ref, slice(0, model // 2), wide),
        batch(wq_hbm, wq_ref, slice(model // 2, model), wide),
        batch(wo_hbm, wo_ref, slice(0, half), slice(0, model)),
        batch(wo_hbm, wo_ref, slice(half, Q_WIDTH), slice(0, model)),
    ]
    arrivals = {("k", 0): (0,), ("v", 0): (1,), ("q", 0): (2, 3), ("o", 0): (4, 5)}

    def begin(index):
        if index < len(batches):
            for copy in batches[index]:
                copy.start()
        if index == len(batches):
            for copy in late:
                copy.start()

    def wait(name, start):
        for index in arrivals.get((name, start), ()):
            for copy in batches[index]:
                copy.wait()
            begin(index + 2)

    for copy in small:
        copy.start()
    for index in range(2):
        begin(index)
    for copy in small:
        copy.wait()
    gain_ref[...] = raw_gain[...].astype(F32) * LIFT
    table_ref[...] = raw_table[...].astype(BF16)
    ids_row = ids_ref[...].astype(F32)
    factors, bias = tables_of(ids_row, table_ref[...])
    cos_ref[...] = factors
    bias_ref[...] = bias
    write_ids(ids_row, out_ref, size)

    def write(start, values):
        out_ref[:size, start : start + PAIR] = values.astype(BF16)

    layer(
        x_ref[...].astype(F32), gain_ref[...], (wq_ref, wk_ref, wv_ref, wo_ref), wait,
        0, cos_ref[:size, :], bias_ref, [], [], k_ref, v_ref, mixed_ref, write,
    )
    for copy in late:
        copy.wait()


def chunk_kernel(index, last, x_ref, gain_ref, wq_ref, wk_ref, wv_ref, wo_ref, *refs):
    refs = list(refs)
    mixed_ref = refs.pop(-1)
    size = mixed_ref.shape[0]
    low, high = index * size, (index + 1) * size
    if index == 0:
        table_ref = refs.pop(0)
        out_ref, k_ref, v_ref, cos_ref, bias_ref = refs
        factors, bias = tables_of(x_ref[size:, : CHUNKS * size].astype(F32)[:1], table_ref[...])
        cos_ref[...] = factors
        bias_ref[...] = bias
        if not last:
            out_ref[size:, :] = x_ref[size:, :]
        keys, values = [], []
    else:
        cos_ref, bias_ref = refs[:2]
        keys, values, refs = refs[2 : 2 + index], refs[2 + index : 2 + 2 * index], refs[2 + 2 * index :]
        if last and index == CHUNKS - 1:
            done, (whole_ref, out_ref, k_ref, v_ref, sems) = refs[:index], refs[index:]
            copies = [
                pltpu.make_async_copy(done[i].at[:size], whole_ref.at[0, i * size : (i + 1) * size], sems.at[i])
                for i in range(index)
            ]
            for copy in copies:
                copy.start()
        else:
            out_ref, k_ref, v_ref = refs

    def write(start, result):
        out_ref[:size, start : start + PAIR] = result.astype(BF16)

    layer(
        x_ref[:size, :].astype(F32), gain_ref[...], (wq_ref, wk_ref, wv_ref, wo_ref), lambda name, start: None,
        low, cos_ref[low:high, :], bias_ref, keys, values, k_ref, v_ref, mixed_ref, write,
    )
    if last and index == CHUNKS - 1:
        copy = pltpu.make_async_copy(out_ref, whole_ref.at[0, low:high], sems.at[index])
        copy.start()
        for each in copies + [copy]:
            each.wait()


VMEM = pl.BlockSpec(memory_space=pltpu.VMEM)
HBM = pl.BlockSpec(memory_space=pltpu.HBM)


def kept(shape, dtype):
    return pltpu.VMEM(shape, dtype)


def held(array):
    return pltpu.with_memory_space_constraint(array, pltpu.VMEM)


def left(array):
    return pltpu.with_memory_space_constraint(array, pltpu.HBM)


def passed_along(array, by):
    length = lax.axis_size("section")
    return lax.ppermute(array, "section", [(i, (i + by) % length) for i in range(length)])


def body(micro, segment, gain, w_query, w_key, w_value, w_out):
    length, model = micro.shape[1], micro.shape[2]
    size = length // CHUNKS
    limits = pltpu.CompilerParams(vmem_limit_bytes=32 * 1024 * 1024)
    table = jnp.asarray(rope_table())
    rows = [size + EXTRA] + [size] * (CHUNKS - 1)
    key_values = [kept((size, KV_WIDTH), BF16)] * 2
    tables = [kept((length, PAIR), F32), kept((length, length), F32)]
    mixing = pltpu.VMEM((size, Q_WIDTH), BF16)

    got = pl.pallas_call(
        functools.partial(opening_kernel, size),
        out_shape=(
            kept((rows[0], model), BF16),
            *key_values,
            *tables,
            kept((model, Q_WIDTH), BF16),
            kept((model, KV_WIDTH), BF16),
            kept((model, KV_WIDTH), BF16),
            kept((Q_WIDTH, model), BF16),
            kept((1, model), F32),
            kept(table.shape, BF16),
            *[kept((size, model), BF16)] * (CHUNKS - 1),
        ),
        in_specs=[HBM] * 8,
        out_specs=(VMEM,) * (10 + CHUNKS),
        scratch_shapes=[
            pltpu.VMEM((size, model), BF16),
            pltpu.VMEM(segment.shape, jnp.int32),
            pltpu.VMEM(gain.shape, BF16),
            pltpu.VMEM(table.shape, F32),
            mixing,
            pltpu.SemaphoreType.DMA((3 + CHUNKS,)),
            pltpu.SemaphoreType.DMA((48,)),
        ],
        compiler_params=limits,
        name="opening",
    )(*(left(array) for array in (micro, segment, gain, table, w_query, w_key, w_value, w_out)))
    out, k_rows, v_rows, cosines, bias = got[:5]
    weights = (got[9], *got[5:9])
    table = got[10]
    streams = [out, *got[11:]]

    for tick_index in range(TICKS):
        last = tick_index == TICKS - 1
        outs, keys, values = [], [], []
        for index in range(CHUNKS):
            if tick_index == 0 and index == 0:
                outs.append(passed_along(streams[0], 1))
                keys.append(k_rows)
                values.append(v_rows)
                continue
            args = [streams[index], *weights]
            shapes = [kept((rows[index], model), BF16), *key_values]
            scratch = [mixing]
            if index == 0:
                args.append(table)
                shapes += tables
            else:
                args += [cosines, bias, *keys, *values]
            specs = [VMEM] * len(shapes)
            ending = last and index == CHUNKS - 1
            if ending:
                args += outs
                shapes = [jax.ShapeDtypeStruct((1, length, model), BF16)]
                specs = [pl.BlockSpec(memory_space=pl.ANY)]
                scratch = [
                    pltpu.VMEM((size, model), BF16), *[pltpu.VMEM((size, KV_WIDTH), BF16)] * 2,
                    pltpu.SemaphoreType.DMA((CHUNKS,)), mixing,
                ]
            got = pl.pallas_call(
                functools.partial(chunk_kernel, index, last),
                out_shape=tuple(shapes), in_specs=[VMEM] * len(args), out_specs=tuple(specs),
                scratch_shapes=scratch, compiler_params=limits, name="chunk_%d_%d" % (tick_index, index),
            )(*map(held, args))
            if ending:
                return got[0]
            if index == 0:
                cosines, bias = got[3:]
            keys.append(got[1])
            values.append(got[2])
            outs.append(got[0] if last else passed_along(got[0], 1))
        streams = outs


def solution(mesh):
    in_specs = (
        P(("groups", "section"), None, None),
        P(("groups", "section"), None),
        P("section", None),
        P("section", None, None),
        P("section", None, None),
        P("section", None, None),
        P("section", None, None),
    )
    out_specs = P(("groups", "section"), None, None)
    return jax.shard_map(body, mesh=mesh, in_specs=in_specs, out_specs=out_specs, check_vma=False)
```

```python
import functools

import jax
import jax.numpy as jnp
import numpy as np
from jax import lax
from jax.experimental import pallas as pl
from jax.experimental.pallas import tpu as pltpu
from jax.sharding import PartitionSpec as P

HEADS = 16
KV_HEADS = 8
HD = 128
TICKS = 4
MAX_LEN = 96
CHUNKS = 2
EXTRA = 16
LIFT = 16.0
HIDDEN = -1e30
PAIR = 2 * HD
Q_WIDTH = HEADS * HD
KV_WIDTH = KV_HEADS * HD
BF16 = jnp.bfloat16
F32 = jnp.float32


def rope_table():
    middle = HD // 2
    spacing = 1000000.0 ** (-2.0 * np.arange(middle) / HD)
    angles = np.arange(MAX_LEN)[:, None] * spacing[None, :]
    cosine, sine = np.cos(angles), np.sin(angles)
    whole = np.concatenate([cosine, cosine, -sine, sine], axis=1).astype(np.float32)
    high = whole.astype(jnp.bfloat16).astype(np.float32)
    low = (whole - high).astype(jnp.bfloat16).astype(np.float32)
    return np.concatenate([high, low], axis=0)


def lower_triangle(rows, columns):
    row_index = lax.broadcasted_iota(jnp.int32, (rows, columns), 0)
    return lax.broadcasted_iota(jnp.int32, (rows, columns), 1) <= row_index


def tables_of(ids_row, table):
    length = ids_row.shape[1]
    across = jnp.broadcast_to(ids_row, (length, length))
    down = across.T
    row_index = lax.broadcasted_iota(jnp.int32, (length, length), 0)
    column = lax.broadcasted_iota(jnp.int32, (length, length), 1)
    matched = across == down
    places = jnp.sum(jnp.where(matched & (column < row_index), 1.0, 0.0), axis=1, keepdims=True)
    bias = jnp.where(matched & (column <= row_index), 0.0, HIDDEN)
    own, earlier_keys = bias[MAX_LEN:, MAX_LEN:], bias[MAX_LEN:, :MAX_LEN]
    merged = jnp.where(lower_triangle(MAX_LEN, MAX_LEN), own, earlier_keys)
    merged = jnp.concatenate([merged, jnp.full((length - MAX_LEN, HD - MAX_LEN), HIDDEN, F32)], axis=1)
    bias = jnp.concatenate([bias[:MAX_LEN, :HD], merged], axis=0)
    slots = lax.broadcasted_iota(jnp.int32, (length, 2 * MAX_LEN), 1)
    slots = jnp.where(slots >= MAX_LEN, slots - MAX_LEN, slots).astype(F32)
    one_hot = jnp.where(slots == places, 1.0, 0.0).astype(BF16)
    factors = jnp.dot(one_hot, table, preferred_element_type=F32)
    return factors, bias


def rotated(values, cosine, sine):
    return values * cosine + pltpu.roll(values, HD // 2, 1) * sine


def layer(x, gain, weights, wait, cos_rows, bias_rows, kept_keys, kept_values, k_ref, v_ref, mixed_ref, write):
    size, model = x.shape
    wq_ref, wk_ref, wv_ref, wo_ref = weights
    scale = lax.rsqrt(jnp.mean(x * x, axis=1, keepdims=True) + 1e-05) * (1.0 / LIFT)
    lifted = (x * gain).astype(BF16)
    cosine = cos_rows[:, :HD] * scale
    sine = cos_rows[:, HD:] * scale
    factor = HD ** (-0.5) * np.log2(np.e)
    cosine_q = cosine * factor
    sine_q = sine * factor

    for start in range(0, KV_WIDTH, PAIR):
        wait("k", start)
        got = jnp.dot(lifted, wk_ref[:, start : start + PAIR], preferred_element_type=F32)
        for half in range(0, PAIR, HD):
            turned = rotated(got[:, half : half + HD], cosine, sine)
            k_ref[:, start + half : start + half + HD] = turned.astype(BF16)
    for start in range(0, KV_WIDTH, PAIR):
        wait("v", start)
        got = jnp.dot(lifted, wv_ref[:, start : start + PAIR], preferred_element_type=F32)
        v_ref[:, start : start + PAIR] = (got * scale).astype(BF16)
    queries = []
    for start in range(0, Q_WIDTH, PAIR):
        wait("q", start)
        got = jnp.dot(lifted, wq_ref[:, start : start + PAIR], preferred_element_type=F32)
        upper = rotated(got[:, :HD], cosine_q, sine_q)
        lower = rotated(got[:, HD:], cosine_q, sine_q)
        queries.append(jnp.concatenate([upper, lower], axis=0).astype(BF16))

    groups = range(KV_HEADS)
    spare = jnp.zeros((HD - size, HD), BF16)
    lower = lower_triangle(size, HD)
    lower_share = jnp.where(lower, 1.0, 0.0).astype(BF16)

    def rows_of(refs, group):
        lanes = slice(group * HD, (group + 1) * HD)
        if len(refs) == 1:
            return refs[0][:, lanes]
        return jnp.concatenate([part for ref in refs for part in (ref[:, lanes], spare)], axis=0)

    key_refs, value_refs = [k_ref, *kept_keys], [v_ref, *kept_values]
    scores = []
    for group in groups:
        key_rows = rows_of(key_refs, group)
        got = lax.dot_general(queries[group], key_rows, (((1,), (1,)), ((), ())), preferred_element_type=F32)
        got = got.reshape(2, size, key_rows.shape[0])
        if kept_keys:
            got = jnp.where(lower[None], got[:, :, :HD], got[:, :, HD:])
        scores.append(got + bias_rows[None])
    most = [jnp.max(part, axis=2, keepdims=True) for part in scores]
    expo = [jnp.exp2(scores[g] - most[g]).astype(BF16) for g in groups]
    if kept_keys:
        own = [part * lower_share[None] for part in expo]
        expo = [jnp.concatenate([mine, part - mine], axis=2) for mine, part in zip(own, expo)]
    got = []
    for group in groups:
        value_rows = rows_of(value_refs, group)
        value_rows = jnp.concatenate([value_rows, jnp.ones((value_rows.shape[0], HD), BF16)], axis=1)
        part = expo[group].reshape(2 * size, value_rows.shape[0])
        got.append(jnp.dot(part, value_rows, preferred_element_type=F32))
    for group in groups:
        total = got[group][:, HD:]
        inverse = pl.reciprocal(total, approx=True)
        inverse = inverse * (2.0 - total * inverse)
        mixed = (got[group][:, :HD] * inverse).astype(BF16)
        mixed_ref[:, group * PAIR : group * PAIR + HD] = mixed[:size]
        mixed_ref[:, group * PAIR + HD : (group + 1) * PAIR] = mixed[size:]
    for start in range(0, model, PAIR):
        wait("o", start)
        update = jnp.dot(mixed_ref[...], wo_ref[:, start : start + PAIR], preferred_element_type=F32)
        write(start, x[:, start : start + PAIR] + update)


def write_ids(ids_row, out_ref, size):
    length = ids_row.shape[1]
    out_ref[size:, :] = jnp.zeros((EXTRA, out_ref.shape[1]), BF16)
    out_ref[size:, :length] = jnp.broadcast_to(ids_row, (EXTRA, length)).astype(BF16)


def opening_kernel(
    size, x_hbm, ids_hbm, gain_hbm, table_hbm, wq_hbm, wk_hbm, wv_hbm, wo_hbm,
    out_ref, k_ref, v_ref, cos_ref, bias_ref, wq_ref, wk_ref, wv_ref, wo_ref, gain_ref, table_ref, *refs,
):
    rest_refs, refs = refs[: CHUNKS - 1], refs[CHUNKS - 1 :]
    x_ref, ids_ref, raw_gain, raw_table, mixed_ref, small_sems, sems = refs
    small = [
        pltpu.make_async_copy(ids_hbm, ids_ref, small_sems.at[0]),
        pltpu.make_async_copy(table_hbm, raw_table, small_sems.at[1]),
        pltpu.make_async_copy(gain_hbm, raw_gain, small_sems.at[2]),
        pltpu.make_async_copy(x_hbm.at[0, :size], x_ref, small_sems.at[3]),
    ]
    late = [
        pltpu.make_async_copy(x_hbm.at[0, (i + 1) * size : (i + 2) * size], rest_refs[i], small_sems.at[4 + i])
        for i in range(CHUNKS - 1)
    ]
    made = []

    def batch(source, target, rows, lanes):
        step = (rows.stop - rows.start) // 2
        copies = []
        for low in range(rows.start, rows.stop, step):
            part = (slice(low, low + step), lanes)
            copies.append(pltpu.make_async_copy(source.at[(0, *part)], target.at[part], sems.at[len(made)]))
            made.append(copies[-1])
        return copies

    model, half = wk_ref.shape[0], Q_WIDTH // 2
    narrow, wide = slice(0, KV_WIDTH), slice(0, Q_WIDTH)
    batches = [
        batch(wk_hbm, wk_ref, slice(0, model), narrow),
        batch(wv_hbm, wv_ref, slice(0, model), narrow),
        batch(wq_hbm, wq_ref, slice(0, model // 2), wide),
        batch(wq_hbm, wq_ref, slice(model // 2, model), wide),
        batch(wo_hbm, wo_ref, slice(0, half), slice(0, model)),
        batch(wo_hbm, wo_ref, slice(half, Q_WIDTH), slice(0, model)),
    ]
    arrivals = {("k", 0): (0,), ("v", 0): (1,), ("q", 0): (2, 3), ("o", 0): (4, 5)}

    def begin(index):
        if index < len(batches):
            for copy in batches[index]:
                copy.start()
        if index == len(batches):
            for copy in late:
                copy.start()

    def wait(name, start):
        for index in arrivals.get((name, start), ()):
            for copy in batches[index]:
                copy.wait()
            begin(index + 3)

    for copy in small:
        copy.start()
    for index in range(3):
        begin(index)
    for copy in small:
        copy.wait()
    gain_ref[...] = raw_gain[...].astype(F32) * LIFT
    table_ref[...] = raw_table[...].astype(BF16)
    ids_row = ids_ref[...].astype(F32)
    factors, bias = tables_of(ids_row, table_ref[...])
    cos_ref[...] = factors
    bias_ref[...] = bias
    write_ids(ids_row, out_ref, size)

    def write(start, values):
        out_ref[:size, start : start + PAIR] = values.astype(BF16)

    layer(
        x_ref[...].astype(F32), gain_ref[...], (wq_ref, wk_ref, wv_ref, wo_ref), wait,
        cos_ref[:size, :], bias_ref[:size, :size], [], [], k_ref, v_ref, mixed_ref, write,
    )
    for copy in late:
        copy.wait()


def chunk_kernel(index, last, x_ref, gain_ref, wq_ref, wk_ref, wv_ref, wo_ref, *refs):
    refs = list(refs)
    mixed_ref = refs.pop(-1)
    size = mixed_ref.shape[0]
    low, high = index * size, (index + 1) * size
    if index == 0:
        table_ref = refs.pop(0)
        out_ref, k_ref, v_ref, cos_ref, bias_ref = refs
        factors, bias = tables_of(x_ref[size:, : CHUNKS * size].astype(F32)[:1], table_ref[...])
        cos_ref[...] = factors
        bias_ref[...] = bias
        if not last:
            out_ref[size:, :] = x_ref[size:, :]
        keys, values = [], []
    else:
        cos_ref, bias_ref = refs[:2]
        keys, values, refs = refs[2 : 2 + index], refs[2 + index : 2 + 2 * index], refs[2 + 2 * index :]
        if last and index == CHUNKS - 1:
            done, (whole_ref, out_ref, k_ref, v_ref, sems) = refs[:index], refs[index:]
            copies = [
                pltpu.make_async_copy(done[i].at[:size], whole_ref.at[0, i * size : (i + 1) * size], sems.at[i])
                for i in range(index)
            ]
            for copy in copies:
                copy.start()
        else:
            out_ref, k_ref, v_ref = refs

    def write(start, result):
        out_ref[:size, start : start + PAIR] = result.astype(BF16)

    layer(
        x_ref[:size, :].astype(F32), gain_ref[...], (wq_ref, wk_ref, wv_ref, wo_ref), lambda name, start: None,
        cos_ref[low:high, :], bias_ref[low:high, :] if index else bias_ref[:size, :size],
        keys, values, k_ref, v_ref, mixed_ref, write,
    )
    if last and index == CHUNKS - 1:
        copy = pltpu.make_async_copy(out_ref, whole_ref.at[0, low:high], sems.at[index])
        copy.start()
        for each in copies + [copy]:
            each.wait()


VMEM = pl.BlockSpec(memory_space=pltpu.VMEM)
HBM = pl.BlockSpec(memory_space=pltpu.HBM)


def kept(shape, dtype):
    return pltpu.VMEM(shape, dtype)


def held(array):
    return pltpu.with_memory_space_constraint(array, pltpu.VMEM)


def left(array):
    return pltpu.with_memory_space_constraint(array, pltpu.HBM)


def passed_along(array, by):
    length = lax.axis_size("section")
    return lax.ppermute(array, "section", [(i, (i + by) % length) for i in range(length)])


def body(micro, segment, gain, w_query, w_key, w_value, w_out):
    length, model = micro.shape[1], micro.shape[2]
    size = length // CHUNKS
    limits = pltpu.CompilerParams(vmem_limit_bytes=32 * 1024 * 1024)
    table = jnp.asarray(rope_table())
    rows = [size + EXTRA] + [size] * (CHUNKS - 1)
    key_values = [kept((size, KV_WIDTH), BF16)] * 2
    tables = [kept((length, PAIR), F32), kept((length, HD), F32)]
    mixing = pltpu.VMEM((size, Q_WIDTH), BF16)

    got = pl.pallas_call(
        functools.partial(opening_kernel, size),
        out_shape=(
            kept((rows[0], model), BF16),
            *key_values,
            *tables,
            kept((model, Q_WIDTH), BF16),
            kept((model, KV_WIDTH), BF16),
            kept((model, KV_WIDTH), BF16),
            kept((Q_WIDTH, model), BF16),
            kept((1, model), F32),
            kept(table.shape, BF16),
            *[kept((size, model), BF16)] * (CHUNKS - 1),
        ),
        in_specs=[HBM] * 8,
        out_specs=(VMEM,) * (10 + CHUNKS),
        scratch_shapes=[
            pltpu.VMEM((size, model), BF16),
            pltpu.VMEM(segment.shape, jnp.int32),
            pltpu.VMEM(gain.shape, BF16),
            pltpu.VMEM(table.shape, F32),
            mixing,
            pltpu.SemaphoreType.DMA((3 + CHUNKS,)),
            pltpu.SemaphoreType.DMA((12,)),
        ],
        compiler_params=limits,
        name="opening",
    )(*(left(array) for array in (micro, segment, gain, table, w_query, w_key, w_value, w_out)))
    out, k_rows, v_rows, cosines, bias = got[:5]
    weights = (got[9], *got[5:9])
    table = got[10]
    streams = [out, *got[11:]]

    for tick_index in range(TICKS):
        last = tick_index == TICKS - 1
        outs, keys, values = [], [], []
        for index in range(CHUNKS):
            if tick_index == 0 and index == 0:
                outs.append(passed_along(streams[0], 1))
                keys.append(k_rows)
                values.append(v_rows)
                continue
            args = [streams[index], *weights]
            shapes = [kept((rows[index], model), BF16), *key_values]
            scratch = [mixing]
            if index == 0:
                args.append(table)
                shapes += tables
            else:
                args += [cosines, bias, *keys, *values]
            specs = [VMEM] * len(shapes)
            ending = last and index == CHUNKS - 1
            if ending:
                args += outs
                shapes = [jax.ShapeDtypeStruct((1, length, model), BF16)]
                specs = [pl.BlockSpec(memory_space=pl.ANY)]
                scratch = [
                    pltpu.VMEM((size, model), BF16), *[pltpu.VMEM((size, KV_WIDTH), BF16)] * 2,
                    pltpu.SemaphoreType.DMA((CHUNKS,)), mixing,
                ]
            got = pl.pallas_call(
                functools.partial(chunk_kernel, index, last),
                out_shape=tuple(shapes), in_specs=[VMEM] * len(args), out_specs=tuple(specs),
                scratch_shapes=scratch, compiler_params=limits, name="chunk_%d_%d" % (tick_index, index),
            )(*map(held, args))
            if ending:
                return got[0]
            if index == 0:
                cosines, bias = got[3:]
            keys.append(got[1])
            values.append(got[2])
            outs.append(got[0] if last else passed_along(got[0], 1))
        streams = outs


def solution(mesh):
    in_specs = (
        P(("groups", "section"), None, None),
        P(("groups", "section"), None),
        P("section", None),
        P("section", None, None),
        P("section", None, None),
        P("section", None, None),
        P("section", None, None),
    )
    out_specs = P(("groups", "section"), None, None)
    return jax.shard_map(body, mesh=mesh, in_specs=in_specs, out_specs=out_specs, check_vma=False)
```

```python
import functools

import jax
import jax.numpy as jnp
import numpy as np
from jax import lax
from jax.experimental import pallas as pl
from jax.experimental.pallas import tpu as pltpu
from jax.sharding import PartitionSpec as P

HEADS = 16
KV_HEADS = 8
HD = 128
TICKS = 4
MAX_LEN = 96
CHUNKS = 2
EXTRA = 16
LIFT = 16.0
HIDDEN = -1e30
PAIR = 2 * HD
Q_WIDTH = HEADS * HD
KV_WIDTH = KV_HEADS * HD
BF16 = jnp.bfloat16
F32 = jnp.float32


def rope_table():
    middle = HD // 2
    spacing = 1000000.0 ** (-2.0 * np.arange(middle) / HD)
    angles = np.arange(MAX_LEN)[:, None] * spacing[None, :]
    cosine, sine = np.cos(angles), np.sin(angles)
    whole = np.concatenate([cosine, cosine, -sine, sine], axis=1).astype(np.float32)
    high = whole.astype(jnp.bfloat16).astype(np.float32)
    low = (whole - high).astype(jnp.bfloat16).astype(np.float32)
    return np.concatenate([high, low], axis=0)


def lower_triangle(rows, columns):
    row_index = lax.broadcasted_iota(jnp.int32, (rows, columns), 0)
    return lax.broadcasted_iota(jnp.int32, (rows, columns), 1) <= row_index


def tables_of(ids_row, table):
    length = ids_row.shape[1]
    across = jnp.broadcast_to(ids_row, (length, length))
    down = across.T
    row_index = lax.broadcasted_iota(jnp.int32, (length, length), 0)
    column = lax.broadcasted_iota(jnp.int32, (length, length), 1)
    matched = across == down
    places = jnp.sum(jnp.where(matched & (column < row_index), 1.0, 0.0), axis=1, keepdims=True)
    bias = jnp.where(matched & (column <= row_index), 0.0, HIDDEN)
    own, earlier_keys = bias[MAX_LEN:, MAX_LEN:], bias[MAX_LEN:, :MAX_LEN]
    merged = jnp.where(lower_triangle(MAX_LEN, MAX_LEN), own, earlier_keys)
    merged = jnp.concatenate([merged, jnp.full((length - MAX_LEN, HD - MAX_LEN), HIDDEN, F32)], axis=1)
    bias = jnp.concatenate([bias[:MAX_LEN, :HD], merged], axis=0)
    slots = lax.broadcasted_iota(jnp.int32, (length, 2 * MAX_LEN), 1)
    slots = jnp.where(slots >= MAX_LEN, slots - MAX_LEN, slots).astype(F32)
    one_hot = jnp.where(slots == places, 1.0, 0.0).astype(BF16)
    factors = jnp.dot(one_hot, table, preferred_element_type=F32)
    return factors, bias


def rotated(values, cosine, sine):
    return values * cosine + pltpu.roll(values, HD // 2, 1) * sine


def layer(x, gain, weights, wait, prepare, kept_keys, kept_values, k_ref, v_ref, mixed_ref, write):
    size, model = x.shape
    wq_ref, wk_ref, wv_ref, wo_ref = weights
    scale = lax.rsqrt(jnp.mean(x * x, axis=1, keepdims=True) + 1e-05) * (1.0 / LIFT)
    lifted = (x * gain).astype(BF16)
    for start in range(0, KV_WIDTH, PAIR):
        wait("v", start)
        got = jnp.dot(lifted, wv_ref[:, start : start + PAIR], preferred_element_type=F32)
        v_ref[:, start : start + PAIR] = (got * scale).astype(BF16)
    cos_rows, bias_rows = prepare()
    cosine = cos_rows[:, :HD] * scale
    sine = cos_rows[:, HD:] * scale
    factor = HD ** (-0.5) * np.log2(np.e)
    cosine_q = cosine * factor
    sine_q = sine * factor
    for start in range(0, KV_WIDTH, PAIR):
        wait("k", start)
        got = jnp.dot(lifted, wk_ref[:, start : start + PAIR], preferred_element_type=F32)
        for half in range(0, PAIR, HD):
            turned = rotated(got[:, half : half + HD], cosine, sine)
            k_ref[:, start + half : start + half + HD] = turned.astype(BF16)
    queries = []
    for start in range(0, Q_WIDTH, PAIR):
        wait("q", start)
        got = jnp.dot(lifted, wq_ref[:, start : start + PAIR], preferred_element_type=F32)
        upper = rotated(got[:, :HD], cosine_q, sine_q)
        lower = rotated(got[:, HD:], cosine_q, sine_q)
        queries.append(jnp.concatenate([upper, lower], axis=0).astype(BF16))

    groups = range(KV_HEADS)
    spare = jnp.zeros((HD - size, HD), BF16)
    lower = lower_triangle(size, HD)
    lower_share = jnp.where(lower, 1.0, 0.0).astype(BF16)

    def rows_of(refs, group):
        lanes = slice(group * HD, (group + 1) * HD)
        if len(refs) == 1:
            return refs[0][:, lanes]
        return jnp.concatenate([part for ref in refs for part in (ref[:, lanes], spare)], axis=0)

    key_refs, value_refs = [k_ref, *kept_keys], [v_ref, *kept_values]
    scores = []
    for group in groups:
        key_rows = rows_of(key_refs, group)
        got = lax.dot_general(queries[group], key_rows, (((1,), (1,)), ((), ())), preferred_element_type=F32)
        got = got.reshape(2, size, key_rows.shape[0])
        if kept_keys:
            got = jnp.where(lower[None], got[:, :, :HD], got[:, :, HD:])
        scores.append(got + bias_rows[None])
    most = [jnp.max(part, axis=2, keepdims=True) for part in scores]
    expo = [jnp.exp2(scores[g] - most[g]).astype(BF16) for g in groups]
    if kept_keys:
        own = [part * lower_share[None] for part in expo]
        expo = [jnp.concatenate([mine, part - mine], axis=2) for mine, part in zip(own, expo)]
    got = []
    for group in groups:
        value_rows = rows_of(value_refs, group)
        value_rows = jnp.concatenate([value_rows, jnp.ones((value_rows.shape[0], HD), BF16)], axis=1)
        part = expo[group].reshape(2 * size, value_rows.shape[0])
        got.append(jnp.dot(part, value_rows, preferred_element_type=F32))
    for group in groups:
        total = got[group][:, HD:]
        inverse = pl.reciprocal(total, approx=True)
        inverse = inverse * (2.0 - total * inverse)
        mixed = (got[group][:, :HD] * inverse).astype(BF16)
        mixed_ref[:, group * PAIR : group * PAIR + HD] = mixed[:size]
        mixed_ref[:, group * PAIR + HD : (group + 1) * PAIR] = mixed[size:]
    for start in range(0, model, PAIR):
        wait("o", start)
        update = jnp.dot(mixed_ref[...], wo_ref[:, start : start + PAIR], preferred_element_type=F32)
        write(start, x[:, start : start + PAIR] + update)


def write_ids(ids_row, out_ref, size):
    length = ids_row.shape[1]
    out_ref[size:, :] = jnp.zeros((EXTRA, out_ref.shape[1]), BF16)
    out_ref[size:, :length] = jnp.broadcast_to(ids_row, (EXTRA, length)).astype(BF16)


def opening_kernel(
    size, x_hbm, ids_hbm, gain_hbm, table_hbm, wq_hbm, wk_hbm, wv_hbm, wo_hbm,
    out_ref, k_ref, v_ref, cos_ref, bias_ref, wq_ref, wk_ref, wv_ref, wo_ref, gain_ref, table_ref, *refs,
):
    rest_refs, refs = refs[: CHUNKS - 1], refs[CHUNKS - 1 :]
    x_ref, ids_ref, raw_gain, raw_table, mixed_ref, small_sems, sems = refs
    small = [
        pltpu.make_async_copy(ids_hbm, ids_ref, small_sems.at[0]),
        pltpu.make_async_copy(table_hbm, raw_table, small_sems.at[1]),
        pltpu.make_async_copy(gain_hbm, raw_gain, small_sems.at[2]),
        pltpu.make_async_copy(x_hbm.at[0, :size], x_ref, small_sems.at[3]),
    ]
    late = [
        pltpu.make_async_copy(x_hbm.at[0, (i + 1) * size : (i + 2) * size], rest_refs[i], small_sems.at[4 + i])
        for i in range(CHUNKS - 1)
    ]
    made = []

    def batch(source, target, rows, lanes):
        step = (rows.stop - rows.start) // 2
        copies = []
        for low in range(rows.start, rows.stop, step):
            part = (slice(low, low + step), lanes)
            copies.append(pltpu.make_async_copy(source.at[(0, *part)], target.at[part], sems.at[len(made)]))
            made.append(copies[-1])
        return copies

    model, half = wk_ref.shape[0], Q_WIDTH // 2
    narrow, wide = slice(0, KV_WIDTH), slice(0, Q_WIDTH)
    batches = [
        batch(wv_hbm, wv_ref, slice(0, model), narrow),
        batch(wk_hbm, wk_ref, slice(0, model), narrow),
        batch(wq_hbm, wq_ref, slice(0, model // 2), wide),
        batch(wq_hbm, wq_ref, slice(model // 2, model), wide),
        batch(wo_hbm, wo_ref, slice(0, half), slice(0, model)),
        batch(wo_hbm, wo_ref, slice(half, Q_WIDTH), slice(0, model)),
    ]
    arrivals = {("v", 0): (0,), ("k", 0): (1,), ("q", 0): (2, 3), ("o", 0): (4, 5)}

    def begin(index):
        if index < len(batches):
            for place, copy in enumerate(batches[index]):
                copy.start(priority=place % 2)
        if index == len(batches):
            for copy in late:
                copy.start()

    def wait(name, start):
        for index in arrivals.get((name, start), ()):
            for copy in batches[index]:
                copy.wait()
            begin(index + 4)

    for copy in small:
        copy.start()
    for index in range(4):
        begin(index)
    for copy in small:
        copy.wait()
    gain_ref[...] = raw_gain[...].astype(F32) * LIFT
    table_ref[...] = raw_table[...].astype(BF16)
    ids_row = ids_ref[...].astype(F32)
    factors, bias = tables_of(ids_row, table_ref[...])
    cos_ref[...] = factors
    bias_ref[...] = bias
    write_ids(ids_row, out_ref, size)

    def write(start, values):
        out_ref[:size, start : start + PAIR] = values.astype(BF16)

    layer(
        x_ref[...].astype(F32), gain_ref[...], (wq_ref, wk_ref, wv_ref, wo_ref), wait,
        lambda: (cos_ref[:size, :], bias_ref[:size, :size]), [], [], k_ref, v_ref, mixed_ref, write,
    )
    for copy in late:
        copy.wait()


def chunk_kernel(index, last, x_ref, gain_ref, wq_ref, wk_ref, wv_ref, wo_ref, *refs):
    refs = list(refs)
    mixed_ref = refs.pop(-1)
    size = mixed_ref.shape[0]
    low, high = index * size, (index + 1) * size
    if index == 0:
        table_ref = refs.pop(0)
        out_ref, k_ref, v_ref, cos_ref, bias_ref = refs
        if not last:
            out_ref[size:, :] = x_ref[size:, :]
        keys, values = [], []
    else:
        cos_ref, bias_ref = refs[:2]
        keys, values, refs = refs[2 : 2 + index], refs[2 + index : 2 + 2 * index], refs[2 + 2 * index :]
        if last and index == CHUNKS - 1:
            done, (whole_ref, out_ref, k_ref, v_ref, sems) = refs[:index], refs[index:]
            copies = [
                pltpu.make_async_copy(done[i].at[:size], whole_ref.at[0, i * size : (i + 1) * size], sems.at[i])
                for i in range(index)
            ]
            for copy in copies:
                copy.start()
        else:
            out_ref, k_ref, v_ref = refs

    def prepare():
        if index:
            return cos_ref[low:high, :], bias_ref[low:high, :]
        factors, bias = tables_of(x_ref[size:, : CHUNKS * size].astype(F32)[:1], table_ref[...])
        cos_ref[...] = factors
        bias_ref[...] = bias
        return factors[:size], bias[:size, :size]

    def write(start, result):
        out_ref[:size, start : start + PAIR] = result.astype(BF16)

    layer(
        x_ref[:size, :].astype(F32), gain_ref[...], (wq_ref, wk_ref, wv_ref, wo_ref), lambda name, start: None,
        prepare, keys, values, k_ref, v_ref, mixed_ref, write,
    )
    if last and index == CHUNKS - 1:
        copy = pltpu.make_async_copy(out_ref, whole_ref.at[0, low:high], sems.at[index])
        copy.start()
        for each in copies + [copy]:
            each.wait()


VMEM = pl.BlockSpec(memory_space=pltpu.VMEM)
HBM = pl.BlockSpec(memory_space=pltpu.HBM)


def kept(shape, dtype):
    return pltpu.VMEM(shape, dtype)


def held(array):
    return pltpu.with_memory_space_constraint(array, pltpu.VMEM)


def left(array):
    return pltpu.with_memory_space_constraint(array, pltpu.HBM)


def passed_along(array, by):
    length = lax.axis_size("section")
    return lax.ppermute(array, "section", [(i, (i + by) % length) for i in range(length)])


def body(micro, segment, gain, w_query, w_key, w_value, w_out):
    length, model = micro.shape[1], micro.shape[2]
    size = length // CHUNKS
    limits = pltpu.CompilerParams(vmem_limit_bytes=32 * 1024 * 1024)
    table = jnp.asarray(rope_table())
    rows = [size + EXTRA] + [size] * (CHUNKS - 1)
    key_values = [kept((size, KV_WIDTH), BF16)] * 2
    tables = [kept((length, PAIR), F32), kept((length, HD), F32)]
    mixing = pltpu.VMEM((size, Q_WIDTH), BF16)

    got = pl.pallas_call(
        functools.partial(opening_kernel, size),
        out_shape=(
            kept((rows[0], model), BF16),
            *key_values,
            *tables,
            kept((model, Q_WIDTH), BF16),
            kept((model, KV_WIDTH), BF16),
            kept((model, KV_WIDTH), BF16),
            kept((Q_WIDTH, model), BF16),
            kept((1, model), F32),
            kept(table.shape, BF16),
            *[kept((size, model), BF16)] * (CHUNKS - 1),
        ),
        in_specs=[HBM] * 8,
        out_specs=(VMEM,) * (10 + CHUNKS),
        scratch_shapes=[
            pltpu.VMEM((size, model), BF16),
            pltpu.VMEM(segment.shape, jnp.int32),
            pltpu.VMEM(gain.shape, BF16),
            pltpu.VMEM(table.shape, F32),
            mixing,
            pltpu.SemaphoreType.DMA((3 + CHUNKS,)),
            pltpu.SemaphoreType.DMA((12,)),
        ],
        compiler_params=limits,
        name="opening",
    )(*(left(array) for array in (micro, segment, gain, table, w_query, w_key, w_value, w_out)))
    out, k_rows, v_rows, cosines, bias = got[:5]
    weights = (got[9], *got[5:9])
    table = got[10]
    streams = [out, *got[11:]]

    for tick_index in range(TICKS):
        last = tick_index == TICKS - 1
        outs, keys, values = [], [], []
        for index in range(CHUNKS):
            if tick_index == 0 and index == 0:
                outs.append(passed_along(streams[0], 1))
                keys.append(k_rows)
                values.append(v_rows)
                continue
            args = [streams[index], *weights]
            shapes = [kept((rows[index], model), BF16), *key_values]
            scratch = [mixing]
            if index == 0:
                args.append(table)
                shapes += tables
            else:
                args += [cosines, bias, *keys, *values]
            specs = [VMEM] * len(shapes)
            ending = last and index == CHUNKS - 1
            if ending:
                args += outs
                shapes = [jax.ShapeDtypeStruct((1, length, model), BF16)]
                specs = [pl.BlockSpec(memory_space=pl.ANY)]
                scratch = [
                    pltpu.VMEM((size, model), BF16), *[pltpu.VMEM((size, KV_WIDTH), BF16)] * 2,
                    pltpu.SemaphoreType.DMA((CHUNKS,)), mixing,
                ]
            got = pl.pallas_call(
                functools.partial(chunk_kernel, index, last),
                out_shape=tuple(shapes), in_specs=[VMEM] * len(args), out_specs=tuple(specs),
                scratch_shapes=scratch, compiler_params=limits, name="chunk_%d_%d" % (tick_index, index),
            )(*map(held, args))
            if ending:
                return got[0]
            if index == 0:
                cosines, bias = got[3:]
            keys.append(got[1])
            values.append(got[2])
            outs.append(got[0] if last else passed_along(got[0], 1))
        streams = outs


def solution(mesh):
    in_specs = (
        P(("groups", "section"), None, None),
        P(("groups", "section"), None),
        P("section", None),
        P("section", None, None),
        P("section", None, None),
        P("section", None, None),
        P("section", None, None),
    )
    out_specs = P(("groups", "section"), None, None)
    return jax.shard_map(body, mesh=mesh, in_specs=in_specs, out_specs=out_specs, check_vma=False)
```

```python
import functools

import jax
import jax.numpy as jnp
import numpy as np
from jax import lax
from jax.experimental import pallas as pl
from jax.experimental.pallas import tpu as pltpu
from jax.sharding import PartitionSpec as P

HEADS = 16
KV_HEADS = 8
HD = 128
TICKS = 4
MAX_LEN = 96
CHUNKS = 2
EXTRA = 16
LIFT = 16.0
HIDDEN = -1e30
PAIR = 2 * HD
Q_WIDTH = HEADS * HD
KV_WIDTH = KV_HEADS * HD
BF16 = jnp.bfloat16
F32 = jnp.float32


def rope_table():
    middle = HD // 2
    spacing = 1000000.0 ** (-2.0 * np.arange(middle) / HD)
    angles = np.arange(MAX_LEN)[:, None] * spacing[None, :]
    cosine, sine = np.cos(angles), np.sin(angles)
    whole = np.concatenate([cosine, cosine, -sine, sine], axis=1).astype(np.float32)
    high = whole.astype(jnp.bfloat16).astype(np.float32)
    low = (whole - high).astype(jnp.bfloat16).astype(np.float32)
    return np.concatenate([high, low], axis=0)


def lower_triangle(rows, columns):
    row_index = lax.broadcasted_iota(jnp.int32, (rows, columns), 0)
    return lax.broadcasted_iota(jnp.int32, (rows, columns), 1) <= row_index


def tables_of(ids_row, table):
    length = ids_row.shape[1]
    across = jnp.broadcast_to(ids_row, (length, length))
    down = across.T
    row_index = lax.broadcasted_iota(jnp.int32, (length, length), 0)
    column = lax.broadcasted_iota(jnp.int32, (length, length), 1)
    matched = across == down
    places = jnp.sum(jnp.where(matched & (column < row_index), 1.0, 0.0), axis=1, keepdims=True)
    bias = jnp.where(matched & (column <= row_index), 0.0, HIDDEN)
    own, earlier_keys = bias[MAX_LEN:, MAX_LEN:], bias[MAX_LEN:, :MAX_LEN]
    merged = jnp.where(lower_triangle(MAX_LEN, MAX_LEN), own, earlier_keys)
    merged = jnp.concatenate([merged, jnp.full((length - MAX_LEN, HD - MAX_LEN), HIDDEN, F32)], axis=1)
    bias = jnp.concatenate([bias[:MAX_LEN, :HD], merged], axis=0)
    slots = lax.broadcasted_iota(jnp.int32, (length, 2 * MAX_LEN), 1)
    slots = jnp.where(slots >= MAX_LEN, slots - MAX_LEN, slots).astype(F32)
    one_hot = jnp.where(slots == places, 1.0, 0.0).astype(BF16)
    factors = jnp.dot(one_hot, table, preferred_element_type=F32)
    return factors, bias


def rotated(values, cosine, sine):
    return values * cosine + pltpu.roll(values, HD // 2, 1) * sine


def layer(x, gain, weights, wait, prepare, kept_keys, kept_values, k_ref, v_ref, mixed_ref, write):
    size, model = x.shape
    wq_ref, wk_ref, wv_ref, wo_ref = weights
    scale = lax.rsqrt(jnp.mean(x * x, axis=1, keepdims=True) + 1e-05) * (1.0 / LIFT)
    lifted = (x * gain).astype(BF16)
    for start in range(0, KV_WIDTH, PAIR):
        wait("v", start)
        got = jnp.dot(lifted, wv_ref[:, start : start + PAIR], preferred_element_type=F32)
        v_ref[:, start : start + PAIR] = (got * scale).astype(BF16)
    cos_rows, bias_rows = prepare()
    cosine = cos_rows[:, :HD] * scale
    sine = cos_rows[:, HD:] * scale
    factor = HD ** (-0.5) * np.log2(np.e)
    cosine_q = cosine * factor
    sine_q = sine * factor
    for start in range(0, KV_WIDTH, PAIR):
        wait("k", start)
        got = jnp.dot(lifted, wk_ref[:, start : start + PAIR], preferred_element_type=F32)
        for half in range(0, PAIR, HD):
            turned = rotated(got[:, half : half + HD], cosine, sine)
            k_ref[:, start + half : start + half + HD] = turned.astype(BF16)
    spare = jnp.zeros((HD - size, HD), BF16)
    lower = lower_triangle(size, HD)
    lower_share = jnp.where(lower, 1.0, 0.0).astype(BF16)
    key_refs, value_refs = [k_ref, *kept_keys], [v_ref, *kept_values]

    def rows_of(refs, group):
        lanes = slice(group * HD, (group + 1) * HD)
        if len(refs) == 1:
            return refs[0][:, lanes]
        return jnp.concatenate([part for ref in refs for part in (ref[:, lanes], spare)], axis=0)

    def query(group):
        lanes = slice(group * PAIR, (group + 1) * PAIR)
        wait("q", group)
        got = jnp.dot(lifted, wq_ref[:, lanes], preferred_element_type=F32)
        turned = [rotated(got[:, half : half + HD], cosine_q, sine_q) for half in range(0, PAIR, HD)]
        return jnp.concatenate(turned, axis=0).astype(BF16)

    def score(group, queries):
        key_rows = rows_of(key_refs, group)
        got = lax.dot_general(queries, key_rows, (((1,), (1,)), ((), ())), preferred_element_type=F32)
        got = got.reshape(2, size, key_rows.shape[0])
        if kept_keys:
            got = jnp.where(lower[None], got[:, :, :HD], got[:, :, HD:])
        return got + bias_rows[None]

    def exponents(scores):
        most = [jnp.max(part, axis=2, keepdims=True) for part in scores]
        expo = [jnp.exp2(part - peak).astype(BF16) for part, peak in zip(scores, most)]
        if kept_keys:
            own = [part * lower_share[None] for part in expo]
            expo = [jnp.concatenate([mine, part - mine], axis=2) for mine, part in zip(own, expo)]
        return expo

    def mix(groups, expo):
        got = []
        for group, part in zip(groups, expo):
            value_rows = rows_of(value_refs, group)
            value_rows = jnp.concatenate([value_rows, jnp.ones((value_rows.shape[0], HD), BF16)], axis=1)
            part = part.reshape(2 * size, value_rows.shape[0])
            got.append(jnp.dot(part, value_rows, preferred_element_type=F32))
        for group, part in zip(groups, got):
            total = part[:, HD:]
            inverse = pl.reciprocal(total, approx=True)
            inverse = inverse * (2.0 - total * inverse)
            mixed = (part[:, :HD] * inverse).astype(BF16)
            mixed_ref[:, group * PAIR : group * PAIR + HD] = mixed[:size]
            mixed_ref[:, group * PAIR + HD : (group + 1) * PAIR] = mixed[size:]

    def products(half):
        rows = slice(half * Q_WIDTH // 2, (half + 1) * Q_WIDTH // 2)
        wait("o", half)
        return [
            jnp.dot(mixed_ref[:, rows], wo_ref[rows, start : start + PAIR], preferred_element_type=F32)
            for start in range(0, model, PAIR)
        ]

    early, late = range(KV_HEADS // 2), range(KV_HEADS // 2, KV_HEADS)
    queries = [query(group) for group in early]
    scores = [score(group, part) for group, part in zip(early, queries)]
    queries = [query(group) for group in late]
    expo = exponents(scores)
    scores = [score(group, part) for group, part in zip(late, queries)]
    mix(early, expo)
    updates = products(0)
    expo = exponents(scores)
    mix(late, expo)
    for start, first, second in zip(range(0, model, PAIR), updates, products(1)):
        write(start, x[:, start : start + PAIR] + (first + second))


def write_ids(ids_row, out_ref, size):
    length = ids_row.shape[1]
    out_ref[size:, :] = jnp.zeros((EXTRA, out_ref.shape[1]), BF16)
    out_ref[size:, :length] = jnp.broadcast_to(ids_row, (EXTRA, length)).astype(BF16)


def opening_kernel(
    size, x_hbm, ids_hbm, gain_hbm, table_hbm, wq_hbm, wk_hbm, wv_hbm, wo_hbm,
    out_ref, k_ref, v_ref, cos_ref, bias_ref, wq_ref, wk_ref, wv_ref, wo_ref, gain_ref, table_ref, *refs,
):
    rest_refs, refs = refs[: CHUNKS - 1], refs[CHUNKS - 1 :]
    x_ref, ids_ref, raw_gain, raw_table, mixed_ref, small_sems, sems = refs
    small = [
        pltpu.make_async_copy(ids_hbm, ids_ref, small_sems.at[0]),
        pltpu.make_async_copy(table_hbm, raw_table, small_sems.at[1]),
        pltpu.make_async_copy(gain_hbm, raw_gain, small_sems.at[2]),
        pltpu.make_async_copy(x_hbm.at[0, :size], x_ref, small_sems.at[3]),
    ]
    late = [
        pltpu.make_async_copy(x_hbm.at[0, (i + 1) * size : (i + 2) * size], rest_refs[i], small_sems.at[4 + i])
        for i in range(CHUNKS - 1)
    ]
    made = []

    def batch(source, target, rows, lanes):
        step = (rows.stop - rows.start) // 2
        copies = []
        for low in range(rows.start, rows.stop, step):
            part = (slice(low, low + step), lanes)
            copies.append(pltpu.make_async_copy(source.at[(0, *part)], target.at[part], sems.at[len(made)]))
            made.append(copies[-1])
        return copies

    model, half = wk_ref.shape[0], Q_WIDTH // 2
    narrow, wide = slice(0, KV_WIDTH), slice(0, Q_WIDTH)
    batches = [
        batch(wv_hbm, wv_ref, slice(0, model), narrow),
        batch(wk_hbm, wk_ref, slice(0, model), narrow),
        batch(wq_hbm, wq_ref, slice(0, model // 2), wide),
        batch(wq_hbm, wq_ref, slice(model // 2, model), wide),
        batch(wo_hbm, wo_ref, slice(0, half), slice(0, model)),
        batch(wo_hbm, wo_ref, slice(half, Q_WIDTH), slice(0, model)),
    ]
    arrivals = {("v", 0): (0,), ("k", 0): (1,), ("q", 0): (2, 3), ("o", 0): (4,), ("o", 1): (5,)}

    def begin(index):
        if index < len(batches):
            for place, copy in enumerate(batches[index]):
                copy.start(priority=place % 2)
        if index == len(batches):
            for copy in late:
                copy.start()

    def wait(name, start):
        for index in arrivals.get((name, start), ()):
            for copy in batches[index]:
                copy.wait()
            begin(index + 6)

    for copy in small:
        copy.start()
    for index in range(6):
        begin(index)
    for copy in small:
        copy.wait()
    gain_ref[...] = raw_gain[...].astype(F32) * LIFT
    table_ref[...] = raw_table[...].astype(BF16)
    ids_row = ids_ref[...].astype(F32)
    factors, bias = tables_of(ids_row, table_ref[...])
    cos_ref[...] = factors
    bias_ref[...] = bias
    write_ids(ids_row, out_ref, size)

    def write(start, values):
        out_ref[:size, start : start + PAIR] = values.astype(BF16)

    layer(
        x_ref[...].astype(F32), gain_ref[...], (wq_ref, wk_ref, wv_ref, wo_ref), wait,
        lambda: (cos_ref[:size, :], bias_ref[:size, :size]), [], [], k_ref, v_ref, mixed_ref, write,
    )
    for copy in late:
        copy.wait()


def chunk_kernel(index, last, x_ref, gain_ref, wq_ref, wk_ref, wv_ref, wo_ref, *refs):
    refs = list(refs)
    mixed_ref = refs.pop(-1)
    size = mixed_ref.shape[0]
    low, high = index * size, (index + 1) * size
    if index == 0:
        table_ref = refs.pop(0)
        out_ref, k_ref, v_ref, cos_ref, bias_ref = refs
        if not last:
            out_ref[size:, :] = x_ref[size:, :]
        keys, values = [], []
    else:
        cos_ref, bias_ref = refs[:2]
        keys, values, refs = refs[2 : 2 + index], refs[2 + index : 2 + 2 * index], refs[2 + 2 * index :]
        if last and index == CHUNKS - 1:
            done, (whole_ref, out_ref, k_ref, v_ref, sems) = refs[:index], refs[index:]
            copies = [
                pltpu.make_async_copy(done[i].at[:size], whole_ref.at[0, i * size : (i + 1) * size], sems.at[i])
                for i in range(index)
            ]
            for copy in copies:
                copy.start()
        else:
            out_ref, k_ref, v_ref = refs

    def prepare():
        if index:
            return cos_ref[low:high, :], bias_ref[low:high, :]
        factors, bias = tables_of(x_ref[size:, : CHUNKS * size].astype(F32)[:1], table_ref[...])
        cos_ref[...] = factors
        bias_ref[...] = bias
        return factors[:size], bias[:size, :size]

    def write(start, result):
        out_ref[:size, start : start + PAIR] = result.astype(BF16)

    layer(
        x_ref[:size, :].astype(F32), gain_ref[...], (wq_ref, wk_ref, wv_ref, wo_ref), lambda name, start: None,
        prepare, keys, values, k_ref, v_ref, mixed_ref, write,
    )
    if last and index == CHUNKS - 1:
        copy = pltpu.make_async_copy(out_ref, whole_ref.at[0, low:high], sems.at[index])
        copy.start()
        for each in copies + [copy]:
            each.wait()


VMEM = pl.BlockSpec(memory_space=pltpu.VMEM)
HBM = pl.BlockSpec(memory_space=pltpu.HBM)


def kept(shape, dtype):
    return pltpu.VMEM(shape, dtype)


def held(array):
    return pltpu.with_memory_space_constraint(array, pltpu.VMEM)


def left(array):
    return pltpu.with_memory_space_constraint(array, pltpu.HBM)


def passed_along(array, by):
    length = lax.axis_size("section")
    return lax.ppermute(array, "section", [(i, (i + by) % length) for i in range(length)])


def body(micro, segment, gain, w_query, w_key, w_value, w_out):
    length, model = micro.shape[1], micro.shape[2]
    size = length // CHUNKS
    limits = pltpu.CompilerParams(vmem_limit_bytes=32 * 1024 * 1024)
    table = jnp.asarray(rope_table())
    rows = [size + EXTRA] + [size] * (CHUNKS - 1)
    key_values = [kept((size, KV_WIDTH), BF16)] * 2
    tables = [kept((length, PAIR), F32), kept((length, HD), F32)]
    mixing = pltpu.VMEM((size, Q_WIDTH), BF16)

    got = pl.pallas_call(
        functools.partial(opening_kernel, size),
        out_shape=(
            kept((rows[0], model), BF16),
            *key_values,
            *tables,
            kept((model, Q_WIDTH), BF16),
            kept((model, KV_WIDTH), BF16),
            kept((model, KV_WIDTH), BF16),
            kept((Q_WIDTH, model), BF16),
            kept((1, model), F32),
            kept(table.shape, BF16),
            *[kept((size, model), BF16)] * (CHUNKS - 1),
        ),
        in_specs=[HBM] * 8,
        out_specs=(VMEM,) * (10 + CHUNKS),
        scratch_shapes=[
            pltpu.VMEM((size, model), BF16),
            pltpu.VMEM(segment.shape, jnp.int32),
            pltpu.VMEM(gain.shape, BF16),
            pltpu.VMEM(table.shape, F32),
            mixing,
            pltpu.SemaphoreType.DMA((3 + CHUNKS,)),
            pltpu.SemaphoreType.DMA((12,)),
        ],
        compiler_params=limits,
        name="opening",
    )(*(left(array) for array in (micro, segment, gain, table, w_query, w_key, w_value, w_out)))
    out, k_rows, v_rows, cosines, bias = got[:5]
    weights = (got[9], *got[5:9])
    table = got[10]
    streams = [out, *got[11:]]

    for tick_index in range(TICKS):
        last = tick_index == TICKS - 1
        outs, keys, values = [], [], []
        for index in range(CHUNKS):
            if tick_index == 0 and index == 0:
                outs.append(passed_along(streams[0], 1))
                keys.append(k_rows)
                values.append(v_rows)
                continue
            args = [streams[index], *weights]
            shapes = [kept((rows[index], model), BF16), *key_values]
            scratch = [mixing]
            if index == 0:
                args.append(table)
                shapes += tables
            else:
                args += [cosines, bias, *keys, *values]
            specs = [VMEM] * len(shapes)
            ending = last and index == CHUNKS - 1
            if ending:
                args += outs
                shapes = [jax.ShapeDtypeStruct((1, length, model), BF16)]
                specs = [pl.BlockSpec(memory_space=pl.ANY)]
                scratch = [
                    pltpu.VMEM((size, model), BF16), *[pltpu.VMEM((size, KV_WIDTH), BF16)] * 2,
                    pltpu.SemaphoreType.DMA((CHUNKS,)), mixing,
                ]
            got = pl.pallas_call(
                functools.partial(chunk_kernel, index, last),
                out_shape=tuple(shapes), in_specs=[VMEM] * len(args), out_specs=tuple(specs),
                scratch_shapes=scratch, compiler_params=limits, name="chunk_%d_%d" % (tick_index, index),
            )(*map(held, args))
            if ending:
                return got[0]
            if index == 0:
                cosines, bias = got[3:]
            keys.append(got[1])
            values.append(got[2])
            outs.append(got[0] if last else passed_along(got[0], 1))
        streams = outs


def solution(mesh):
    in_specs = (
        P(("groups", "section"), None, None),
        P(("groups", "section"), None),
        P("section", None),
        P("section", None, None),
        P("section", None, None),
        P("section", None, None),
        P("section", None, None),
    )
    out_specs = P(("groups", "section"), None, None)
    return jax.shard_map(body, mesh=mesh, in_specs=in_specs, out_specs=out_specs, check_vma=False)
```

```python
import functools

import jax
import jax.numpy as jnp
import numpy as np
from jax import lax
from jax.experimental import pallas as pl
from jax.experimental.pallas import tpu as pltpu
from jax.sharding import PartitionSpec as P

HEADS = 16
KV_HEADS = 8
HD = 128
TICKS = 4
MAX_LEN = 96
CHUNKS = 2
EXTRA = 16
LIFT = 16.0
HIDDEN = -1e30
PAIR = 2 * HD
Q_WIDTH = HEADS * HD
KV_WIDTH = KV_HEADS * HD
BF16 = jnp.bfloat16
F32 = jnp.float32


def rope_table():
    middle = HD // 2
    spacing = 1000000.0 ** (-2.0 * np.arange(middle) / HD)
    angles = np.arange(MAX_LEN)[:, None] * spacing[None, :]
    cosine, sine = np.cos(angles), np.sin(angles)
    whole = np.concatenate([cosine, cosine, -sine, sine], axis=1).astype(np.float32)
    high = whole.astype(jnp.bfloat16).astype(np.float32)
    low = (whole - high).astype(jnp.bfloat16).astype(np.float32)
    return np.concatenate([high, low], axis=0)


def lower_triangle(rows, columns):
    row_index = lax.broadcasted_iota(jnp.int32, (rows, columns), 0)
    return lax.broadcasted_iota(jnp.int32, (rows, columns), 1) <= row_index


def tables_of(ids_row, table):
    length = ids_row.shape[1]
    across = jnp.broadcast_to(ids_row, (length, length))
    down = across.T
    row_index = lax.broadcasted_iota(jnp.int32, (length, length), 0)
    column = lax.broadcasted_iota(jnp.int32, (length, length), 1)
    matched = across == down
    places = jnp.sum(jnp.where(matched & (column < row_index), 1.0, 0.0), axis=1, keepdims=True)
    bias = jnp.where(matched & (column <= row_index), 0.0, HIDDEN)
    own, earlier_keys = bias[MAX_LEN:, MAX_LEN:], bias[MAX_LEN:, :MAX_LEN]
    merged = jnp.where(lower_triangle(MAX_LEN, MAX_LEN), own, earlier_keys)
    merged = jnp.concatenate([merged, jnp.full((length - MAX_LEN, HD - MAX_LEN), HIDDEN, F32)], axis=1)
    bias = jnp.concatenate([bias[:MAX_LEN, :HD], merged], axis=0)
    slots = lax.broadcasted_iota(jnp.int32, (length, 2 * MAX_LEN), 1)
    slots = jnp.where(slots >= MAX_LEN, slots - MAX_LEN, slots).astype(F32)
    one_hot = jnp.where(slots == places, 1.0, 0.0).astype(BF16)
    factors = jnp.dot(one_hot, table, preferred_element_type=F32)
    return factors, bias


def rotated(values, cosine, sine):
    return values * cosine + pltpu.roll(values, HD // 2, 1) * sine


def layer(halves, x, gain, weights, wait, prepare, kept_keys, kept_values, k_ref, v_ref, mixed_ref, write):
    size, model = x.shape
    wq_ref, wk_ref, wv_ref, wo_ref = weights
    scale = lax.rsqrt(jnp.mean(x * x, axis=1, keepdims=True) + 1e-05) * (1.0 / LIFT)
    lifted = (x * gain).astype(BF16)
    for start in range(0, KV_WIDTH, PAIR):
        wait("v", start)
        got = jnp.dot(lifted, wv_ref[:, start : start + PAIR], preferred_element_type=F32)
        v_ref[:, start : start + PAIR] = (got * scale).astype(BF16)
    cos_rows, bias_rows = prepare()
    cosine = cos_rows[:, :HD] * scale
    sine = cos_rows[:, HD:] * scale
    factor = HD ** (-0.5) * np.log2(np.e)
    cosine_q = cosine * factor
    sine_q = sine * factor
    for start in range(0, KV_WIDTH, PAIR):
        wait("k", start)
        got = jnp.dot(lifted, wk_ref[:, start : start + PAIR], preferred_element_type=F32)
        for half in range(0, PAIR, HD):
            turned = rotated(got[:, half : half + HD], cosine, sine)
            k_ref[:, start + half : start + half + HD] = turned.astype(BF16)
    spare = jnp.zeros((HD - size, HD), BF16)
    lower = lower_triangle(size, HD)
    lower_share = jnp.where(lower, 1.0, 0.0).astype(BF16)
    key_refs, value_refs = [k_ref, *kept_keys], [v_ref, *kept_values]

    def rows_of(refs, group):
        lanes = slice(group * HD, (group + 1) * HD)
        if len(refs) == 1:
            return refs[0][:, lanes]
        return jnp.concatenate([part for ref in refs for part in (ref[:, lanes], spare)], axis=0)

    def query(group):
        lanes = slice(group * PAIR, (group + 1) * PAIR)
        wait("q", group)
        got = jnp.dot(lifted, wq_ref[:, lanes], preferred_element_type=F32)
        turned = [rotated(got[:, half : half + HD], cosine_q, sine_q) for half in range(0, PAIR, HD)]
        return jnp.concatenate(turned, axis=0).astype(BF16)

    def score(group, queries):
        key_rows = rows_of(key_refs, group)
        got = lax.dot_general(queries, key_rows, (((1,), (1,)), ((), ())), preferred_element_type=F32)
        got = got.reshape(2, size, key_rows.shape[0])
        if kept_keys:
            got = jnp.where(lower[None], got[:, :, :HD], got[:, :, HD:])
        return got + bias_rows[None]

    def exponents(scores):
        most = [jnp.max(part, axis=2, keepdims=True) for part in scores]
        expo = [jnp.exp2(part - peak).astype(BF16) for part, peak in zip(scores, most)]
        if kept_keys:
            own = [part * lower_share[None] for part in expo]
            expo = [jnp.concatenate([mine, part - mine], axis=2) for mine, part in zip(own, expo)]
        return expo

    def mix(groups, expo):
        got = []
        for group, part in zip(groups, expo):
            value_rows = rows_of(value_refs, group)
            value_rows = jnp.concatenate([value_rows, jnp.ones((value_rows.shape[0], HD), BF16)], axis=1)
            part = part.reshape(2 * size, value_rows.shape[0])
            got.append(jnp.dot(part, value_rows, preferred_element_type=F32))
        for group, part in zip(groups, got):
            total = part[:, HD:]
            inverse = pl.reciprocal(total, approx=True)
            inverse = inverse * (2.0 - total * inverse)
            mixed = (part[:, :HD] * inverse).astype(BF16)
            mixed_ref[:, group * PAIR : group * PAIR + HD] = mixed[:size]
            mixed_ref[:, group * PAIR + HD : (group + 1) * PAIR] = mixed[size:]

    def products(half):
        rows = slice(half * Q_WIDTH // 2, (half + 1) * Q_WIDTH // 2)
        return [
            jnp.dot(mixed_ref[:, rows], wo_ref[rows, start : start + PAIR], preferred_element_type=F32)
            for start in range(0, model, PAIR)
        ]

    groups = range(KV_HEADS)
    if not halves:
        queries = [query(group) for group in groups]
        expo = exponents([score(group, part) for group, part in zip(groups, queries)])
        mix(groups, expo)
        for start in range(0, model, PAIR):
            wait("o", start)
            update = jnp.dot(mixed_ref[...], wo_ref[:, start : start + PAIR], preferred_element_type=F32)
            write(start, x[:, start : start + PAIR] + update)
        return
    early, late = groups[: KV_HEADS // 2], groups[KV_HEADS // 2 :]
    queries = [query(group) for group in early]
    scores = [score(group, part) for group, part in zip(early, queries)]
    queries = [query(group) for group in late]
    expo = exponents(scores)
    scores = [score(group, part) for group, part in zip(late, queries)]
    mix(early, expo)
    updates = products(0)
    expo = exponents(scores)
    mix(late, expo)
    for start, first, second in zip(range(0, model, PAIR), updates, products(1)):
        write(start, x[:, start : start + PAIR] + (first + second))


def write_ids(ids_row, out_ref, size):
    length = ids_row.shape[1]
    out_ref[size:, :] = jnp.zeros((EXTRA, out_ref.shape[1]), BF16)
    out_ref[size:, :length] = jnp.broadcast_to(ids_row, (EXTRA, length)).astype(BF16)


def opening_kernel(
    size, x_hbm, ids_hbm, gain_hbm, table_hbm, wq_hbm, wk_hbm, wv_hbm, wo_hbm,
    out_ref, k_ref, v_ref, cos_ref, bias_ref, wq_ref, wk_ref, wv_ref, wo_ref, gain_ref, table_ref, *refs,
):
    rest_refs, refs = refs[: CHUNKS - 1], refs[CHUNKS - 1 :]
    x_ref, ids_ref, raw_gain, raw_table, mixed_ref, small_sems, sems = refs
    small = [
        pltpu.make_async_copy(ids_hbm, ids_ref, small_sems.at[0]),
        pltpu.make_async_copy(table_hbm, raw_table, small_sems.at[1]),
        pltpu.make_async_copy(gain_hbm, raw_gain, small_sems.at[2]),
        pltpu.make_async_copy(x_hbm.at[0, :size], x_ref, small_sems.at[3]),
    ]
    late = [
        pltpu.make_async_copy(x_hbm.at[0, (i + 1) * size : (i + 2) * size], rest_refs[i], small_sems.at[4 + i])
        for i in range(CHUNKS - 1)
    ]
    made = []

    def batch(source, target, rows, lanes):
        step = (rows.stop - rows.start) // 2
        copies = []
        for low in range(rows.start, rows.stop, step):
            part = (slice(low, low + step), lanes)
            copies.append(pltpu.make_async_copy(source.at[(0, *part)], target.at[part], sems.at[len(made)]))
            made.append(copies[-1])
        return copies

    model, half = wk_ref.shape[0], Q_WIDTH // 2
    narrow = slice(0, KV_WIDTH)
    batches = [
        batch(wv_hbm, wv_ref, slice(0, model), narrow),
        batch(wk_hbm, wk_ref, slice(0, model), narrow),
        batch(wq_hbm, wq_ref, slice(0, model), slice(0, half)),
        batch(wq_hbm, wq_ref, slice(0, model), slice(half, Q_WIDTH)),
        batch(wo_hbm, wo_ref, slice(0, half), slice(0, model)),
        batch(wo_hbm, wo_ref, slice(half, Q_WIDTH), slice(0, model)),
    ]
    arrivals = {("v", 0): (0,), ("k", 0): (1,), ("q", 0): (2,), ("q", KV_HEADS // 2): (3,), ("o", 0): (4, 5)}

    def begin(index):
        for place, copy in enumerate(batches[index]):
            copy.start(priority=place % 2)

    def wait(name, place):
        for index in arrivals.get((name, place), ()):
            for copy in batches[index]:
                copy.wait()
            if index in (1, 2):
                begin(index + 3)
            if index == 3:
                for copy in late:
                    copy.start()

    for copy in small:
        copy.start()
    for index in range(4):
        begin(index)
    for copy in small:
        copy.wait()
    gain_ref[...] = raw_gain[...].astype(F32) * LIFT
    table_ref[...] = raw_table[...].astype(BF16)
    ids_row = ids_ref[...].astype(F32)
    factors, bias = tables_of(ids_row, table_ref[...])
    cos_ref[...] = factors
    bias_ref[...] = bias
    write_ids(ids_row, out_ref, size)

    def write(start, values):
        out_ref[:size, start : start + PAIR] = values.astype(BF16)

    layer(
        False, x_ref[...].astype(F32), gain_ref[...], (wq_ref, wk_ref, wv_ref, wo_ref), wait,
        lambda: (cos_ref[:size, :], bias_ref[:size, :size]), [], [], k_ref, v_ref, mixed_ref, write,
    )
    for copy in late:
        copy.wait()


def chunk_kernel(index, last, x_ref, gain_ref, wq_ref, wk_ref, wv_ref, wo_ref, *refs):
    refs = list(refs)
    mixed_ref = refs.pop(-1)
    size = mixed_ref.shape[0]
    low, high = index * size, (index + 1) * size
    if index == 0:
        table_ref = refs.pop(0)
        out_ref, k_ref, v_ref, cos_ref, bias_ref = refs
        if not last:
            out_ref[size:, :] = x_ref[size:, :]
        keys, values = [], []
    else:
        cos_ref, bias_ref = refs[:2]
        keys, values, refs = refs[2 : 2 + index], refs[2 + index : 2 + 2 * index], refs[2 + 2 * index :]
        if last and index == CHUNKS - 1:
            done, (whole_ref, out_ref, k_ref, v_ref, sems) = refs[:index], refs[index:]
            copies = [
                pltpu.make_async_copy(done[i].at[:size], whole_ref.at[0, i * size : (i + 1) * size], sems.at[i])
                for i in range(index)
            ]
            for copy in copies:
                copy.start()
        else:
            out_ref, k_ref, v_ref = refs

    def prepare():
        if index:
            return cos_ref[low:high, :], bias_ref[low:high, :]
        factors, bias = tables_of(x_ref[size:, : CHUNKS * size].astype(F32)[:1], table_ref[...])
        cos_ref[...] = factors
        bias_ref[...] = bias
        return factors[:size], bias[:size, :size]

    def write(start, result):
        out_ref[:size, start : start + PAIR] = result.astype(BF16)

    layer(
        index > 0 and not last, x_ref[:size, :].astype(F32), gain_ref[...], (wq_ref, wk_ref, wv_ref, wo_ref), lambda name, start: None,
        prepare, keys, values, k_ref, v_ref, mixed_ref, write,
    )
    if last and index == CHUNKS - 1:
        copy = pltpu.make_async_copy(out_ref, whole_ref.at[0, low:high], sems.at[index])
        copy.start()
        for each in copies + [copy]:
            each.wait()


VMEM = pl.BlockSpec(memory_space=pltpu.VMEM)
HBM = pl.BlockSpec(memory_space=pltpu.HBM)


def kept(shape, dtype):
    return pltpu.VMEM(shape, dtype)


def held(array):
    return pltpu.with_memory_space_constraint(array, pltpu.VMEM)


def left(array):
    return pltpu.with_memory_space_constraint(array, pltpu.HBM)


def passed_along(array, by):
    length = lax.axis_size("section")
    return lax.ppermute(array, "section", [(i, (i + by) % length) for i in range(length)])


def body(micro, segment, gain, w_query, w_key, w_value, w_out):
    length, model = micro.shape[1], micro.shape[2]
    size = length // CHUNKS
    limits = pltpu.CompilerParams(vmem_limit_bytes=32 * 1024 * 1024)
    table = jnp.asarray(rope_table())
    rows = [size + EXTRA] + [size] * (CHUNKS - 1)
    key_values = [kept((size, KV_WIDTH), BF16)] * 2
    tables = [kept((length, PAIR), F32), kept((length, HD), F32)]
    mixing = pltpu.VMEM((size, Q_WIDTH), BF16)

    got = pl.pallas_call(
        functools.partial(opening_kernel, size),
        out_shape=(
            kept((rows[0], model), BF16),
            *key_values,
            *tables,
            kept((model, Q_WIDTH), BF16),
            kept((model, KV_WIDTH), BF16),
            kept((model, KV_WIDTH), BF16),
            kept((Q_WIDTH, model), BF16),
            kept((1, model), F32),
            kept(table.shape, BF16),
            *[kept((size, model), BF16)] * (CHUNKS - 1),
        ),
        in_specs=[HBM] * 8,
        out_specs=(VMEM,) * (10 + CHUNKS),
        scratch_shapes=[
            pltpu.VMEM((size, model), BF16),
            pltpu.VMEM(segment.shape, jnp.int32),
            pltpu.VMEM(gain.shape, BF16),
            pltpu.VMEM(table.shape, F32),
            mixing,
            pltpu.SemaphoreType.DMA((3 + CHUNKS,)),
            pltpu.SemaphoreType.DMA((12,)),
        ],
        compiler_params=limits,
        name="opening",
    )(*(left(array) for array in (micro, segment, gain, table, w_query, w_key, w_value, w_out)))
    out, k_rows, v_rows, cosines, bias = got[:5]
    weights = (got[9], *got[5:9])
    table = got[10]
    streams = [out, *got[11:]]

    for tick_index in range(TICKS):
        last = tick_index == TICKS - 1
        outs, keys, values = [], [], []
        for index in range(CHUNKS):
            if tick_index == 0 and index == 0:
                outs.append(passed_along(streams[0], 1))
                keys.append(k_rows)
                values.append(v_rows)
                continue
            args = [streams[index], *weights]
            shapes = [kept((rows[index], model), BF16), *key_values]
            scratch = [mixing]
            if index == 0:
                args.append(table)
                shapes += tables
            else:
                args += [cosines, bias, *keys, *values]
            specs = [VMEM] * len(shapes)
            ending = last and index == CHUNKS - 1
            if ending:
                args += outs
                shapes = [jax.ShapeDtypeStruct((1, length, model), BF16)]
                specs = [pl.BlockSpec(memory_space=pl.ANY)]
                scratch = [
                    pltpu.VMEM((size, model), BF16), *[pltpu.VMEM((size, KV_WIDTH), BF16)] * 2,
                    pltpu.SemaphoreType.DMA((CHUNKS,)), mixing,
                ]
            got = pl.pallas_call(
                functools.partial(chunk_kernel, index, last),
                out_shape=tuple(shapes), in_specs=[VMEM] * len(args), out_specs=tuple(specs),
                scratch_shapes=scratch, compiler_params=limits, name="chunk_%d_%d" % (tick_index, index),
            )(*map(held, args))
            if ending:
                return got[0]
            if index == 0:
                cosines, bias = got[3:]
            keys.append(got[1])
            values.append(got[2])
            outs.append(got[0] if last else passed_along(got[0], 1))
        streams = outs


def solution(mesh):
    in_specs = (
        P(("groups", "section"), None, None),
        P(("groups", "section"), None),
        P("section", None),
        P("section", None, None),
        P("section", None, None),
        P("section", None, None),
        P("section", None, None),
    )
    out_specs = P(("groups", "section"), None, None)
    return jax.shard_map(body, mesh=mesh, in_specs=in_specs, out_specs=out_specs, check_vma=False)
```

```python
import functools

import jax
import jax.numpy as jnp
import numpy as np
from jax import lax
from jax.experimental import pallas as pl
from jax.experimental.pallas import tpu as pltpu
from jax.sharding import PartitionSpec as P

HEADS = 16
KV_HEADS = 8
HD = 128
TICKS = 4
MAX_LEN = 96
CHUNKS = 2
EXTRA = 16
LIFT = 16.0
HIDDEN = -1e30
PAIR = 2 * HD
Q_WIDTH = HEADS * HD
KV_WIDTH = KV_HEADS * HD
BF16 = jnp.bfloat16
F32 = jnp.float32


def rope_table():
    middle = HD // 2
    spacing = 1000000.0 ** (-2.0 * np.arange(middle) / HD)
    angles = np.arange(MAX_LEN)[:, None] * spacing[None, :]
    cosine, sine = np.cos(angles), np.sin(angles)
    whole = np.concatenate([cosine, cosine, -sine, sine], axis=1).astype(np.float32)
    high = whole.astype(jnp.bfloat16).astype(np.float32)
    low = (whole - high).astype(jnp.bfloat16).astype(np.float32)
    return np.concatenate([high, low], axis=0)


def lower_triangle(rows, columns):
    row_index = lax.broadcasted_iota(jnp.int32, (rows, columns), 0)
    return lax.broadcasted_iota(jnp.int32, (rows, columns), 1) <= row_index


def tables_of(ids_row, table):
    length = ids_row.shape[1]
    across = jnp.broadcast_to(ids_row, (length, length))
    down = across.T
    row_index = lax.broadcasted_iota(jnp.int32, (length, length), 0)
    column = lax.broadcasted_iota(jnp.int32, (length, length), 1)
    matched = across == down
    places = jnp.sum(jnp.where(matched & (column < row_index), 1.0, 0.0), axis=1, keepdims=True)
    bias = jnp.where(matched & (column <= row_index), 0.0, HIDDEN)
    own, earlier_keys = bias[MAX_LEN:, MAX_LEN:], bias[MAX_LEN:, :MAX_LEN]
    merged = jnp.where(lower_triangle(MAX_LEN, MAX_LEN), own, earlier_keys)
    merged = jnp.concatenate([merged, jnp.full((length - MAX_LEN, HD - MAX_LEN), HIDDEN, F32)], axis=1)
    bias = jnp.concatenate([bias[:MAX_LEN, :HD], merged], axis=0)
    slots = lax.broadcasted_iota(jnp.int32, (length, 2 * MAX_LEN), 1)
    slots = jnp.where(slots >= MAX_LEN, slots - MAX_LEN, slots).astype(F32)
    one_hot = jnp.where(slots == places, 1.0, 0.0).astype(BF16)
    factors = jnp.dot(one_hot, table, preferred_element_type=F32)
    return factors, bias


def rotated(values, cosine, sine):
    return values * cosine + pltpu.roll(values, HD // 2, 1) * sine


def layer(halves, x, gain, weights, wait, prepare, kept_keys, kept_values, k_ref, v_ref, mixed_ref, write):
    size, model = x.shape
    wq_ref, wk_ref, wv_ref, wo_ref = weights
    scale = lax.rsqrt(jnp.mean(x * x, axis=1, keepdims=True) + 1e-05) * (1.0 / LIFT)
    lifted = (x * gain).astype(BF16)
    for start in range(0, KV_WIDTH, PAIR):
        wait("v", start)
        got = jnp.dot(lifted, wv_ref[:, start : start + PAIR], preferred_element_type=F32)
        v_ref[:, start : start + PAIR] = (got * scale).astype(BF16)
    cos_rows, bias_rows = prepare()
    cosine = cos_rows[:, :HD] * scale
    sine = cos_rows[:, HD:] * scale
    factor = HD ** (-0.5) * np.log2(np.e)
    cosine_q = cosine * factor
    sine_q = sine * factor
    for start in range(0, KV_WIDTH, PAIR):
        wait("k", start)
        got = jnp.dot(lifted, wk_ref[:, start : start + PAIR], preferred_element_type=F32)
        for half in range(0, PAIR, HD):
            turned = rotated(got[:, half : half + HD], cosine, sine)
            k_ref[:, start + half : start + half + HD] = turned.astype(BF16)
    spare = jnp.zeros((HD - size, HD), BF16)
    lower = lower_triangle(size, HD)
    lower_share = jnp.where(lower, 1.0, 0.0).astype(BF16)
    key_refs, value_refs = [k_ref, *kept_keys], [v_ref, *kept_values]

    def rows_of(refs, group):
        lanes = slice(group * HD, (group + 1) * HD)
        if len(refs) == 1:
            return refs[0][:, lanes]
        return jnp.concatenate([part for ref in refs for part in (ref[:, lanes], spare)], axis=0)

    def query(group):
        lanes = slice(group * PAIR, (group + 1) * PAIR)
        wait("q", group)
        got = jnp.dot(lifted, wq_ref[:, lanes], preferred_element_type=F32)
        turned = [rotated(got[:, half : half + HD], cosine_q, sine_q) for half in range(0, PAIR, HD)]
        return jnp.concatenate(turned, axis=0).astype(BF16)

    def score(group, queries):
        key_rows = rows_of(key_refs, group)
        got = lax.dot_general(queries, key_rows, (((1,), (1,)), ((), ())), preferred_element_type=F32)
        got = got.reshape(2, size, key_rows.shape[0])
        if kept_keys:
            got = jnp.where(lower[None], got[:, :, :HD], got[:, :, HD:])
        return got + bias_rows[None]

    def exponents(scores):
        most = [jnp.max(part, axis=2, keepdims=True) for part in scores]
        expo = [jnp.exp2(part - peak).astype(BF16) for part, peak in zip(scores, most)]
        if kept_keys:
            own = [part * lower_share[None] for part in expo]
            expo = [jnp.concatenate([mine, part - mine], axis=2) for mine, part in zip(own, expo)]
        return expo

    def mix(groups, expo):
        got = []
        for group, part in zip(groups, expo):
            value_rows = rows_of(value_refs, group)
            value_rows = jnp.concatenate([value_rows, jnp.ones((value_rows.shape[0], HD), BF16)], axis=1)
            part = part.reshape(2 * size, value_rows.shape[0])
            got.append(jnp.dot(part, value_rows, preferred_element_type=F32))
        for group, part in zip(groups, got):
            total = part[:, HD:]
            inverse = pl.reciprocal(total, approx=True)
            inverse = inverse * (2.0 - total * inverse)
            mixed = (part[:, :HD] * inverse).astype(BF16)
            mixed_ref[:, group * PAIR : group * PAIR + HD] = mixed[:size]
            mixed_ref[:, group * PAIR + HD : (group + 1) * PAIR] = mixed[size:]

    def products(half):
        rows = slice(half * Q_WIDTH // 2, (half + 1) * Q_WIDTH // 2)
        return [
            jnp.dot(mixed_ref[:, rows], wo_ref[rows, start : start + PAIR], preferred_element_type=F32)
            for start in range(0, model, PAIR)
        ]

    groups = range(KV_HEADS)
    if not halves:
        queries = [query(group) for group in groups]
        expo = exponents([score(group, part) for group, part in zip(groups, queries)])
        mix(groups, expo)
        for start in range(0, model, PAIR):
            wait("o", start)
            update = jnp.dot(mixed_ref[...], wo_ref[:, start : start + PAIR], preferred_element_type=F32)
            write(start, x[:, start : start + PAIR] + update)
        return
    early, late = groups[: KV_HEADS // 2], groups[KV_HEADS // 2 :]
    queries = [query(group) for group in early]
    scores = [score(group, part) for group, part in zip(early, queries)]
    queries = [query(group) for group in late]
    expo = exponents(scores)
    scores = [score(group, part) for group, part in zip(late, queries)]
    mix(early, expo)
    updates = products(0)
    expo = exponents(scores)
    mix(late, expo)
    for start, first, second in zip(range(0, model, PAIR), updates, products(1)):
        write(start, x[:, start : start + PAIR] + (first + second))


def write_ids(ids_row, ids_out):
    ids_out[...] = jnp.zeros(ids_out.shape, BF16)
    ids_out[:, : ids_row.shape[1]] = jnp.broadcast_to(ids_row, (EXTRA, ids_row.shape[1])).astype(BF16)


def opening_kernel(
    size, x_hbm, ids_hbm, gain_hbm, table_hbm, wq_hbm, wk_hbm, wv_hbm, wo_hbm,
    out_ref, ids_out, k_ref, v_ref, cos_ref, bias_ref, wq_ref, wk_ref, wv_ref, wo_ref, gain_ref, table_ref, *refs,
):
    rest_refs, refs = refs[: CHUNKS - 1], refs[CHUNKS - 1 :]
    x_ref, ids_ref, raw_gain, raw_table, mixed_ref, small_sems, sems = refs
    small = [
        pltpu.make_async_copy(ids_hbm, ids_ref, small_sems.at[0]),
        pltpu.make_async_copy(table_hbm, raw_table, small_sems.at[1]),
        pltpu.make_async_copy(gain_hbm, raw_gain, small_sems.at[2]),
        pltpu.make_async_copy(x_hbm.at[0, :size], x_ref, small_sems.at[3]),
    ]
    late = [
        pltpu.make_async_copy(x_hbm.at[0, (i + 1) * size : (i + 2) * size], rest_refs[i], small_sems.at[4 + i])
        for i in range(CHUNKS - 1)
    ]
    made = []

    def batch(source, target, rows, lanes):
        step = (rows.stop - rows.start) // 2
        copies = []
        for low in range(rows.start, rows.stop, step):
            part = (slice(low, low + step), lanes)
            copies.append(pltpu.make_async_copy(source.at[(0, *part)], target.at[part], sems.at[len(made)]))
            made.append(copies[-1])
        return copies

    model, half = wk_ref.shape[0], Q_WIDTH // 2
    narrow = slice(0, KV_WIDTH)
    batches = [
        batch(wv_hbm, wv_ref, slice(0, model), narrow),
        batch(wk_hbm, wk_ref, slice(0, model), narrow),
        batch(wq_hbm, wq_ref, slice(0, model), slice(0, half)),
        batch(wq_hbm, wq_ref, slice(0, model), slice(half, Q_WIDTH)),
        batch(wo_hbm, wo_ref, slice(0, half), slice(0, model)),
        batch(wo_hbm, wo_ref, slice(half, Q_WIDTH), slice(0, model)),
    ]
    arrivals = {("v", 0): (0,), ("k", 0): (1,), ("q", 0): (2,), ("q", KV_HEADS // 2): (3,), ("o", 0): (4, 5)}

    def begin(index):
        for place, copy in enumerate(batches[index]):
            copy.start(priority=place % 2)

    def wait(name, place):
        for index in arrivals.get((name, place), ()):
            for copy in batches[index]:
                copy.wait()
            if index in (1, 2):
                begin(index + 3)
            if index == 3:
                for copy in late:
                    copy.start()

    for copy in small:
        copy.start()
    for index in range(4):
        begin(index)
    for copy in small:
        copy.wait()
    gain_ref[...] = raw_gain[...].astype(F32) * LIFT
    table_ref[...] = raw_table[...].astype(BF16)
    ids_row = ids_ref[...].astype(F32)
    factors, bias = tables_of(ids_row, table_ref[...])
    cos_ref[...] = factors
    bias_ref[...] = bias
    write_ids(ids_row, ids_out)

    def write(start, values):
        out_ref[:size, start : start + PAIR] = values.astype(BF16)

    layer(
        False, x_ref[...].astype(F32), gain_ref[...], (wq_ref, wk_ref, wv_ref, wo_ref), wait,
        lambda: (cos_ref[:size, :], bias_ref[:size, :size]), [], [], k_ref, v_ref, mixed_ref, write,
    )
    for copy in late:
        copy.wait()


def chunk_kernel(index, last, x_ref, gain_ref, wq_ref, wk_ref, wv_ref, wo_ref, *refs):
    refs = list(refs)
    mixed_ref = refs.pop(-1)
    size = mixed_ref.shape[0]
    low, high = index * size, (index + 1) * size
    if index == 0:
        ids_ref, table_ref, out_ref, k_ref, v_ref, cos_ref, bias_ref, *ids_out = refs
        for ref in ids_out:
            ref[...] = ids_ref[...]
        keys, values = [], []
    else:
        cos_ref, bias_ref = refs[:2]
        keys, values, refs = refs[2 : 2 + index], refs[2 + index : 2 + 2 * index], refs[2 + 2 * index :]
        if last and index == CHUNKS - 1:
            done, (whole_ref, out_ref, k_ref, v_ref, sems) = refs[:index], refs[index:]
            copies = [
                pltpu.make_async_copy(done[i].at[:size], whole_ref.at[0, i * size : (i + 1) * size], sems.at[i])
                for i in range(index)
            ]
            for copy in copies:
                copy.start()
        else:
            out_ref, k_ref, v_ref = refs

    def prepare():
        if index:
            return cos_ref[low:high, :], bias_ref[low:high, :]
        factors, bias = tables_of(ids_ref[:, : CHUNKS * size].astype(F32)[:1], table_ref[...])
        cos_ref[...] = factors
        bias_ref[...] = bias
        return factors[:size], bias[:size, :size]

    def write(start, result):
        out_ref[:size, start : start + PAIR] = result.astype(BF16)

    layer(
        index > 0 and not last, x_ref[:size, :].astype(F32), gain_ref[...], (wq_ref, wk_ref, wv_ref, wo_ref), lambda name, start: None,
        prepare, keys, values, k_ref, v_ref, mixed_ref, write,
    )
    if last and index == CHUNKS - 1:
        copy = pltpu.make_async_copy(out_ref, whole_ref.at[0, low:high], sems.at[index])
        copy.start()
        for each in copies + [copy]:
            each.wait()


VMEM = pl.BlockSpec(memory_space=pltpu.VMEM)
HBM = pl.BlockSpec(memory_space=pltpu.HBM)


def kept(shape, dtype):
    return pltpu.VMEM(shape, dtype)


def held(array):
    return pltpu.with_memory_space_constraint(array, pltpu.VMEM)


def left(array):
    return pltpu.with_memory_space_constraint(array, pltpu.HBM)


def passed_along(array, by):
    length = lax.axis_size("section")
    return lax.ppermute(array, "section", [(i, (i + by) % length) for i in range(length)])


def body(micro, segment, gain, w_query, w_key, w_value, w_out):
    length, model = micro.shape[1], micro.shape[2]
    size = length // CHUNKS
    limits = pltpu.CompilerParams(vmem_limit_bytes=32 * 1024 * 1024)
    table = jnp.asarray(rope_table())
    costs = [pl.CostEstimate(flops=flops, bytes_accessed=1024, transcendentals=0) for flops in (20 * 10**9, 1024)]
    ids_shape = kept((EXTRA, PAIR), BF16)
    key_values = [kept((size, KV_WIDTH), BF16)] * 2
    tables = [kept((length, PAIR), F32), kept((length, HD), F32)]
    mixing = pltpu.VMEM((size, Q_WIDTH), BF16)

    got = pl.pallas_call(
        functools.partial(opening_kernel, size),
        out_shape=(
            kept((size, model), BF16),
            ids_shape,
            *key_values,
            *tables,
            kept((model, Q_WIDTH), BF16),
            kept((model, KV_WIDTH), BF16),
            kept((model, KV_WIDTH), BF16),
            kept((Q_WIDTH, model), BF16),
            kept((1, model), F32),
            kept(table.shape, BF16),
            *[kept((size, model), BF16)] * (CHUNKS - 1),
        ),
        in_specs=[HBM] * 8,
        out_specs=(VMEM,) * (11 + CHUNKS),
        scratch_shapes=[
            pltpu.VMEM((size, model), BF16),
            pltpu.VMEM(segment.shape, jnp.int32),
            pltpu.VMEM(gain.shape, BF16),
            pltpu.VMEM(table.shape, F32),
            mixing,
            pltpu.SemaphoreType.DMA((3 + CHUNKS,)),
            pltpu.SemaphoreType.DMA((12,)),
        ],
        compiler_params=limits,
        name="opening",
    )(*(left(array) for array in (micro, segment, gain, table, w_query, w_key, w_value, w_out)))
    out, ids, k_rows, v_rows, cosines, bias = got[:6]
    weights = (got[10], *got[6:10])
    table = got[11]
    streams = [out, *got[12:]]

    for tick_index in range(TICKS):
        last = tick_index == TICKS - 1
        outs, keys, values = [], [], []
        for index in range(CHUNKS):
            if tick_index == 0 and index == 0:
                outs.append(passed_along(streams[0], 1))
                ids = passed_along(ids, 1)
                keys.append(k_rows)
                values.append(v_rows)
                continue
            args = [streams[index], *weights]
            shapes = [kept((size, model), BF16), *key_values]
            scratch = [mixing]
            if index == 0:
                args += [ids, table]
                shapes += tables + [ids_shape] * (not last)
            else:
                args += [cosines, bias, *keys, *values]
            specs = [VMEM] * len(shapes)
            ending = last and index == CHUNKS - 1
            if ending:
                args += outs
                shapes = [jax.ShapeDtypeStruct((1, length, model), BF16)]
                specs = [pl.BlockSpec(memory_space=pl.ANY)]
                scratch = [
                    pltpu.VMEM((size, model), BF16), *[pltpu.VMEM((size, KV_WIDTH), BF16)] * 2,
                    pltpu.SemaphoreType.DMA((CHUNKS,)), mixing,
                ]
            got = pl.pallas_call(
                functools.partial(chunk_kernel, index, last),
                out_shape=tuple(shapes), in_specs=[VMEM] * len(args), out_specs=tuple(specs),
                scratch_shapes=scratch, compiler_params=limits, cost_estimate=costs[index > 0], name="chunk_%d_%d" % (tick_index, index),
            )(*map(held, args))
            if ending:
                return got[0]
            if index == 0:
                cosines, bias = got[3:5]
                if not last:
                    ids = passed_along(got[5], 1)
            keys.append(got[1])
            values.append(got[2])
            outs.append(got[0] if last else passed_along(got[0], 1))
        streams = outs


def solution(mesh):
    in_specs = (
        P(("groups", "section"), None, None),
        P(("groups", "section"), None),
        P("section", None),
        P("section", None, None),
        P("section", None, None),
        P("section", None, None),
        P("section", None, None),
    )
    out_specs = P(("groups", "section"), None, None)
    return jax.shard_map(body, mesh=mesh, in_specs=in_specs, out_specs=out_specs, check_vma=False)
```

```python
import functools

import jax
import jax.numpy as jnp
import numpy as np
from jax import lax
from jax.experimental import pallas as pl
from jax.experimental.pallas import tpu as pltpu
from jax.sharding import PartitionSpec as P

HEADS = 16
KV_HEADS = 8
HD = 128
TICKS = 4
MAX_LEN = 96
CHUNKS = 2
EXTRA = 16
LIFT = 16.0
HIDDEN = -1e30
PAIR = 2 * HD
Q_WIDTH = HEADS * HD
KV_WIDTH = KV_HEADS * HD
BF16 = jnp.bfloat16
F32 = jnp.float32


def rope_table():
    middle = HD // 2
    spacing = 1000000.0 ** (-2.0 * np.arange(middle) / HD)
    angles = np.arange(MAX_LEN)[:, None] * spacing[None, :]
    cosine, sine = np.cos(angles), np.sin(angles)
    whole = np.concatenate([cosine, cosine, -sine, sine], axis=1).astype(np.float32)
    high = whole.astype(jnp.bfloat16).astype(np.float32)
    low = (whole - high).astype(jnp.bfloat16).astype(np.float32)
    return np.concatenate([high, low], axis=0)


def lower_triangle(rows, columns):
    row_index = lax.broadcasted_iota(jnp.int32, (rows, columns), 0)
    return lax.broadcasted_iota(jnp.int32, (rows, columns), 1) <= row_index


def tables_of(ids_row, table):
    length = ids_row.shape[1]
    across = jnp.broadcast_to(ids_row, (length, length))
    down = across.T
    row_index = lax.broadcasted_iota(jnp.int32, (length, length), 0)
    column = lax.broadcasted_iota(jnp.int32, (length, length), 1)
    matched = across == down
    places = jnp.sum(jnp.where(matched & (column < row_index), 1.0, 0.0), axis=1, keepdims=True)
    bias = jnp.where(matched & (column <= row_index), 0.0, HIDDEN)
    own, earlier_keys = bias[MAX_LEN:, MAX_LEN:], bias[MAX_LEN:, :MAX_LEN]
    merged = jnp.where(lower_triangle(MAX_LEN, MAX_LEN), own, earlier_keys)
    merged = jnp.concatenate([merged, jnp.full((length - MAX_LEN, HD - MAX_LEN), HIDDEN, F32)], axis=1)
    bias = jnp.concatenate([bias[:MAX_LEN, :HD], merged], axis=0)
    slots = lax.broadcasted_iota(jnp.int32, (length, 2 * MAX_LEN), 1)
    slots = jnp.where(slots >= MAX_LEN, slots - MAX_LEN, slots).astype(F32)
    one_hot = jnp.where(slots == places, 1.0, 0.0).astype(BF16)
    factors = jnp.dot(one_hot, table, preferred_element_type=F32)
    return factors, bias


def rotated(values, cosine, sine):
    return values * cosine + pltpu.roll(values, HD // 2, 1) * sine


def layer(halves, x, gain, weights, wait, prepare, kept_keys, kept_values, k_ref, v_ref, mixed_ref, write):
    size, model = x.shape
    wq_ref, wk_ref, wv_ref, wo_ref = weights
    scale = lax.rsqrt(jnp.mean(x * x, axis=1, keepdims=True) + 1e-05) * (1.0 / LIFT)
    lifted = (x * gain).astype(BF16)
    for start in range(0, KV_WIDTH, PAIR):
        wait("v", start)
        got = jnp.dot(lifted, wv_ref[:, start : start + PAIR], preferred_element_type=F32)
        v_ref[:, start : start + PAIR] = (got * scale).astype(BF16)
    cos_rows, bias_rows = prepare()
    cosine = cos_rows[:, :HD] * scale
    sine = cos_rows[:, HD:] * scale
    factor = HD ** (-0.5) * np.log2(np.e)
    cosine_q = cosine * factor
    sine_q = sine * factor
    for start in range(0, KV_WIDTH, PAIR):
        wait("k", start)
        got = jnp.dot(lifted, wk_ref[:, start : start + PAIR], preferred_element_type=F32)
        for half in range(0, PAIR, HD):
            turned = rotated(got[:, half : half + HD], cosine, sine)
            k_ref[:, start + half : start + half + HD] = turned.astype(BF16)
    spare = jnp.zeros((HD - size, HD), BF16)
    lower = lower_triangle(size, HD)
    lower_share = jnp.where(lower, 1.0, 0.0).astype(BF16)
    key_refs, value_refs = [k_ref, *kept_keys], [v_ref, *kept_values]

    def rows_of(refs, group):
        lanes = slice(group * HD, (group + 1) * HD)
        if len(refs) == 1:
            return refs[0][:, lanes]
        return jnp.concatenate([part for ref in refs for part in (ref[:, lanes], spare)], axis=0)

    def query(group):
        lanes = slice(group * PAIR, (group + 1) * PAIR)
        wait("q", group)
        got = jnp.dot(lifted, wq_ref[:, lanes], preferred_element_type=F32)
        turned = [rotated(got[:, half : half + HD], cosine_q, sine_q) for half in range(0, PAIR, HD)]
        return jnp.concatenate(turned, axis=0).astype(BF16)

    def score(group, queries):
        key_rows = rows_of(key_refs, group)
        got = lax.dot_general(queries, key_rows, (((1,), (1,)), ((), ())), preferred_element_type=F32)
        got = got.reshape(2, size, key_rows.shape[0])
        if kept_keys:
            got = jnp.where(lower[None], got[:, :, :HD], got[:, :, HD:])
        return got + bias_rows[None]

    def exponents(scores):
        most = [jnp.max(part, axis=2, keepdims=True) for part in scores]
        expo = [jnp.exp2(part - peak).astype(BF16) for part, peak in zip(scores, most)]
        if kept_keys:
            own = [part * lower_share[None] for part in expo]
            expo = [jnp.concatenate([mine, part - mine], axis=2) for mine, part in zip(own, expo)]
        return expo

    def mix(groups, expo):
        got = []
        for group, part in zip(groups, expo):
            value_rows = rows_of(value_refs, group)
            value_rows = jnp.concatenate([value_rows, jnp.ones((value_rows.shape[0], HD), BF16)], axis=1)
            part = part.reshape(2 * size, value_rows.shape[0])
            got.append(jnp.dot(part, value_rows, preferred_element_type=F32))
        for group, part in zip(groups, got):
            total = part[:, HD:]
            inverse = pl.reciprocal(total, approx=True)
            inverse = inverse * (2.0 - total * inverse)
            mixed = (part[:, :HD] * inverse).astype(BF16)
            mixed_ref[:, group * PAIR : group * PAIR + HD] = mixed[:size]
            mixed_ref[:, group * PAIR + HD : (group + 1) * PAIR] = mixed[size:]

    def products(half):
        rows = slice(half * Q_WIDTH // 2, (half + 1) * Q_WIDTH // 2)
        return [
            jnp.dot(mixed_ref[:, rows], wo_ref[rows, start : start + PAIR], preferred_element_type=F32)
            for start in range(0, model, PAIR)
        ]

    groups = range(KV_HEADS)
    if not halves:
        queries = [query(group) for group in groups]
        expo = exponents([score(group, part) for group, part in zip(groups, queries)])
        mix(groups, expo)
        for start in range(0, model, PAIR):
            wait("o", start)
            update = jnp.dot(mixed_ref[...], wo_ref[:, start : start + PAIR], preferred_element_type=F32)
            write(start, x[:, start : start + PAIR] + update)
        return
    early, late = groups[: KV_HEADS // 2], groups[KV_HEADS // 2 :]
    queries = [query(group) for group in early]
    scores = [score(group, part) for group, part in zip(early, queries)]
    queries = [query(group) for group in late]
    expo = exponents(scores)
    scores = [score(group, part) for group, part in zip(late, queries)]
    mix(early, expo)
    updates = products(0)
    expo = exponents(scores)
    mix(late, expo)
    for start, first, second in zip(range(0, model, PAIR), updates, products(1)):
        write(start, x[:, start : start + PAIR] + (first + second))


def write_ids(ids_row, ids_out):
    ids_out[...] = jnp.zeros(ids_out.shape, BF16)
    ids_out[:, : ids_row.shape[1]] = jnp.broadcast_to(ids_row, (EXTRA, ids_row.shape[1])).astype(BF16)


def opening_kernel(
    size, x_hbm, ids_hbm, gain_hbm, table_hbm, wq_hbm, wk_hbm, wv_hbm, wo_hbm,
    out_ref, k_ref, v_ref, cos_ref, bias_ref, wq_ref, wk_ref, wv_ref, wo_ref, gain_ref, table_ref, *refs,
):
    rest_refs, refs = refs[: CHUNKS - 1], refs[CHUNKS - 1 :]
    x_ref, ids_ref, raw_gain, raw_table, mixed_ref, small_sems, sems = refs
    small = [
        pltpu.make_async_copy(ids_hbm, ids_ref, small_sems.at[0]),
        pltpu.make_async_copy(table_hbm, raw_table, small_sems.at[1]),
        pltpu.make_async_copy(gain_hbm, raw_gain, small_sems.at[2]),
        pltpu.make_async_copy(x_hbm.at[0, :size], x_ref, small_sems.at[3]),
    ]
    late = [
        pltpu.make_async_copy(x_hbm.at[0, (i + 1) * size : (i + 2) * size], rest_refs[i], small_sems.at[4 + i])
        for i in range(CHUNKS - 1)
    ]
    made = []

    def batch(source, target, rows, lanes):
        step = (rows.stop - rows.start) // 2
        copies = []
        for low in range(rows.start, rows.stop, step):
            part = (slice(low, low + step), lanes)
            copies.append(pltpu.make_async_copy(source.at[(0, *part)], target.at[part], sems.at[len(made)]))
            made.append(copies[-1])
        return copies

    model, half = wk_ref.shape[0], Q_WIDTH // 2
    narrow = slice(0, KV_WIDTH)
    batches = [
        batch(wv_hbm, wv_ref, slice(0, model), narrow),
        batch(wk_hbm, wk_ref, slice(0, model), narrow),
        batch(wq_hbm, wq_ref, slice(0, model), slice(0, half)),
        batch(wq_hbm, wq_ref, slice(0, model), slice(half, Q_WIDTH)),
        batch(wo_hbm, wo_ref, slice(0, half), slice(0, model)),
        batch(wo_hbm, wo_ref, slice(half, Q_WIDTH), slice(0, model)),
    ]
    arrivals = {("v", 0): (0,), ("k", 0): (1,), ("q", 0): (2,), ("q", KV_HEADS // 2): (3,), ("o", 0): (4, 5)}

    def begin(index):
        for place, copy in enumerate(batches[index]):
            copy.start(priority=place % 2)

    def wait(name, place):
        for index in arrivals.get((name, place), ()):
            for copy in batches[index]:
                copy.wait()
            if index in (1, 2):
                begin(index + 3)
            if index == 3:
                for copy in late:
                    copy.start()

    for copy in small:
        copy.start()
    for index in range(4):
        begin(index)
    for copy in small:
        copy.wait()
    gain_ref[...] = raw_gain[...].astype(F32) * LIFT
    table_ref[...] = raw_table[...].astype(BF16)
    ids_row = ids_ref[...].astype(F32)
    factors, bias = tables_of(ids_row, table_ref[...])
    cos_ref[...] = factors
    bias_ref[...] = bias
    write_ids(ids_row, out_ref.at[x_ref.shape[0] :])

    def write(start, values):
        out_ref[:size, start : start + PAIR] = values.astype(BF16)

    layer(
        False, x_ref[...].astype(F32), gain_ref[...], (wq_ref, wk_ref, wv_ref, wo_ref), wait,
        lambda: (cos_ref[:size, :], bias_ref[:size, :size]), [], [], k_ref, v_ref, mixed_ref, write,
    )
    for copy in late:
        copy.wait()


def chunk_kernel(index, last, x_ref, gain_ref, wq_ref, wk_ref, wv_ref, wo_ref, *refs):
    refs = list(refs)
    mixed_ref = refs.pop(-1)
    size = mixed_ref.shape[0]
    low, high = index * size, (index + 1) * size
    if index == 0:
        ids_ref, table_ref, out_ref, k_ref, v_ref, cos_ref, bias_ref, *ids_out = refs
        if ids_ref.shape[0] > EXTRA:
            ids_ref = ids_ref.at[size:, :PAIR]
        for ref in ids_out:
            ref[...] = ids_ref[...]
        keys, values = [], []
    else:
        cos_ref, bias_ref = refs[:2]
        keys, values, refs = refs[2 : 2 + index], refs[2 + index : 2 + 2 * index], refs[2 + 2 * index :]
        if last and index == CHUNKS - 1:
            done, (whole_ref, out_ref, k_ref, v_ref, sems) = refs[:index], refs[index:]
            copies = [
                pltpu.make_async_copy(done[i].at[:size], whole_ref.at[0, i * size : (i + 1) * size], sems.at[i])
                for i in range(index)
            ]
            for copy in copies:
                copy.start()
        else:
            out_ref, k_ref, v_ref = refs

    def prepare():
        if index:
            return cos_ref[low:high, :], bias_ref[low:high, :]
        factors, bias = tables_of(ids_ref[:, : CHUNKS * size].astype(F32)[:1], table_ref[...])
        cos_ref[...] = factors
        bias_ref[...] = bias
        return factors[:size], bias[:size, :size]

    def write(start, result):
        out_ref[:size, start : start + PAIR] = result.astype(BF16)

    layer(
        index > 0 and not last, x_ref[:size, :].astype(F32), gain_ref[...], (wq_ref, wk_ref, wv_ref, wo_ref), lambda name, start: None,
        prepare, keys, values, k_ref, v_ref, mixed_ref, write,
    )
    if last and index == CHUNKS - 1:
        copy = pltpu.make_async_copy(out_ref, whole_ref.at[0, low:high], sems.at[index])
        copy.start()
        for each in copies + [copy]:
            each.wait()


VMEM = pl.BlockSpec(memory_space=pltpu.VMEM)
HBM = pl.BlockSpec(memory_space=pltpu.HBM)


def kept(shape, dtype):
    return pltpu.VMEM(shape, dtype)


def held(array):
    return pltpu.with_memory_space_constraint(array, pltpu.VMEM)


def left(array):
    return pltpu.with_memory_space_constraint(array, pltpu.HBM)


def passed_along(array, by):
    length = lax.axis_size("section")
    return lax.ppermute(array, "section", [(i, (i + by) % length) for i in range(length)])


def body(micro, segment, gain, w_query, w_key, w_value, w_out):
    length, model = micro.shape[1], micro.shape[2]
    size = length // CHUNKS
    limits = pltpu.CompilerParams(vmem_limit_bytes=32 * 1024 * 1024)
    table = jnp.asarray(rope_table())
    costs = [pl.CostEstimate(flops=flops, bytes_accessed=1024, transcendentals=0) for flops in (20 * 10**9, 1024)]
    ids_shape = kept((EXTRA, PAIR), BF16)
    key_values = [kept((size, KV_WIDTH), BF16)] * 2
    tables = [kept((length, PAIR), F32), kept((length, HD), F32)]
    mixing = pltpu.VMEM((size, Q_WIDTH), BF16)

    got = pl.pallas_call(
        functools.partial(opening_kernel, size),
        out_shape=(
            kept((size + EXTRA, model), BF16),
            *key_values,
            *tables,
            kept((model, Q_WIDTH), BF16),
            kept((model, KV_WIDTH), BF16),
            kept((model, KV_WIDTH), BF16),
            kept((Q_WIDTH, model), BF16),
            kept((1, model), F32),
            kept(table.shape, BF16),
            *[kept((size, model), BF16)] * (CHUNKS - 1),
        ),
        in_specs=[HBM] * 8,
        out_specs=(VMEM,) * (10 + CHUNKS),
        scratch_shapes=[
            pltpu.VMEM((size, model), BF16),
            pltpu.VMEM(segment.shape, jnp.int32),
            pltpu.VMEM(gain.shape, BF16),
            pltpu.VMEM(table.shape, F32),
            mixing,
            pltpu.SemaphoreType.DMA((3 + CHUNKS,)),
            pltpu.SemaphoreType.DMA((12,)),
        ],
        compiler_params=limits,
        name="opening",
    )(*(left(array) for array in (micro, segment, gain, table, w_query, w_key, w_value, w_out)))
    out, k_rows, v_rows, cosines, bias = got[:5]
    weights = (got[9], *got[5:9])
    table = got[10]
    streams = [out, *got[11:]]

    for tick_index in range(TICKS):
        last = tick_index == TICKS - 1
        outs, keys, values = [], [], []
        for index in range(CHUNKS):
            if tick_index == 0 and index == 0:
                outs.append(passed_along(streams[0], 1))
                ids = outs[0]
                keys.append(k_rows)
                values.append(v_rows)
                continue
            args = [streams[index], *weights]
            shapes = [kept((size, model), BF16), *key_values]
            scratch = [mixing]
            if index == 0:
                args += [ids, table]
                shapes += tables + [ids_shape] * (not last)
            else:
                args += [cosines, bias, *keys, *values]
            specs = [VMEM] * len(shapes)
            ending = last and index == CHUNKS - 1
            if ending:
                args += outs
                shapes = [jax.ShapeDtypeStruct((1, length, model), BF16)]
                specs = [pl.BlockSpec(memory_space=pl.ANY)]
                scratch = [
                    pltpu.VMEM((size, model), BF16), *[pltpu.VMEM((size, KV_WIDTH), BF16)] * 2,
                    pltpu.SemaphoreType.DMA((CHUNKS,)), mixing,
                ]
            got = pl.pallas_call(
                functools.partial(chunk_kernel, index, last),
                out_shape=tuple(shapes), in_specs=[VMEM] * len(args), out_specs=tuple(specs),
                scratch_shapes=scratch, compiler_params=limits, cost_estimate=costs[index > 0], name="chunk_%d_%d" % (tick_index, index),
            )(*map(held, args))
            if ending:
                return got[0]
            if index == 0:
                cosines, bias = got[3:5]
                if not last:
                    ids = passed_along(got[5], 1)
            keys.append(got[1])
            values.append(got[2])
            outs.append(got[0] if last else passed_along(got[0], 1))
        streams = outs


def solution(mesh):
    in_specs = (
        P(("groups", "section"), None, None),
        P(("groups", "section"), None),
        P("section", None),
        P("section", None, None),
        P("section", None, None),
        P("section", None, None),
        P("section", None, None),
    )
    out_specs = P(("groups", "section"), None, None)
    return jax.shard_map(body, mesh=mesh, in_specs=in_specs, out_specs=out_specs, check_vma=False)
```

```python
import functools

import jax
import jax.numpy as jnp
import numpy as np
from jax import lax
from jax.experimental import pallas as pl
from jax.experimental.pallas import tpu as pltpu
from jax.sharding import PartitionSpec as P

HEADS = 16
KV_HEADS = 8
HD = 128
TICKS = 4
MAX_LEN = 96
CHUNKS = 2
EXTRA = 16
LIFT = 16.0
HIDDEN = -1e30
PAIR = 2 * HD
Q_WIDTH = HEADS * HD
KV_WIDTH = KV_HEADS * HD
BF16 = jnp.bfloat16
F32 = jnp.float32


def rope_table():
    middle = HD // 2
    spacing = 1000000.0 ** (-2.0 * np.arange(middle) / HD)
    angles = np.arange(MAX_LEN)[:, None] * spacing[None, :]
    cosine, sine = np.cos(angles), np.sin(angles)
    whole = np.concatenate([cosine, cosine, -sine, sine], axis=1).astype(np.float32)
    high = whole.astype(jnp.bfloat16).astype(np.float32)
    low = (whole - high).astype(jnp.bfloat16).astype(np.float32)
    return np.concatenate([high, low], axis=0)


def lower_triangle(rows, columns):
    row_index = lax.broadcasted_iota(jnp.int32, (rows, columns), 0)
    return lax.broadcasted_iota(jnp.int32, (rows, columns), 1) <= row_index


def tables_of(ids_row, table):
    length = ids_row.shape[1]
    across = jnp.broadcast_to(ids_row, (length, length))
    down = across.T
    row_index = lax.broadcasted_iota(jnp.int32, (length, length), 0)
    column = lax.broadcasted_iota(jnp.int32, (length, length), 1)
    matched = across == down
    places = jnp.sum(jnp.where(matched & (column < row_index), 1.0, 0.0), axis=1, keepdims=True)
    bias = jnp.where(matched & (column <= row_index), 0.0, HIDDEN)
    own, earlier_keys = bias[MAX_LEN:, MAX_LEN:], bias[MAX_LEN:, :MAX_LEN]
    merged = jnp.where(lower_triangle(MAX_LEN, MAX_LEN), own, earlier_keys)
    merged = jnp.concatenate([merged, jnp.full((length - MAX_LEN, HD - MAX_LEN), HIDDEN, F32)], axis=1)
    bias = jnp.concatenate([bias[:MAX_LEN, :HD], merged], axis=0)
    slots = lax.broadcasted_iota(jnp.int32, (length, 2 * MAX_LEN), 1)
    slots = jnp.where(slots >= MAX_LEN, slots - MAX_LEN, slots).astype(F32)
    one_hot = jnp.where(slots == places, 1.0, 0.0).astype(BF16)
    factors = jnp.dot(one_hot, table, preferred_element_type=F32)
    return factors, bias


def rotated(values, cosine, sine):
    return values * cosine + pltpu.roll(values, HD // 2, 1) * sine


def layer(x, gain, weights, wait, prepare, kept_keys, kept_values, k_ref, v_ref, mixed_ref, write):
    size, model = x.shape
    wq_ref, wk_ref, wv_ref, wo_ref = weights
    scale = lax.rsqrt(jnp.mean(x * x, axis=1, keepdims=True) + 1e-05) * (1.0 / LIFT)
    lifted = (x * gain).astype(BF16)
    for start in range(0, KV_WIDTH, PAIR):
        wait("v", start)
        got = jnp.dot(lifted, wv_ref[:, start : start + PAIR], preferred_element_type=F32)
        v_ref[:, start : start + PAIR] = (got * scale).astype(BF16)
    cos_rows, bias_rows = prepare()
    cosine = cos_rows[:, :HD] * scale
    sine = cos_rows[:, HD:] * scale
    factor = HD ** (-0.5) * np.log2(np.e)
    cosine_q = cosine * factor
    sine_q = sine * factor
    for start in range(0, KV_WIDTH, PAIR):
        wait("k", start)
        got = jnp.dot(lifted, wk_ref[:, start : start + PAIR], preferred_element_type=F32)
        for half in range(0, PAIR, HD):
            turned = rotated(got[:, half : half + HD], cosine, sine)
            k_ref[:, start + half : start + half + HD] = turned.astype(BF16)
    queries = []
    for start in range(0, Q_WIDTH, PAIR):
        wait("q", start)
        got = jnp.dot(lifted, wq_ref[:, start : start + PAIR], preferred_element_type=F32)
        upper = rotated(got[:, :HD], cosine_q, sine_q)
        lower = rotated(got[:, HD:], cosine_q, sine_q)
        queries.append(jnp.concatenate([upper, lower], axis=0).astype(BF16))

    groups = range(KV_HEADS)
    spare = jnp.zeros((HD - size, HD), BF16)
    lower = lower_triangle(size, HD)
    lower_share = jnp.where(lower, 1.0, 0.0).astype(BF16)

    def rows_of(refs, group):
        lanes = slice(group * HD, (group + 1) * HD)
        if len(refs) == 1:
            return refs[0][:, lanes]
        return jnp.concatenate([part for ref in refs for part in (ref[:, lanes], spare)], axis=0)

    key_refs, value_refs = [k_ref, *kept_keys], [v_ref, *kept_values]
    scores = []
    for group in groups:
        key_rows = rows_of(key_refs, group)
        got = lax.dot_general(queries[group], key_rows, (((1,), (1,)), ((), ())), preferred_element_type=F32)
        got = got.reshape(2, size, key_rows.shape[0])
        if kept_keys:
            got = jnp.where(lower[None], got[:, :, :HD], got[:, :, HD:])
        scores.append(got + bias_rows[None])
    most = [jnp.max(part, axis=2, keepdims=True) for part in scores]
    expo = [jnp.exp2(scores[g] - most[g]).astype(BF16) for g in groups]
    if kept_keys:
        own = [part * lower_share[None] for part in expo]
        expo = [jnp.concatenate([mine, part - mine], axis=2) for mine, part in zip(own, expo)]
    got = []
    for group in groups:
        value_rows = rows_of(value_refs, group)
        value_rows = jnp.concatenate([value_rows, jnp.ones((value_rows.shape[0], HD), BF16)], axis=1)
        part = expo[group].reshape(2 * size, value_rows.shape[0])
        got.append(jnp.dot(part, value_rows, preferred_element_type=F32))
    for group in groups:
        total = got[group][:, HD:]
        inverse = pl.reciprocal(total, approx=True)
        inverse = inverse * (2.0 - total * inverse)
        mixed = (got[group][:, :HD] * inverse).astype(BF16)
        mixed_ref[:, group * PAIR : group * PAIR + HD] = mixed[:size]
        mixed_ref[:, group * PAIR + HD : (group + 1) * PAIR] = mixed[size:]
    for start in range(0, model, PAIR):
        wait("o", start)
        update = jnp.dot(mixed_ref[...], wo_ref[:, start : start + PAIR], preferred_element_type=F32)
        write(start, x[:, start : start + PAIR] + update)


def write_ids(ids_row, out_ref, size):
    length = ids_row.shape[1]
    out_ref[size:, :] = jnp.zeros((EXTRA, out_ref.shape[1]), BF16)
    out_ref[size:, :length] = jnp.broadcast_to(ids_row, (EXTRA, length)).astype(BF16)


def opening_kernel(
    size, x_hbm, ids_hbm, gain_hbm, table_hbm, wq_hbm, wk_hbm, wv_hbm, wo_hbm,
    out_ref, k_ref, v_ref, cos_ref, bias_ref, wq_ref, wk_ref, wv_ref, wo_ref, gain_ref, table_ref, *refs,
):
    rest_refs, refs = refs[: CHUNKS - 1], refs[CHUNKS - 1 :]
    x_ref, ids_ref, raw_gain, raw_table, mixed_ref, small_sems, sems = refs
    small = [
        pltpu.make_async_copy(ids_hbm, ids_ref, small_sems.at[0]),
        pltpu.make_async_copy(table_hbm, raw_table, small_sems.at[1]),
        pltpu.make_async_copy(gain_hbm, raw_gain, small_sems.at[2]),
        pltpu.make_async_copy(x_hbm.at[0, :size], x_ref, small_sems.at[3]),
    ]
    late = [
        pltpu.make_async_copy(x_hbm.at[0, (i + 1) * size : (i + 2) * size], rest_refs[i], small_sems.at[4 + i])
        for i in range(CHUNKS - 1)
    ]
    made = []

    def batch(source, target, rows, lanes):
        step = (rows.stop - rows.start) // 2
        copies = []
        for low in range(rows.start, rows.stop, step):
            part = (slice(low, low + step), lanes)
            copies.append(pltpu.make_async_copy(source.at[(0, *part)], target.at[part], sems.at[len(made)]))
            made.append(copies[-1])
        return copies

    model, half = wk_ref.shape[0], Q_WIDTH // 2
    narrow, wide = slice(0, KV_WIDTH), slice(0, Q_WIDTH)
    batches = [
        batch(wv_hbm, wv_ref, slice(0, model), narrow),
        batch(wk_hbm, wk_ref, slice(0, model), narrow),
        batch(wq_hbm, wq_ref, slice(0, model // 2), wide),
        batch(wq_hbm, wq_ref, slice(model // 2, model), wide),
        batch(wo_hbm, wo_ref, slice(0, half), slice(0, model)),
        batch(wo_hbm, wo_ref, slice(half, Q_WIDTH), slice(0, model)),
    ]
    arrivals = {("v", 0): (0,), ("k", 0): (1,), ("q", 0): (2, 3), ("o", 0): (4, 5)}

    def begin(index):
        if index < len(batches):
            for place, copy in enumerate(batches[index]):
                copy.start(priority=place % 2)
        if index == len(batches):
            for copy in late:
                copy.start()

    def wait(name, start):
        for index in arrivals.get((name, start), ()):
            for copy in batches[index]:
                copy.wait()
            begin(index + 4)

    for copy in small:
        copy.start()
    for index in range(4):
        begin(index)
    for copy in small:
        copy.wait()
    gain_ref[...] = raw_gain[...].astype(F32) * LIFT
    table_ref[...] = raw_table[...].astype(BF16)
    ids_row = ids_ref[...].astype(F32)
    factors, bias = tables_of(ids_row, table_ref[...])
    cos_ref[...] = factors
    bias_ref[...] = bias
    write_ids(ids_row, out_ref, size)

    def write(start, values):
        out_ref[:size, start : start + PAIR] = values.astype(BF16)

    layer(
        x_ref[...].astype(F32), gain_ref[...], (wq_ref, wk_ref, wv_ref, wo_ref), wait,
        lambda: (cos_ref[:size, :], bias_ref[:size, :size]), [], [], k_ref, v_ref, mixed_ref, write,
    )
    for copy in late:
        copy.wait()


def chunk_kernel(index, last, x_ref, gain_ref, wq_ref, wk_ref, wv_ref, wo_ref, *refs):
    refs = list(refs)
    mixed_ref = refs.pop(-1)
    size = mixed_ref.shape[0]
    low, high = index * size, (index + 1) * size
    if index == 0:
        table_ref = refs.pop(0)
        out_ref, k_ref, v_ref, cos_ref, bias_ref = refs
        if not last:
            out_ref[size:, :] = x_ref[size:, :]
        keys, values = [], []
    else:
        cos_ref, bias_ref = refs[:2]
        keys, values, refs = refs[2 : 2 + index], refs[2 + index : 2 + 2 * index], refs[2 + 2 * index :]
        if last and index == CHUNKS - 1:
            done, (whole_ref, out_ref, k_ref, v_ref, sems) = refs[:index], refs[index:]
            copies = [
                pltpu.make_async_copy(done[i].at[:size], whole_ref.at[0, i * size : (i + 1) * size], sems.at[i])
                for i in range(index)
            ]
            for copy in copies:
                copy.start()
        else:
            out_ref, k_ref, v_ref = refs

    def prepare():
        if index:
            return cos_ref[low:high, :], bias_ref[low:high, :]
        factors, bias = tables_of(x_ref[size:, : CHUNKS * size].astype(F32)[:1], table_ref[...])
        cos_ref[...] = factors
        bias_ref[...] = bias
        return factors[:size], bias[:size, :size]

    def write(start, result):
        out_ref[:size, start : start + PAIR] = result.astype(BF16)
        if last and index == CHUNKS - 1 and start % (2 * PAIR):
            lanes = slice(start - PAIR, start + PAIR)
            copies.append(
                pltpu.make_async_copy(out_ref.at[:, lanes], whole_ref.at[0, low:high, lanes], sems.at[len(copies)])
            )
            copies[-1].start()

    layer(
        x_ref[:size, :].astype(F32), gain_ref[...], (wq_ref, wk_ref, wv_ref, wo_ref), lambda name, start: None,
        prepare, keys, values, k_ref, v_ref, mixed_ref, write,
    )
    if last and index == CHUNKS - 1:
        for each in copies:
            each.wait()


VMEM = pl.BlockSpec(memory_space=pltpu.VMEM)
HBM = pl.BlockSpec(memory_space=pltpu.HBM)


def kept(shape, dtype):
    return pltpu.VMEM(shape, dtype)


def held(array):
    return pltpu.with_memory_space_constraint(array, pltpu.VMEM)


def left(array):
    return pltpu.with_memory_space_constraint(array, pltpu.HBM)


def passed_along(array, by):
    length = lax.axis_size("section")
    return lax.ppermute(array, "section", [(i, (i + by) % length) for i in range(length)])


def body(micro, segment, gain, w_query, w_key, w_value, w_out):
    length, model = micro.shape[1], micro.shape[2]
    size = length // CHUNKS
    limits = pltpu.CompilerParams(vmem_limit_bytes=32 * 1024 * 1024)
    table = jnp.asarray(rope_table())
    rows = [size + EXTRA] + [size] * (CHUNKS - 1)
    key_values = [kept((size, KV_WIDTH), BF16)] * 2
    tables = [kept((length, PAIR), F32), kept((length, HD), F32)]
    mixing = pltpu.VMEM((size, Q_WIDTH), BF16)

    got = pl.pallas_call(
        functools.partial(opening_kernel, size),
        out_shape=(
            kept((rows[0], model), BF16),
            *key_values,
            *tables,
            kept((model, Q_WIDTH), BF16),
            kept((model, KV_WIDTH), BF16),
            kept((model, KV_WIDTH), BF16),
            kept((Q_WIDTH, model), BF16),
            kept((1, model), F32),
            kept(table.shape, BF16),
            *[kept((size, model), BF16)] * (CHUNKS - 1),
        ),
        in_specs=[HBM] * 8,
        out_specs=(VMEM,) * (10 + CHUNKS),
        scratch_shapes=[
            pltpu.VMEM((size, model), BF16),
            pltpu.VMEM(segment.shape, jnp.int32),
            pltpu.VMEM(gain.shape, BF16),
            pltpu.VMEM(table.shape, F32),
            mixing,
            pltpu.SemaphoreType.DMA((3 + CHUNKS,)),
            pltpu.SemaphoreType.DMA((12,)),
        ],
        compiler_params=limits,
        name="opening",
    )(*(left(array) for array in (micro, segment, gain, table, w_query, w_key, w_value, w_out)))
    out, k_rows, v_rows, cosines, bias = got[:5]
    weights = (got[9], *got[5:9])
    table = got[10]
    streams = [out, *got[11:]]

    for tick_index in range(TICKS):
        last = tick_index == TICKS - 1
        outs, keys, values = [], [], []
        for index in range(CHUNKS):
            if tick_index == 0 and index == 0:
                outs.append(passed_along(streams[0], 1))
                keys.append(k_rows)
                values.append(v_rows)
                continue
            args = [streams[index], *weights]
            shapes = [kept((rows[index], model), BF16), *key_values]
            scratch = [mixing]
            if index == 0:
                args.append(table)
                shapes += tables
            else:
                args += [cosines, bias, *keys, *values]
            specs = [VMEM] * len(shapes)
            ending = last and index == CHUNKS - 1
            if ending:
                args += outs
                shapes = [jax.ShapeDtypeStruct((1, length, model), BF16)]
                specs = [pl.BlockSpec(memory_space=pl.ANY)]
                scratch = [
                    pltpu.VMEM((size, model), BF16), *[pltpu.VMEM((size, KV_WIDTH), BF16)] * 2,
                    pltpu.SemaphoreType.DMA((CHUNKS + 1,)), mixing,
                ]
            got = pl.pallas_call(
                functools.partial(chunk_kernel, index, last),
                out_shape=tuple(shapes), in_specs=[VMEM] * len(args), out_specs=tuple(specs),
                scratch_shapes=scratch, compiler_params=limits, name="chunk_%d_%d" % (tick_index, index),
            )(*map(held, args))
            if ending:
                return got[0]
            if index == 0:
                cosines, bias = got[3:]
            keys.append(got[1])
            values.append(got[2])
            outs.append(got[0] if last else passed_along(got[0], 1))
        streams = outs


def solution(mesh):
    in_specs = (
        P(("groups", "section"), None, None),
        P(("groups", "section"), None),
        P("section", None),
        P("section", None, None),
        P("section", None, None),
        P("section", None, None),
        P("section", None, None),
    )
    out_specs = P(("groups", "section"), None, None)
    return jax.shard_map(body, mesh=mesh, in_specs=in_specs, out_specs=out_specs, check_vma=False)
```
